512 devices in a mesh: party: 2 (over z_lo), sample: 32 (over x, z_hi, core), feat: 8 (over y).
Axes of the slice: x: 4, y: 8, z: 8 (z_hi: 4, z_lo: 2; z = z_hi * 2 + z_lo), core: 2. Of those that a mesh axis runs over, the one named last changes fastest.
Arguments:
- x_share: bfloat16 [2, 8192, 8192], P('party', 'sample', 'feat'), may hold values from -3 to 3
- a_share: bfloat16 [2, 8192, 8192], P('party', 'sample', 'feat'), may hold values from -3 to 3
- w_share: float32 [2, 8192, 256], P('party', 'feat'), may hold values from -0.0625 to 0.0625
- b_share: bfloat16 [2, 8192, 256], P('party', 'feat'), may hold values from -0.0625 to 0.0625
- c_share: bfloat16 [2, 8192, 256], P('party', 'sample'), may hold values from -6 to 6
- mask_lin: bfloat16 [2, 8192, 256], P('party', 'sample'), may hold values from -12 to 12
- mask_sq: bfloat16 [2, 8192, 256], P('party', 'sample'), may hold values from -30 to 30
- mask_cube: bfloat16 [2, 8192, 256], P('party', 'sample'), may hold values from -240 to 240
- y_share: bfloat16 [2, 8192, 256], P('party', 'sample'), may hold values from -6 to 6
- r_mask: bfloat16 [2, 8192, 256], P('party', 'sample'), may hold values from -3 to 3
- grad_product: bfloat16 [2, 8192, 256], P('party', 'feat'), may hold values from -240 to 240
Outputs:
- new_weights: float32 [2, 8192, 256], P('party', 'feat')
The draws below stay inside these ranges and needn't reach their ends.
All inputs are finite; a program needn't handle non-finite values.
Results may differ from the reference program's by a relative error of at most 0.0018.
Values may be sent and summed in bfloat16 or wider, within the bound.
A program may use at most 64 MiB of HBM per device.

```python
import jax
import jax.numpy as jnp

FEATURES = 8192
PHENO = 256
SAMPLES = 8192


def steps_of(key, extent, split, least, high):
    def one(dim, parts):
        draws = jax.random.uniform(jax.random.fold_in(jax.random.fold_in(key, 6), dim), (parts,), jnp.float32, least / len(split), high / len(split))
        return jnp.repeat(jnp.exp(draws), extent[dim] // parts).reshape((-1,) + (1,) * (len(extent) - dim - 1))

    gain = one(*split[0])
    for cut in split[1:]:
        gain = gain * one(*cut)
    return gain


def noise(own_key, extent, scale, reach, pieces=(), dtype=jnp.bfloat16):
    result = jax.random.normal(own_key, extent, jnp.float32) * scale
    if len(pieces) > 0:
        result = steps_of(own_key, extent, pieces, -0.22, 0.18) * result
    return jnp.clip(result, min=-reach, max=reach).astype(dtype)


def setup_inputs(seed: int = 0) -> dict:
    arg_keys = jax.random.split(jax.random.key(seed), 12)
    return {
        "x_share": noise(arg_keys[0], (2, SAMPLES, FEATURES), 0.5, 3.0, ((0, 2), (1, 32), (2, 8))),
        "a_share": noise(arg_keys[1], (2, SAMPLES, FEATURES), 0.5, 3.0, ((0, 2), (1, 32), (2, 8))),
        "w_share": noise(arg_keys[2], (2, FEATURES, PHENO), FEATURES ** -0.5, 0.0625, ((0, 2), (1, 8)), jnp.float32),
        "b_share": noise(arg_keys[3], (2, FEATURES, PHENO), FEATURES ** -0.5, 0.0625, ((0, 2), (1, 8))),
        "c_share": noise(arg_keys[4], (2, SAMPLES, PHENO), 1.0, 6.0, ((0, 2), (1, 32))),
        "mask_lin": noise(arg_keys[5], (2, SAMPLES, PHENO), 2.0, 12.0, ((0, 2), (1, 32))),
        "mask_sq": noise(arg_keys[6], (2, SAMPLES, PHENO), 5.0, 30.0, ((0, 2), (1, 32))),
        "mask_cube": noise(arg_keys[7], (2, SAMPLES, PHENO), 40.0, 240.0, ((0, 2), (1, 32))),
        "y_share": noise(arg_keys[8], (2, SAMPLES, PHENO), 1.0, 6.0, ((0, 2), (1, 32))),
        "r_mask": noise(arg_keys[9], (2, SAMPLES, PHENO), 0.5, 3.0, ((0, 2), (1, 32))),
        "grad_product": noise(arg_keys[10], (2, FEATURES, PHENO), 40.0, 240.0, ((0, 2), (1, 8))),
    }


learn_rate = 64.0
slope_one = 0.197
cube_coef = 0.004


def reference(x_share, a_share, w_share, b_share, c_share, mask_lin, mask_sq, mask_cube, y_share, r_mask, grad_product):
    masked_inputs = (x_share.astype(jnp.float32) - a_share.astype(jnp.float32)).astype(jnp.bfloat16)
    opened_inputs = (masked_inputs[0].astype(jnp.float32) + masked_inputs[1].astype(jnp.float32)).astype(jnp.bfloat16)
    masked_weights = (w_share - b_share.astype(jnp.float32)).astype(jnp.bfloat16)
    opened_weights = (masked_weights[0].astype(jnp.float32) + masked_weights[1].astype(jnp.float32)).astype(jnp.bfloat16)
    both_terms = jnp.dot(opened_inputs, opened_weights, preferred_element_type=jnp.float32)
    margins = []
    for party in range(2):
        select = 1.0 if party == 0 else 0.0
        margin = select * both_terms
        margin = margin + jnp.dot(opened_inputs, b_share[party], preferred_element_type=jnp.float32)
        margin = margin + jnp.dot(a_share[party], opened_weights, preferred_element_type=jnp.float32)
        margins.append(margin + c_share[party].astype(jnp.float32))
    spread = (margins[0] - mask_lin[0].astype(jnp.float32)) + (margins[1] - mask_lin[1].astype(jnp.float32))
    masked_parts = []
    for party in range(2):
        select = 1.0 if party == 0 else 0.0
        linear = mask_lin[party].astype(jnp.float32)
        cubed = select * (spread * spread * spread) + 3.0 * (spread * spread) * linear
        cubed = cubed + 3.0 * spread * mask_sq[party].astype(jnp.float32) + mask_cube[party].astype(jnp.float32)
        residual = 0.5 * select + slope_one * margins[party] - cube_coef * cubed - y_share[party].astype(jnp.float32)
        masked_parts.append((residual - r_mask[party].astype(jnp.float32)).astype(jnp.bfloat16))
    opened_residual = (masked_parts[0].astype(jnp.float32) + masked_parts[1].astype(jnp.float32)).astype(jnp.bfloat16)
    samples = x_share.shape[1]
    inputs_t = opened_inputs.T
    public_term = jnp.dot(inputs_t, opened_residual, preferred_element_type=jnp.float32)
    results = []
    for party in range(2):
        select = 1.0 if party == 0 else 0.0
        gradient = select * public_term
        gradient = gradient + jnp.dot(inputs_t, r_mask[party], preferred_element_type=jnp.float32)
        gradient = gradient + jnp.dot(a_share[party].T, opened_residual, preferred_element_type=jnp.float32)
        gradient = gradient + grad_product[party].astype(jnp.float32)
        results.append(w_share[party] - (learn_rate / samples) * gradient)
    return jnp.stack(results)
```

```python
import jax
import jax.numpy as jnp
from jax import lax
from jax.experimental import pallas as pl
from jax.experimental.pallas import tpu as pltpu
from jax.sharding import Mesh
from jax.sharding import PartitionSpec as P

SAMPLE = ("sample_0", "sample_1", "sample_2")
MESH = pl.DeviceIdType.MESH
F32 = jnp.float32
BF16 = jnp.bfloat16

learn_rate = 64.0
slope_one = 0.197
cube_coef = 0.004

ROWS = 256
COLS = 1024
PH = 256
CHUNK = 64
CHUNKS = ROWS // CHUNK
GROUP = 16
PIECE = ROWS // GROUP
HALF = COLS // 2
QUARTER = HALF // 4
LAST = QUARTER // 4
SMALL = 6
ORDER = (8, 7, 9, 6, 10, 5, 11, 4, 12, 3, 13, 2, 14, 1, 15)


def kernel(
    x_ref, a_ref, w_ref, b_ref, c_ref, lin_ref, sq_ref, cube_ref, y_ref, r_ref,
    grad_ref,
    xv, av, wv, bv, sv, mv, om, ev, et, at, wm, ow, opened, zv, zbuf, pack, pbuf,
    rbuf, gv, gbuf, xbuf, hv, hbuf,
    load_sem, in_send, in_recv, wt_send, wt_recv, pk_send, pk_recv,
    z_send, z_recv, r_send, r_recv, g_send, g_recv, x_send, x_recv, h_send, h_recv,
    f_send, f_recv, k_send, k_recv,
):
    party = lax.axis_index("party")
    xi = lax.axis_index("sample_0")
    hi = lax.axis_index("sample_1")
    core = lax.axis_index("sample_2")
    feat = lax.axis_index("feat")
    me = feat * 2 + party
    select = (party == 0).astype(F32)

    def at_place(p=None, x=None, h=None, c=None, f=None):
        return (
            party if p is None else p,
            xi if x is None else x,
            hi if h is None else h,
            core if c is None else c,
            feat if f is None else f,
        )

    def in_group(d):
        t = lax.rem(me + d, GROUP)
        return at_place(p=lax.rem(t, 2), f=lax.div(t, 2))

    partner = at_place(p=1 - party)
    sibling = at_place(c=1 - core)
    other_z = at_place(p=1 - party, h=lax.rem(hi + 3 + 2 * party, 4))
    across = [(dx, dh) for dx in range(4) for dh in range(4) if dx or dh]

    def at_sample(dx, dh):
        return at_place(x=lax.rem(xi + dx, 4), h=lax.rem(hi + dh, 4))

    loads = [
        pltpu.make_async_copy(src.at[0], dst, load_sem.at[i])
        for i, (src, dst) in enumerate(
            [(x_ref, xv), (a_ref, av), (w_ref, wv), (b_ref, bv)]
            + [
                (ref, sv.at[i])
                for i, ref in enumerate((c_ref, lin_ref, sq_ref, cube_ref, y_ref, r_ref))
            ]
        )
    ]
    for load in loads:
        load.start()

    greeted = [sibling, partner, other_z]
    greeted += [in_group(d) for d in ORDER if d != 1 and d != 15]
    greeted += [at_place(p=1 - party, f=lax.rem(feat + 7 + 2 * party, 8))]
    greeted += [at_sample(dx, dh) for dx, dh in across]
    barrier = pltpu.get_barrier_semaphore()
    for place in greeted:
        pl.semaphore_signal(barrier, inc=1, device_id=place, device_id_type=MESH)

    loads[0].wait()
    loads[1].wait()
    mv[...] = (xv[...].astype(F32) - av[...].astype(F32)).astype(BF16)
    loads[2].wait()
    loads[3].wait()
    wm[...] = (wv[...] - bv[...].astype(F32)).astype(BF16)
    pl.semaphore_wait(barrier, len(greeted))

    def remote(src, dst, send, recv, place):
        return pltpu.make_async_remote_copy(
            src_ref=src, dst_ref=dst, send_sem=send, recv_sem=recv,
            device_id=place, device_id_type=MESH,
        )

    inputs = []
    for k in range(CHUNKS):
        rows = pl.ds(k * CHUNK, CHUNK)
        inputs.append(remote(mv.at[rows], om.at[rows], in_send.at[k], in_recv.at[k], partner))
    my_half = pl.ds(pl.multiple_of(core * HALF, HALF), HALF)
    weights = remote(wm.at[my_half], ow.at[my_half], wt_send.at[0], wt_recv.at[0], other_z)
    weights.start()
    for copy in inputs:
        copy.start()

    for load in loads[4:]:
        load.wait()
    mine = pl.ds(pl.multiple_of(me * PIECE, PIECE), PIECE)
    theirs = pl.ds(
        pl.multiple_of((feat * 2 + 1 - party) * PIECE, PIECE), PIECE
    )
    for i in range(SMALL):
        pack[i] = sv[i, theirs, :]
    packed = remote(pack, pbuf, pk_send.at[0], pk_recv.at[0], partner)
    packed.start()

    at[...] = av[...].T
    weights.wait_recv()
    passed = remote(ow.at[my_half], ow.at[my_half], wt_send.at[1], wt_recv.at[1], sibling)
    passed.start()
    passed.wait()
    opened[...] = (wm[...].astype(F32) + ow[...].astype(F32)).astype(BF16)
    zv[...] = jnp.dot(av[...], opened[...], preferred_element_type=F32)

    for k in range(CHUNKS):
        rows = pl.ds(k * CHUNK, CHUNK)
        inputs[k].wait_recv()
        part = (mv[rows, :].astype(F32) + om[rows, :].astype(F32)).astype(BF16)
        ev[rows, :] = part
        both = select * jnp.dot(part, opened[...], preferred_element_type=F32)
        zv[rows, :] += both + jnp.dot(part, bv[...], preferred_element_type=F32)

    sums = {}
    for d in ORDER:
        t = lax.rem(me + d, GROUP)
        rows = pl.ds(pl.multiple_of(t * PIECE, PIECE), PIECE)
        sums[d] = remote(zv.at[rows], zbuf.at[d], z_send.at[d], z_recv.at[d], in_group(d))
        sums[d].start()

    et[...] = ev[...].T
    gv[...] = jnp.dot(et[...], sv[SMALL - 1], preferred_element_type=F32)
    packed.wait()

    own = zv[mine, :]
    for d in range(2, GROUP, 2):
        sums[d].wait_recv()
        own = own + zbuf[d]
    sums[1].wait_recv()
    far = zbuf[1]
    for d in range(3, GROUP, 2):
        sums[d].wait_recv()
        far = far + zbuf[d]

    def values(i):
        return sv[i, mine, :].astype(F32), pbuf[i].astype(F32)

    own_c, far_c = values(0)
    own_lin, far_lin = values(1)
    own_margin, far_margin = own + own_c, far + far_c
    spread = (own_margin - own_lin) + (far_margin - far_lin)

    def residual(s, margin, i):
        linear = values(1)[i]
        cubed = s * (spread * spread * spread) + 3.0 * (spread * spread) * linear
        cubed = cubed + 3.0 * spread * values(2)[i] + values(3)[i]
        result = 0.5 * s + slope_one * margin - cube_coef * cubed - values(4)[i]
        return (result - values(5)[i]).astype(BF16).astype(F32)

    rbuf[mine, :] = (residual(select, own_margin, 0) + residual(1.0 - select, far_margin, 1)).astype(
        BF16
    )
    spreads = {}
    for d in ORDER:
        spreads[d] = remote(
            rbuf.at[mine], rbuf.at[mine], r_send.at[d], r_recv.at[d], in_group(d)
        )
        spreads[d].start()
    for d in ORDER:
        spreads[d].wait_recv()

    def add_terms(first):
        rows = pl.ds(pl.multiple_of(first, HALF), HALF)
        term = select * jnp.dot(et[rows, :], rbuf[...], preferred_element_type=F32)
        gv[rows, :] += term + jnp.dot(at[rows, :], rbuf[...], preferred_element_type=F32)

    add_terms((1 - core) * HALF)
    their_half = pl.ds(pl.multiple_of((1 - core) * HALF, HALF), HALF)
    crossing = remote(gv.at[their_half], gbuf, g_send.at[0], g_recv.at[0], sibling)
    crossing.start()
    add_terms(core * HALF)
    crossing.wait_recv()
    gbuf[...] += gv[my_half, :]

    quarters = {}
    for d in (2, 1, 3):
        t = lax.rem(xi + d, 4)
        rows = pl.ds(pl.multiple_of(t * QUARTER, QUARTER), QUARTER)
        quarters[d] = remote(
            gbuf.at[rows], xbuf.at[d], x_send.at[d], x_recv.at[d], at_sample(d, 0)
        )
        quarters[d].start()
    total = gbuf[pl.ds(pl.multiple_of(xi * QUARTER, QUARTER), QUARTER), :]
    for d in (1, 3, 2):
        quarters[d].wait_recv()
        total = total + xbuf[d]
    hv[...] = total

    lasts = {}
    for d in (2, 1, 3):
        t = lax.rem(hi + d, 4)
        rows = pl.ds(pl.multiple_of(t * LAST, LAST), LAST)
        lasts[d] = remote(hv.at[rows], hbuf.at[d], h_send.at[d], h_recv.at[d], at_sample(0, d))
        lasts[d].start()
    total = hv[pl.ds(pl.multiple_of(hi * LAST, LAST), LAST), :]
    for d in (1, 3, 2):
        lasts[d].wait_recv()
        total = total + hbuf[d]

    place = pl.ds(pl.multiple_of(core * HALF + xi * QUARTER + hi * LAST, LAST), LAST)
    grad_ref[place, :] = total.astype(BF16)
    finals = []
    for i, (dx, dh) in enumerate(across):
        finals.append(
            remote(
                grad_ref.at[place], grad_ref.at[place], f_send.at[i], f_recv.at[i], at_sample(dx, dh)
            )
        )
    for copy in finals[::-1]:
        copy.start()
    for copy in finals:
        copy.wait_recv()
    ending = remote(grad_ref.at[my_half], grad_ref.at[my_half], k_send.at[0], k_recv.at[0], sibling)
    ending.start()

    weights.wait_send()
    for copy in inputs + [sums[d] for d in ORDER] + [spreads[d] for d in ORDER]:
        copy.wait_send()
    crossing.wait_send()
    for copy in [quarters[d] for d in (1, 2, 3)] + [lasts[d] for d in (1, 2, 3)] + finals:
        copy.wait_send()
    ending.wait()


def gradient(x, a, w, b, c, lin, sq, cube, y, r):
    dma = pltpu.SemaphoreType.DMA
    return pl.pallas_call(
        kernel,
        out_shape=jax.ShapeDtypeStruct((COLS, PH), BF16),
        in_specs=[pl.BlockSpec(memory_space=pl.ANY)] * 10,
        out_specs=pl.BlockSpec(memory_space=pltpu.VMEM),
        scratch_shapes=[
            pltpu.VMEM((ROWS, COLS), BF16),
            pltpu.VMEM((ROWS, COLS), BF16),
            pltpu.VMEM((COLS, PH), F32),
            pltpu.VMEM((COLS, PH), BF16),
            pltpu.VMEM((SMALL, ROWS, PH), BF16),
            pltpu.VMEM((ROWS, COLS), BF16),
            pltpu.VMEM((ROWS, COLS), BF16),
            pltpu.VMEM((ROWS, COLS), BF16),
            pltpu.VMEM((COLS, ROWS), BF16),
            pltpu.VMEM((COLS, ROWS), BF16),
            pltpu.VMEM((COLS, PH), BF16),
            pltpu.VMEM((COLS, PH), BF16),
            pltpu.VMEM((COLS, PH), BF16),
            pltpu.VMEM((ROWS, PH), F32),
            pltpu.VMEM((GROUP, PIECE, PH), F32),
            pltpu.VMEM((SMALL, PIECE, PH), BF16),
            pltpu.VMEM((SMALL, PIECE, PH), BF16),
            pltpu.VMEM((ROWS, PH), BF16),
            pltpu.VMEM((COLS, PH), F32),
            pltpu.VMEM((HALF, PH), F32),
            pltpu.VMEM((4, QUARTER, PH), F32),
            pltpu.VMEM((QUARTER, PH), F32),
            pltpu.VMEM((4, LAST, PH), F32),
            dma((10,)),
            dma((CHUNKS,)), dma((CHUNKS,)),
            dma((2,)), dma((2,)),
            dma((1,)), dma((1,)),
            dma((GROUP,)), dma((GROUP,)),
            dma((GROUP,)), dma((GROUP,)),
            dma((1,)), dma((1,)),
            dma((4,)), dma((4,)),
            dma((4,)), dma((4,)),
            dma((15,)), dma((15,)),
            dma((1,)), dma((1,)),
        ],
        compiler_params=pltpu.CompilerParams(
            collective_id=0, has_side_effects=True, vmem_limit_bytes=40 * 2**20
        ),
        cost_estimate=pl.CostEstimate(
            flops=12 * ROWS * COLS * PH, bytes_accessed=5 * 2**20, transcendentals=0
        ),
    )(x, a, w, b, c, lin, sq, cube, y, r)


def shards(x, a, w, b, c, lin, sq, cube, y, r, grad_product):
    grad = gradient(x, a, w, b, c, lin, sq, cube, y, r)
    samples = x.shape[1] * lax.axis_size(SAMPLE)
    whole = grad.astype(F32) + grad_product[0].astype(F32)
    return (w[0] - learn_rate / samples * whole)[None]


def solution(mesh):
    torus = Mesh(
        mesh.devices.reshape(mesh.shape["party"], 4, 4, 2, mesh.shape["feat"]),
        ("party", "sample_0", "sample_1", "sample_2", "feat"),
    )
    return jax.shard_map(
        shards,
        mesh=torus,
        in_specs=(
            P("party", SAMPLE, "feat"),
            P("party", SAMPLE, "feat"),
            P("party", "feat", None),
            P("party", "feat", None),
            P("party", SAMPLE, None),
            P("party", SAMPLE, None),
            P("party", SAMPLE, None),
            P("party", SAMPLE, None),
            P("party", SAMPLE, None),
            P("party", SAMPLE, None),
            P("party", "feat", None),
        ),
        out_specs=P("party", "feat", None),
        check_vma=False,
    )
```

```python
import jax
import jax.numpy as jnp
from jax import lax
from jax.experimental import pallas as pl
from jax.experimental.pallas import tpu as pltpu
from jax.sharding import Mesh
from jax.sharding import PartitionSpec as P

SAMPLE = ("sample_0", "sample_1", "sample_2")
MESH = pl.DeviceIdType.MESH
F32 = jnp.float32
BF16 = jnp.bfloat16

learn_rate = 64.0
slope_one = 0.197
cube_coef = 0.004

ROWS = 256
COLS = 1024
PH = 256
CHUNK = 64
CHUNKS = ROWS // CHUNK
BLOCKS = 2
BLOCK = ROWS // BLOCKS
PER = CHUNKS // BLOCKS
FEATS = 8
PIECE = BLOCK // FEATS
HALF = COLS // 2
SUBS = 2
SUB = HALF // SUBS
QUARTER = SUB // 4
LAST = QUARTER // 4
SMALL = 6
ALONG = (4, 3, 5, 2, 6, 1, 7)


def kernel(
    x_ref, a_ref, w_ref, b_ref, c_ref, lin_ref, sq_ref, cube_ref, y_ref, r_ref,
    grad_ref,
    xv, av, wv, bv, sv, mv, om, ev, et, ea, wm, ow, opened, zv, zbuf, psum, pack, pbuf,
    rr, gv, gbuf, xbuf, hv, hbuf,
    y_token, z_token, x_token, load_sem, in_send, in_recv, wt_send, wt_recv, pk_send, pk_recv,
    z_send, z_recv, p_send, p_recv, r_send, r_recv, g_send, g_recv, x_send, x_recv,
    h_send, h_recv, f_send, f_recv, e_send, e_recv, k_send, k_recv,
):
    party = lax.axis_index("party")
    xi = lax.axis_index("sample_0")
    hi = lax.axis_index("sample_1")
    core = lax.axis_index("sample_2")
    feat = lax.axis_index("feat")
    select = (party == 0).astype(F32)

    def at_place(p=None, x=None, h=None, c=None, f=None):
        return (
            party if p is None else p,
            xi if x is None else x,
            hi if h is None else h,
            core if c is None else c,
            feat if f is None else f,
        )

    partner = at_place(p=1 - party)
    sibling = at_place(c=1 - core)
    other_z = at_place(p=1 - party, h=lax.rem(hi + 3 + 2 * party, 4))

    def along_y(d):
        return at_place(f=lax.rem(feat + d, FEATS))

    def along_x(d):
        return at_place(x=lax.rem(xi + d, 4))

    def along_z(d):
        return at_place(h=lax.rem(hi + d, 4))

    loads = [
        pltpu.make_async_copy(src.at[0], dst, load_sem.at[i])
        for i, (src, dst) in enumerate(
            [(x_ref, xv), (a_ref, av), (w_ref, wv), (b_ref, bv)]
            + [
                (ref, sv.at[i])
                for i, ref in enumerate((c_ref, lin_ref, sq_ref, cube_ref, y_ref, r_ref))
            ]
        )
    ]
    for load in loads:
        load.start()

    near_y, near_x, near_z = [along_y(1), along_y(7)], [along_x(1), along_x(3)], [partner, other_z]
    greeted = near_z + near_y + near_x + [sibling]
    barrier = pltpu.get_barrier_semaphore()
    for place in greeted:
        pl.semaphore_signal(barrier, inc=1, device_id=place, device_id_type=MESH)

    loads[0].wait()
    loads[1].wait()
    mv[...] = (xv[...].astype(F32) - av[...].astype(F32)).astype(BF16)
    pl.semaphore_wait(barrier, len(greeted))

    def pass_on(r):
        for token, places in ((y_token, near_y), (z_token, near_z), (x_token, near_x)):
            if r < token.shape[0]:
                for place in places:
                    pl.semaphore_signal(token.at[r], inc=1, device_id=place, device_id_type=MESH)

    def hear(r):
        for token in (y_token, z_token, x_token):
            if r < token.shape[0]:
                pl.semaphore_wait(token.at[r], 2)

    sent = []

    def remote(src, dst, send, recv, place):
        copy = pltpu.make_async_remote_copy(
            src_ref=src, dst_ref=dst, send_sem=send, recv_sem=recv,
            device_id=place, device_id_type=MESH,
        )
        copy.start()
        sent.append(copy)
        return copy

    def slab(first, size):
        return pl.ds(pl.multiple_of(first, size), size)

    inputs = []
    for k in range(CHUNKS):
        rows = pl.ds(k * CHUNK, CHUNK)
        inputs.append(remote(mv.at[rows], om.at[rows], in_send.at[k], in_recv.at[k], partner))
    my_half = slab(core * HALF, HALF)
    loads[2].wait()
    loads[3].wait()
    wm[...] = (wv[...] - bv[...].astype(F32)).astype(BF16)
    weights = remote(wm.at[my_half], ow.at[my_half], wt_send.at[0], wt_recv.at[0], other_z)
    pass_on(0)

    for load in loads[4:]:
        load.wait()
    for i in range(SMALL):
        for j in range(BLOCKS):
            pack[i, pl.ds(j * PIECE, PIECE), :] = sv[i, slab(j * BLOCK + feat * PIECE, PIECE), :]
    packed = remote(pack, pbuf, pk_send.at[0], pk_recv.at[0], partner)

    ea[:, ROWS:] = av[...].T
    hear(0)
    pass_on(1)
    hear(1)
    pass_on(2)
    hear(2)
    weights.wait_recv()
    passed = remote(ow.at[my_half], ow.at[my_half], wt_send.at[1], wt_recv.at[1], sibling)
    passed.wait_recv()
    opened[...] = (wm[...].astype(F32) + ow[...].astype(F32)).astype(BF16)
    zv[...] = jnp.dot(av[...], opened[...], preferred_element_type=F32)

    def margins(k):
        rows = pl.ds(k * CHUNK, CHUNK)
        inputs[k].wait_recv()
        part = (mv[rows, :].astype(F32) + om[rows, :].astype(F32)).astype(BF16)
        ev[rows, :] = part
        both = select * jnp.dot(part, opened[...], preferred_element_type=F32)
        zv[rows, :] += both + jnp.dot(part, bv[...], preferred_element_type=F32)

    def share(j):
        copies = []
        for d in ALONG:
            rows = slab(j * BLOCK + lax.rem(feat + d, FEATS) * PIECE, PIECE)
            copies.append(
                remote(zv.at[rows], zbuf.at[j, d], z_send.at[j, d], z_recv.at[j, d], along_y(d))
            )
        return copies

    def add_up(j, copies):
        for copy in copies:
            copy.wait_recv()
        total = zv[slab(j * BLOCK + feat * PIECE, PIECE), :]
        for d in range(1, FEATS):
            total = total + zbuf[j, d]
        psum[j, 0] = total
        return remote(psum.at[j, 0], psum.at[j, 1], p_send.at[j], p_recv.at[j], partner)

    def residuals(j, copy):
        copy.wait_recv()
        own_rows = pl.ds(j * PIECE, PIECE)
        own = [pack[i, own_rows, :].astype(F32) for i in range(SMALL)]
        far = [pbuf[i, own_rows, :].astype(F32) for i in range(SMALL)]
        own_margin, far_margin = psum[j, 0] + own[0], psum[j, 1] + far[0]
        spread = (own_margin - own[1]) + (far_margin - far[1])

        def masked(s, margin, value):
            cubed = s * (spread * spread * spread) + 3.0 * (spread * spread) * value[1]
            cubed = cubed + 3.0 * spread * value[2] + value[3]
            result = 0.5 * s + slope_one * margin - cube_coef * cubed - value[4]
            return (result - value[5]).astype(BF16).astype(F32)

        both = masked(select, own_margin, own) + masked(1.0 - select, far_margin, far)
        rows = slab(j * BLOCK + feat * PIECE, PIECE)
        rr[rows, :] = both.astype(BF16)
        return [
            remote(rr.at[rows], rr.at[rows], r_send.at[j, d], r_recv.at[j, d], along_y(d))
            for d in ALONG
        ]

    def turned(j):
        rows = pl.ds(j * BLOCK, BLOCK)
        flipped = ev[rows, :].T
        et[:, rows] = flipped
        ea[:, rows] = (flipped.astype(F32) * select).astype(BF16)

    margins(0)
    margins(1)
    shared_0 = share(0)
    turned(0)
    margins(2)
    margins(3)
    shared_1 = share(1)
    summed_0 = add_up(0, shared_0)
    packed.wait_recv()
    opened_0 = residuals(0, summed_0)
    turned(1)
    gv[...] = jnp.dot(et[...], sv[SMALL - 1], preferred_element_type=F32)
    summed_1 = add_up(1, shared_1)
    opened_1 = residuals(1, summed_1)
    for copy in opened_0 + opened_1:
        copy.wait_recv()
    rr[ROWS:, :] = rr[:ROWS, :]

    def terms(first):
        rows = slab(first, SUB)
        return gv[rows, :] + jnp.dot(ea[rows, :], rr[...], preferred_element_type=F32)

    crossing = []
    for n in range(SUBS):
        their = slab((1 - core) * HALF + n * SUB, SUB)
        gv[their, :] = terms((1 - core) * HALF + n * SUB)
        crossing.append(remote(gv.at[their], gbuf.at[n], g_send.at[n], g_recv.at[n], sibling))
    for n in range(SUBS):
        gv[slab(core * HALF + n * SUB, SUB), :] = terms(core * HALF + n * SUB)

    quarters = []
    for n in range(SUBS):
        crossing[n].wait_recv()
        gbuf[n] += gv[slab(core * HALF + n * SUB, SUB), :]
        quarters.append(
            [
                remote(
                    gbuf.at[n, slab(lax.rem(xi + d, 4) * QUARTER, QUARTER)],
                    xbuf.at[n, d], x_send.at[n, d], x_recv.at[n, d], along_x(d),
                )
                for d in (2, 1, 3)
            ]
        )
    lasts = []
    for n in range(SUBS):
        for copy in quarters[n]:
            copy.wait_recv()
        total = gbuf[n, slab(xi * QUARTER, QUARTER), :]
        hv[n] = total + xbuf[n, 1] + xbuf[n, 2] + xbuf[n, 3]
        lasts.append(
            [
                remote(
                    hv.at[n, slab(lax.rem(hi + d, 4) * LAST, LAST)],
                    hbuf.at[n, d], h_send.at[n, d], h_recv.at[n, d], along_z(d),
                )
                for d in (2, 1, 3)
            ]
        )
    back_z = []
    for n in range(SUBS):
        for copy in lasts[n]:
            copy.wait_recv()
        total = hv[n, slab(hi * LAST, LAST), :]
        total = total + hbuf[n, 1] + hbuf[n, 2] + hbuf[n, 3]
        rows = slab(core * HALF + n * SUB + xi * QUARTER + hi * LAST, LAST)
        grad_ref[rows, :] = total.astype(BF16)
        back_z.append(
            [
                remote(grad_ref.at[rows], grad_ref.at[rows], f_send.at[n, d], f_recv.at[n, d], along_z(d))
                for d in (2, 1, 3)
            ]
        )
    back_x = []
    for n in range(SUBS):
        for copy in back_z[n]:
            copy.wait_recv()
        rows = slab(core * HALF + n * SUB + xi * QUARTER, QUARTER)
        back_x.append(
            [
                remote(grad_ref.at[rows], grad_ref.at[rows], e_send.at[n, d], e_recv.at[n, d], along_x(d))
                for d in (2, 1, 3)
            ]
        )
    back_core = []
    for n in range(SUBS):
        for copy in back_x[n]:
            copy.wait_recv()
        rows = slab(core * HALF + n * SUB, SUB)
        back_core.append(
            remote(grad_ref.at[rows], grad_ref.at[rows], k_send.at[n], k_recv.at[n], sibling)
        )
    for copy in back_core:
        copy.wait_recv()
    for copy in sent:
        copy.wait_send()


def gradient(x, a, w, b, c, lin, sq, cube, y, r):
    dma = pltpu.SemaphoreType.DMA
    return pl.pallas_call(
        kernel,
        out_shape=jax.ShapeDtypeStruct((COLS, PH), BF16),
        in_specs=[pl.BlockSpec(memory_space=pltpu.HBM)] * 10,
        out_specs=pl.BlockSpec(memory_space=pltpu.VMEM),
        scratch_shapes=[
            pltpu.VMEM((ROWS, COLS), BF16),
            pltpu.VMEM((ROWS, COLS), BF16),
            pltpu.VMEM((COLS, PH), F32),
            pltpu.VMEM((COLS, PH), BF16),
            pltpu.VMEM((SMALL, ROWS, PH), BF16),
            pltpu.VMEM((ROWS, COLS), BF16),
            pltpu.VMEM((ROWS, COLS), BF16),
            pltpu.VMEM((ROWS, COLS), BF16),
            pltpu.VMEM((COLS, ROWS), BF16),
            pltpu.VMEM((COLS, 2 * ROWS), BF16),
            pltpu.VMEM((COLS, PH), BF16),
            pltpu.VMEM((COLS, PH), BF16),
            pltpu.VMEM((COLS, PH), BF16),
            pltpu.VMEM((ROWS, PH), F32),
            pltpu.VMEM((BLOCKS, FEATS, PIECE, PH), F32),
            pltpu.VMEM((BLOCKS, 2, PIECE, PH), F32),
            pltpu.VMEM((SMALL, BLOCKS * PIECE, PH), BF16),
            pltpu.VMEM((SMALL, BLOCKS * PIECE, PH), BF16),
            pltpu.VMEM((2 * ROWS, PH), BF16),
            pltpu.VMEM((COLS, PH), F32),
            pltpu.VMEM((SUBS, SUB, PH), F32),
            pltpu.VMEM((SUBS, 4, QUARTER, PH), F32),
            pltpu.VMEM((SUBS, QUARTER, PH), F32),
            pltpu.VMEM((SUBS, 4, LAST, PH), F32),
            pltpu.SemaphoreType.REGULAR((3,)),
            pltpu.SemaphoreType.REGULAR((3,)),
            pltpu.SemaphoreType.REGULAR((1,)),
            dma((10,)),
            dma((CHUNKS,)), dma((CHUNKS,)),
            dma((2,)), dma((2,)),
            dma((1,)), dma((1,)),
            dma((BLOCKS, FEATS)), dma((BLOCKS, FEATS)),
            dma((BLOCKS,)), dma((BLOCKS,)),
            dma((BLOCKS, FEATS)), dma((BLOCKS, FEATS)),
            dma((SUBS,)), dma((SUBS,)),
            dma((SUBS, 4)), dma((SUBS, 4)),
            dma((SUBS, 4)), dma((SUBS, 4)),
            dma((SUBS, 4)), dma((SUBS, 4)),
            dma((SUBS, 4)), dma((SUBS, 4)),
            dma((SUBS,)), dma((SUBS,)),
        ],
        compiler_params=pltpu.CompilerParams(
            collective_id=0, has_side_effects=True, vmem_limit_bytes=60 * 2**20
        ),
        cost_estimate=pl.CostEstimate(
            flops=12 * ROWS * COLS * PH, bytes_accessed=5 * 2**20, transcendentals=0
        ),
    )(x, a, w, b, c, lin, sq, cube, y, r)


def shards(x, a, w, b, c, lin, sq, cube, y, r, grad_product):
    grad = gradient(x, a, w, b, c, lin, sq, cube, y, r)
    samples = x.shape[1] * lax.axis_size(SAMPLE)
    whole = grad.astype(F32) + grad_product[0].astype(F32)
    return (w[0] - learn_rate / samples * whole)[None]


def solution(mesh):
    torus = Mesh(
        mesh.devices.reshape(mesh.shape["party"], 4, 4, 2, mesh.shape["feat"]),
        ("party", "sample_0", "sample_1", "sample_2", "feat"),
    )
    return jax.shard_map(
        shards,
        mesh=torus,
        in_specs=(
            P("party", SAMPLE, "feat"),
            P("party", SAMPLE, "feat"),
            P("party", "feat", None),
            P("party", "feat", None),
            P("party", SAMPLE, None),
            P("party", SAMPLE, None),
            P("party", SAMPLE, None),
            P("party", SAMPLE, None),
            P("party", SAMPLE, None),
            P("party", SAMPLE, None),
            P("party", "feat", None),
        ),
        out_specs=P("party", "feat", None),
        check_vma=False,
    )
```

```python
import jax
import jax.numpy as jnp
from jax import lax
from jax.experimental import pallas as pl
from jax.experimental.pallas import tpu as pltpu
from jax.sharding import Mesh
from jax.sharding import PartitionSpec as P

SAMPLE = ("sample_0", "sample_1", "sample_2")
MESH = pl.DeviceIdType.MESH
F32 = jnp.float32
BF16 = jnp.bfloat16

learn_rate = 64.0
slope_one = 0.197
cube_coef = 0.004

ROWS = 256
COLS = 1024
PH = 256
CHUNK = 64
CHUNKS = ROWS // CHUNK
BLOCKS = 2
BLOCK = ROWS // BLOCKS
PER = CHUNKS // BLOCKS
FEATS = 8
PIECE = BLOCK // FEATS
HALF = COLS // 2
SUBS = 2
SUB = HALF // SUBS
QUARTER = SUB // 4
LAST = QUARTER // 4
SMALL = 6
ALONG = (4, 3, 5, 2, 6, 1, 7)
MIDDLE = 120.0
GRADIENT = (-22.0, 384.0)
MARGIN = (-14.0, 960.0)


def coded(value, span):
    least, step = span
    level = jnp.log2(jnp.maximum(jnp.abs(value), 2.0**least)) - least
    level = jnp.floor(level * step + 0.5)
    high = jnp.floor(level * (1 / 128))
    code = jnp.exp2(high - MIDDLE) * (1.0 + (level - 128.0 * high) * (1 / 128))
    return jnp.where(value < 0, -code, code).astype(BF16)


def decoded(code, span):
    least, step = span
    code = code.astype(F32)
    size = jnp.abs(code)
    high = jnp.floor(jnp.log2(size) + 0.003)
    low = size * jnp.exp2(-high) - 1.0
    value = jnp.exp2((low + (high + MIDDLE)) * (128 / step) + least)
    return jnp.where(code < 0, -value, value)


def kernel(
    x_ref, a_ref, w_ref, b_ref, c_ref, lin_ref, sq_ref, cube_ref, y_ref, r_ref,
    grad_ref,
    xv, av, wv, bv, sv, mv, om, ev, et, ea, wm, ow, opened, zv, zc, zbuf, psum, pack, pbuf,
    rr, gv, gbuf, gc, xbuf, hv, hc, hbuf, back,
    y_token, z_token, x_token, load_sem, in_send, in_recv, wt_send, wt_recv, pk_send, pk_recv,
    z_send, z_recv, p_send, p_recv, r_send, r_recv, g_send, g_recv, x_send, x_recv,
    h_send, h_recv, f_send, f_recv, e_send, e_recv, k_send, k_recv,
):
    party = lax.axis_index("party")
    xi = lax.axis_index("sample_0")
    hi = lax.axis_index("sample_1")
    core = lax.axis_index("sample_2")
    feat = lax.axis_index("feat")
    select = (party == 0).astype(F32)

    def at_place(p=None, x=None, h=None, c=None, f=None):
        return (
            party if p is None else p,
            xi if x is None else x,
            hi if h is None else h,
            core if c is None else c,
            feat if f is None else f,
        )

    partner = at_place(p=1 - party)
    sibling = at_place(c=1 - core)
    other_z = at_place(p=1 - party, h=lax.rem(hi + 3 + 2 * party, 4))

    def along_y(d):
        return at_place(f=lax.rem(feat + d, FEATS))

    def along_x(d):
        return at_place(x=lax.rem(xi + d, 4))

    def along_z(d):
        return at_place(h=lax.rem(hi + d, 4))

    near_y, near_x, near_z = [along_y(1), along_y(7)], [along_x(1), along_x(3)], [partner, other_z]
    greeted = near_z + [sibling] + near_y + near_x
    barrier = pltpu.get_barrier_semaphore()
    loads = [
        pltpu.make_async_copy(src.at[0], dst, load_sem.at[i])
        for i, (src, dst) in enumerate(
            [(x_ref, xv), (a_ref, av), (w_ref, wv), (b_ref, bv)]
            + [
                (ref, sv.at[i])
                for i, ref in enumerate((c_ref, lin_ref, sq_ref, cube_ref, y_ref, r_ref))
            ]
        )
    ]
    loads[0].start()
    loads[1].start()
    for place in greeted:
        pl.semaphore_signal(barrier, inc=1, device_id=place, device_id_type=MESH)
    for load in loads[2:]:
        load.start()

    loads[0].wait()
    loads[1].wait()
    mv[...] = (xv[...].astype(F32) - av[...].astype(F32)).astype(BF16)
    pl.semaphore_wait(barrier, len(greeted))

    def pass_on(r):
        for token, places in ((y_token, near_y), (z_token, near_z), (x_token, near_x)):
            if r < token.shape[0]:
                for place in places:
                    pl.semaphore_signal(token.at[r], inc=1, device_id=place, device_id_type=MESH)

    def hear(r):
        for token in (y_token, z_token, x_token):
            if r < token.shape[0]:
                pl.semaphore_wait(token.at[r], 2)

    sent = []

    def remote(src, dst, send, recv, place):
        copy = pltpu.make_async_remote_copy(
            src_ref=src, dst_ref=dst, send_sem=send, recv_sem=recv,
            device_id=place, device_id_type=MESH,
        )
        copy.start()
        sent.append(copy)
        return copy

    def slab(first, size):
        return pl.ds(pl.multiple_of(first, size), size)

    inputs = []
    for k in range(CHUNKS):
        rows = pl.ds(k * CHUNK, CHUNK)
        inputs.append(remote(mv.at[rows], om.at[rows], in_send.at[k], in_recv.at[k], partner))
    my_half = slab(core * HALF, HALF)
    loads[2].wait()
    loads[3].wait()
    wm[...] = (wv[...] - bv[...].astype(F32)).astype(BF16)
    weights = remote(wm.at[my_half], ow.at[my_half], wt_send.at[0], wt_recv.at[0], other_z)
    pass_on(0)

    for load in loads[4:]:
        load.wait()
    for i in range(SMALL):
        for j in range(BLOCKS):
            pack[i, pl.ds(j * PIECE, PIECE), :] = sv[i, slab(j * BLOCK + feat * PIECE, PIECE), :]
    packed = remote(pack, pbuf, pk_send.at[0], pk_recv.at[0], partner)

    ea[:, ROWS:] = av[...].T
    hear(0)
    pass_on(1)
    hear(1)
    pass_on(2)
    hear(2)
    weights.wait_recv()
    passed = remote(ow.at[my_half], ow.at[my_half], wt_send.at[1], wt_recv.at[1], sibling)
    passed.wait_recv()
    opened[...] = (wm[...].astype(F32) + ow[...].astype(F32)).astype(BF16)
    zv[...] = jnp.dot(av[...], opened[...], preferred_element_type=F32)

    def margins(k):
        rows = pl.ds(k * CHUNK, CHUNK)
        inputs[k].wait_recv()
        part = (mv[rows, :].astype(F32) + om[rows, :].astype(F32)).astype(BF16)
        ev[rows, :] = part
        both = select * jnp.dot(part, opened[...], preferred_element_type=F32)
        total = zv[rows, :] + both + jnp.dot(part, bv[...], preferred_element_type=F32)
        zv[rows, :] = total
        zc[rows, :] = coded(total, MARGIN)

    def share(j):
        copies = []
        for d in ALONG:
            rows = slab(j * BLOCK + lax.rem(feat + d, FEATS) * PIECE, PIECE)
            copies.append(
                remote(zc.at[rows], zbuf.at[j, d], z_send.at[j, d], z_recv.at[j, d], along_y(d))
            )
        return copies

    def add_up(j, copies):
        for copy in copies:
            copy.wait_recv()
        total = zv[slab(j * BLOCK + feat * PIECE, PIECE), :]
        for d in range(1, FEATS):
            total = total + decoded(zbuf[j, d], MARGIN)
        psum[j, 0] = total
        return remote(psum.at[j, 0], psum.at[j, 1], p_send.at[j], p_recv.at[j], partner)

    def residuals(j, copy):
        copy.wait_recv()
        own_rows = pl.ds(j * PIECE, PIECE)
        own = [pack[i, own_rows, :].astype(F32) for i in range(SMALL)]
        far = [pbuf[i, own_rows, :].astype(F32) for i in range(SMALL)]
        own_margin, far_margin = psum[j, 0] + own[0], psum[j, 1] + far[0]
        spread = (own_margin - own[1]) + (far_margin - far[1])

        def masked(s, margin, value):
            cubed = s * (spread * spread * spread) + 3.0 * (spread * spread) * value[1]
            cubed = cubed + 3.0 * spread * value[2] + value[3]
            result = 0.5 * s + slope_one * margin - cube_coef * cubed - value[4]
            return (result - value[5]).astype(BF16).astype(F32)

        both = masked(select, own_margin, own) + masked(1.0 - select, far_margin, far)
        rows = slab(j * BLOCK + feat * PIECE, PIECE)
        rr[rows, :] = both.astype(BF16)
        return [
            remote(rr.at[rows], rr.at[rows], r_send.at[j, d], r_recv.at[j, d], along_y(d))
            for d in ALONG
        ]

    def turned(j):
        rows = pl.ds(j * BLOCK, BLOCK)
        flipped = ev[rows, :].T
        et[:, rows] = flipped
        ea[:, rows] = (flipped.astype(F32) * select).astype(BF16)

    margins(0)
    margins(1)
    shared_0 = share(0)
    turned(0)
    margins(2)
    margins(3)
    shared_1 = share(1)
    summed_0 = add_up(0, shared_0)
    packed.wait_recv()
    opened_0 = residuals(0, summed_0)
    turned(1)
    gv[...] = jnp.dot(et[...], sv[SMALL - 1], preferred_element_type=F32)
    summed_1 = add_up(1, shared_1)
    opened_1 = residuals(1, summed_1)
    for copy in opened_0 + opened_1:
        copy.wait_recv()
    rr[ROWS:, :] = rr[:ROWS, :]

    def terms(first):
        rows = slab(first, SUB)
        return gv[rows, :] + jnp.dot(ea[rows, :], rr[...], preferred_element_type=F32)

    crossing = []
    for n in range(SUBS):
        their = slab((1 - core) * HALF + n * SUB, SUB)
        gv[their, :] = terms((1 - core) * HALF + n * SUB)
        crossing.append(remote(gv.at[their], gbuf.at[n], g_send.at[n], g_recv.at[n], sibling))
    for n in range(SUBS):
        gv[slab(core * HALF + n * SUB, SUB), :] = terms(core * HALF + n * SUB)

    quarters = []
    for n in range(SUBS):
        crossing[n].wait_recv()
        total = gbuf[n] + gv[slab(core * HALF + n * SUB, SUB), :]
        gbuf[n] = total
        gc[n] = coded(total, GRADIENT)
        quarters.append(
            [
                remote(
                    gc.at[n, slab(lax.rem(xi + d, 4) * QUARTER, QUARTER)],
                    xbuf.at[n, d], x_send.at[n, d], x_recv.at[n, d], along_x(d),
                )
                for d in (2, 1, 3)
            ]
        )
    lasts = []
    for n in range(SUBS):
        for copy in quarters[n]:
            copy.wait_recv()
        total = gbuf[n, slab(xi * QUARTER, QUARTER), :]
        total = total + decoded(xbuf[n, 1], GRADIENT) + decoded(xbuf[n, 2], GRADIENT) + decoded(xbuf[n, 3], GRADIENT)
        hv[n] = total
        hc[n] = coded(total, GRADIENT)
        lasts.append(
            [
                remote(
                    hc.at[n, slab(lax.rem(hi + d, 4) * LAST, LAST)],
                    hbuf.at[n, d], h_send.at[n, d], h_recv.at[n, d], along_z(d),
                )
                for d in (2, 1, 3)
            ]
        )
    back_z = []
    for n in range(SUBS):
        for copy in lasts[n]:
            copy.wait_recv()
        total = hv[n, slab(hi * LAST, LAST), :]
        total = total + decoded(hbuf[n, 1], GRADIENT) + decoded(hbuf[n, 2], GRADIENT) + decoded(hbuf[n, 3], GRADIENT)
        rows = slab(core * HALF + n * SUB + xi * QUARTER + hi * LAST, LAST)
        back[rows, :] = coded(total, GRADIENT)
        back_z.append(
            [
                remote(back.at[rows], back.at[rows], f_send.at[n, d], f_recv.at[n, d], along_z(d))
                for d in (2, 1, 3)
            ]
        )
    back_x = []
    for n in range(SUBS):
        for copy in back_z[n]:
            copy.wait_recv()
        rows = slab(core * HALF + n * SUB + xi * QUARTER, QUARTER)
        back_x.append(
            [
                remote(back.at[rows], back.at[rows], e_send.at[n, d], e_recv.at[n, d], along_x(d))
                for d in (2, 1, 3)
            ]
        )
    back_core = []
    for n in range(SUBS):
        for copy in back_x[n]:
            copy.wait_recv()
        rows = slab(core * HALF + n * SUB, SUB)
        back_core.append(
            remote(back.at[rows], back.at[rows], k_send.at[n], k_recv.at[n], sibling)
        )
    for n in range(SUBS):
        rows = slab(core * HALF + n * SUB, SUB)
        grad_ref[rows, :] = decoded(back[rows, :], GRADIENT)
    for n in range(SUBS):
        back_core[n].wait_recv()
        rows = slab((1 - core) * HALF + n * SUB, SUB)
        grad_ref[rows, :] = decoded(back[rows, :], GRADIENT)
    for copy in sent:
        copy.wait_send()


def gradient(x, a, w, b, c, lin, sq, cube, y, r):
    dma = pltpu.SemaphoreType.DMA
    return pl.pallas_call(
        kernel,
        out_shape=pltpu.VMEM((COLS, PH), F32),
        in_specs=[pl.BlockSpec(memory_space=pltpu.HBM)] * 10,
        out_specs=pl.BlockSpec(memory_space=pltpu.VMEM),
        scratch_shapes=[
            pltpu.VMEM((ROWS, COLS), BF16),
            pltpu.VMEM((ROWS, COLS), BF16),
            pltpu.VMEM((COLS, PH), F32),
            pltpu.VMEM((COLS, PH), BF16),
            pltpu.VMEM((SMALL, ROWS, PH), BF16),
            pltpu.VMEM((ROWS, COLS), BF16),
            pltpu.VMEM((ROWS, COLS), BF16),
            pltpu.VMEM((ROWS, COLS), BF16),
            pltpu.VMEM((COLS, ROWS), BF16),
            pltpu.VMEM((COLS, 2 * ROWS), BF16),
            pltpu.VMEM((COLS, PH), BF16),
            pltpu.VMEM((COLS, PH), BF16),
            pltpu.VMEM((COLS, PH), BF16),
            pltpu.VMEM((ROWS, PH), F32),
            pltpu.VMEM((ROWS, PH), BF16),
            pltpu.VMEM((BLOCKS, FEATS, PIECE, PH), BF16),
            pltpu.VMEM((BLOCKS, 2, PIECE, PH), F32),
            pltpu.VMEM((SMALL, BLOCKS * PIECE, PH), BF16),
            pltpu.VMEM((SMALL, BLOCKS * PIECE, PH), BF16),
            pltpu.VMEM((2 * ROWS, PH), BF16),
            pltpu.VMEM((COLS, PH), F32),
            pltpu.VMEM((SUBS, SUB, PH), F32),
            pltpu.VMEM((SUBS, SUB, PH), BF16),
            pltpu.VMEM((SUBS, 4, QUARTER, PH), BF16),
            pltpu.VMEM((SUBS, QUARTER, PH), F32),
            pltpu.VMEM((SUBS, QUARTER, PH), BF16),
            pltpu.VMEM((SUBS, 4, LAST, PH), BF16),
            pltpu.VMEM((COLS, PH), BF16),
            pltpu.SemaphoreType.REGULAR((3,)),
            pltpu.SemaphoreType.REGULAR((3,)),
            pltpu.SemaphoreType.REGULAR((1,)),
            dma((10,)),
            dma((CHUNKS,)), dma((CHUNKS,)),
            dma((2,)), dma((2,)),
            dma((1,)), dma((1,)),
            dma((BLOCKS, FEATS)), dma((BLOCKS, FEATS)),
            dma((BLOCKS,)), dma((BLOCKS,)),
            dma((BLOCKS, FEATS)), dma((BLOCKS, FEATS)),
            dma((SUBS,)), dma((SUBS,)),
            dma((SUBS, 4)), dma((SUBS, 4)),
            dma((SUBS, 4)), dma((SUBS, 4)),
            dma((SUBS, 4)), dma((SUBS, 4)),
            dma((SUBS, 4)), dma((SUBS, 4)),
            dma((SUBS,)), dma((SUBS,)),
        ],
        compiler_params=pltpu.CompilerParams(
            collective_id=0, has_side_effects=True, vmem_limit_bytes=60 * 2**20
        ),
        cost_estimate=pl.CostEstimate(
            flops=12 * ROWS * COLS * PH, bytes_accessed=5 * 2**20, transcendentals=0
        ),
    )(x, a, w, b, c, lin, sq, cube, y, r)


def shards(x, a, w, b, c, lin, sq, cube, y, r, grad_product):
    grad = gradient(x, a, w, b, c, lin, sq, cube, y, r)
    samples = x.shape[1] * lax.axis_size(SAMPLE)
    whole = grad + grad_product[0].astype(F32)
    return (w[0] - learn_rate / samples * whole)[None]


def solution(mesh):
    torus = Mesh(
        mesh.devices.reshape(mesh.shape["party"], 4, 4, 2, mesh.shape["feat"]),
        ("party", "sample_0", "sample_1", "sample_2", "feat"),
    )
    return jax.shard_map(
        shards,
        mesh=torus,
        in_specs=(
            P("party", SAMPLE, "feat"),
            P("party", SAMPLE, "feat"),
            P("party", "feat", None),
            P("party", "feat", None),
            P("party", SAMPLE, None),
            P("party", SAMPLE, None),
            P("party", SAMPLE, None),
            P("party", SAMPLE, None),
            P("party", SAMPLE, None),
            P("party", SAMPLE, None),
            P("party", "feat", None),
        ),
        out_specs=P("party", "feat", None),
        check_vma=False,
    )
```

```python
import jax
import jax.numpy as jnp
from jax import lax
from jax.experimental import pallas as pl
from jax.experimental.pallas import tpu as pltpu
from jax.sharding import Mesh
from jax.sharding import PartitionSpec as P

SAMPLE = ("sample_0", "sample_1", "sample_2")
MESH = pl.DeviceIdType.MESH
F32 = jnp.float32
BF16 = jnp.bfloat16

learn_rate = 64.0
slope_one = 0.197
cube_coef = 0.004

ROWS = 256
COLS = 1024
PH = 256
CHUNK = 64
CHUNKS = ROWS // CHUNK
BLOCKS = 2
BLOCK = ROWS // BLOCKS
PER = CHUNKS // BLOCKS
FEATS = 8
PIECE = BLOCK // FEATS
HALF = COLS // 2
SUBS = 4
SUB = HALF // SUBS
QUARTER = SUB // 4
SMALL = 6
ALONG = (4, 3, 5, 2, 6, 1, 7)
MIDDLE = 120.0
GRADIENT = (-22.0, 384.0)
MARGIN = (-14.0, 960.0)


def coded(value, span):
    least, step = span
    level = jnp.log2(jnp.maximum(jnp.abs(value), 2.0**least)) - least
    level = jnp.floor(level * step + 0.5)
    high = jnp.floor(level * (1 / 128))
    code = jnp.exp2(high - MIDDLE) * (1.0 + (level - 128.0 * high) * (1 / 128))
    return jnp.where(value < 0, -code, code).astype(BF16)


def decoded(code, span):
    least, step = span
    code = code.astype(F32)
    size = jnp.abs(code)
    high = jnp.floor(jnp.log2(size) + 0.003)
    low = size * jnp.exp2(-high) - 1.0
    value = jnp.exp2((low + (high + MIDDLE)) * (128 / step) + least)
    return jnp.where(code < 0, -value, value)


def kernel(
    x_ref, a_ref, w_ref, b_ref, c_ref, lin_ref, sq_ref, cube_ref, y_ref, r_ref,
    grad_ref,
    xv, av, wv, bv, sv, mv, om, ev, et, ea, wm, ow, opened, zv, zc, zbuf, psum, pack, pbuf,
    rr, gv, gbuf, gc, xbuf, hbuf, back,
    y_token, z_token, x_token, load_sem, first_sem, in_send, in_recv, wt_send, wt_recv, pk_send, pk_recv,
    z_send, z_recv, p_send, p_recv, r_send, r_recv, g_send, g_recv, x_send, x_recv,
    h_send, h_recv, e_send, e_recv, k_send, k_recv,
):
    party = lax.axis_index("party")
    xi = lax.axis_index("sample_0")
    hi = lax.axis_index("sample_1")
    core = lax.axis_index("sample_2")
    feat = lax.axis_index("feat")
    select = (party == 0).astype(F32)

    def at_place(p=None, x=None, h=None, c=None, f=None):
        return (
            party if p is None else p,
            xi if x is None else x,
            hi if h is None else h,
            core if c is None else c,
            feat if f is None else f,
        )

    partner = at_place(p=1 - party)
    sibling = at_place(c=1 - core)
    other_z = at_place(p=1 - party, h=lax.rem(hi + 3 + 2 * party, 4))

    def along_y(d):
        return at_place(f=lax.rem(feat + d, FEATS))

    def along_x(d):
        return at_place(x=lax.rem(xi + d, 4))

    def along_z(d):
        return at_place(h=lax.rem(hi + d, 4))

    near_y, near_x, near_z = [along_y(1), along_y(7)], [along_x(1), along_x(3)], [partner, other_z]
    greeted = near_z + [sibling] + near_y + near_x
    barrier = pltpu.get_barrier_semaphore()
    loads = [
        pltpu.make_async_copy(src.at[0], dst, load_sem.at[i])
        for i, (src, dst) in enumerate(
            [(w_ref, wv), (b_ref, bv)]
            + [
                (ref, sv.at[i])
                for i, ref in enumerate((c_ref, lin_ref, sq_ref, cube_ref, y_ref, r_ref))
            ]
        )
    ]
    first_loads = []
    for k in range(CHUNKS):
        rows = pl.ds(k * CHUNK, CHUNK)
        for i, (src, dst) in enumerate([(x_ref, xv), (a_ref, av)]):
            first_loads.append(
                pltpu.make_async_copy(src.at[0, rows], dst.at[rows], first_sem.at[k, i])
            )
            first_loads[-1].start()
    for place in greeted:
        pl.semaphore_signal(barrier, inc=1, device_id=place, device_id_type=MESH)
    for load in loads:
        load.start()


    def masked_chunk(k):
        first_loads[2 * k].wait()
        first_loads[2 * k + 1].wait()
        rows = pl.ds(k * CHUNK, CHUNK)
        mv[rows, :] = (xv[rows, :].astype(F32) - av[rows, :].astype(F32)).astype(BF16)

    masked_chunk(0)
    pl.semaphore_wait(barrier, len(greeted))

    def pass_on(r):
        for token, places in ((y_token, near_y), (z_token, near_z), (x_token, near_x)):
            if r < token.shape[0]:
                for place in places:
                    pl.semaphore_signal(token.at[r], inc=1, device_id=place, device_id_type=MESH)

    def hear(r):
        for token in (y_token, z_token, x_token):
            if r < token.shape[0]:
                pl.semaphore_wait(token.at[r], 2)

    sent = []

    def remote(src, dst, send, recv, place):
        copy = pltpu.make_async_remote_copy(
            src_ref=src, dst_ref=dst, send_sem=send, recv_sem=recv,
            device_id=place, device_id_type=MESH,
        )
        copy.start()
        sent.append(copy)
        return copy

    def slab(first, size):
        return pl.ds(pl.multiple_of(first, size), size)

    inputs = []
    for k in range(CHUNKS):
        if k > 0:
            masked_chunk(k)
        rows = pl.ds(k * CHUNK, CHUNK)
        inputs.append(remote(mv.at[rows], om.at[rows], in_send.at[k], in_recv.at[k], partner))
    my_half = slab(core * HALF, HALF)
    loads[0].wait()
    loads[1].wait()
    wm[...] = (wv[...] - bv[...].astype(F32)).astype(BF16)
    weights = remote(wm.at[my_half], ow.at[my_half], wt_send.at[0], wt_recv.at[0], other_z)
    pass_on(0)

    for load in loads[2:]:
        load.wait()
    for i in range(SMALL):
        for j in range(BLOCKS):
            pack[i, pl.ds(j * PIECE, PIECE), :] = sv[i, slab(j * BLOCK + feat * PIECE, PIECE), :]
    packed = remote(pack, pbuf, pk_send.at[0], pk_recv.at[0], partner)

    ea[:, ROWS:] = av[...].T
    hear(0)
    pass_on(1)
    hear(1)
    pass_on(2)
    hear(2)
    weights.wait_recv()
    passed = remote(ow.at[my_half], ow.at[my_half], wt_send.at[1], wt_recv.at[1], sibling)
    passed.wait_recv()
    opened[...] = (wm[...].astype(F32) + ow[...].astype(F32)).astype(BF16)
    zv[...] = jnp.dot(av[...], opened[...], preferred_element_type=F32)

    def margins(k):
        rows = pl.ds(k * CHUNK, CHUNK)
        inputs[k].wait_recv()
        part = (mv[rows, :].astype(F32) + om[rows, :].astype(F32)).astype(BF16)
        ev[rows, :] = part
        both = select * jnp.dot(part, opened[...], preferred_element_type=F32)
        total = zv[rows, :] + both + jnp.dot(part, bv[...], preferred_element_type=F32)
        zv[rows, :] = total
        zc[rows, :] = coded(total, MARGIN)

    def share(j):
        copies = []
        for d in ALONG:
            rows = slab(j * BLOCK + lax.rem(feat + d, FEATS) * PIECE, PIECE)
            copies.append(
                remote(zc.at[rows], zbuf.at[j, d], z_send.at[j, d], z_recv.at[j, d], along_y(d))
            )
        return copies

    def add_up(j, copies):
        for copy in copies:
            copy.wait_recv()
        total = zv[slab(j * BLOCK + feat * PIECE, PIECE), :]
        for d in range(1, FEATS):
            total = total + decoded(zbuf[j, d], MARGIN)
        psum[j, 0] = total
        return remote(psum.at[j, 0], psum.at[j, 1], p_send.at[j], p_recv.at[j], partner)

    def residuals(j, copy):
        copy.wait_recv()
        own_rows = pl.ds(j * PIECE, PIECE)
        own = [pack[i, own_rows, :].astype(F32) for i in range(SMALL)]
        far = [pbuf[i, own_rows, :].astype(F32) for i in range(SMALL)]
        own_margin, far_margin = psum[j, 0] + own[0], psum[j, 1] + far[0]
        spread = (own_margin - own[1]) + (far_margin - far[1])

        def masked(s, margin, value):
            cubed = s * (spread * spread * spread) + 3.0 * (spread * spread) * value[1]
            cubed = cubed + 3.0 * spread * value[2] + value[3]
            result = 0.5 * s + slope_one * margin - cube_coef * cubed - value[4]
            return (result - value[5]).astype(BF16).astype(F32)

        both = masked(select, own_margin, own) + masked(1.0 - select, far_margin, far)
        rows = slab(j * BLOCK + feat * PIECE, PIECE)
        rr[rows, :] = both.astype(BF16)
        return [
            remote(rr.at[rows], rr.at[rows], r_send.at[j, d], r_recv.at[j, d], along_y(d))
            for d in ALONG
        ]

    def turned(j):
        rows = pl.ds(j * BLOCK, BLOCK)
        flipped = ev[rows, :].T
        et[:, rows] = flipped
        ea[:, rows] = (flipped.astype(F32) * select).astype(BF16)

    margins(0)
    margins(1)
    shared_0 = share(0)
    turned(0)
    margins(2)
    margins(3)
    shared_1 = share(1)
    summed_0 = add_up(0, shared_0)
    packed.wait_recv()
    opened_0 = residuals(0, summed_0)
    turned(1)
    gv[...] = jnp.dot(et[...], sv[SMALL - 1], preferred_element_type=F32)
    summed_1 = add_up(1, shared_1)
    opened_1 = residuals(1, summed_1)
    for copy in opened_0 + opened_1:
        copy.wait_recv()
    rr[ROWS:, :] = rr[:ROWS, :]

    def terms(first):
        rows = slab(first, SUB)
        return gv[rows, :] + jnp.dot(ea[rows, :], rr[...], preferred_element_type=F32)

    crossing = []
    for n in range(SUBS):
        their = slab((1 - core) * HALF + n * SUB, SUB)
        gv[their, :] = terms((1 - core) * HALF + n * SUB)
        crossing.append(remote(gv.at[their], gbuf.at[n], g_send.at[n], g_recv.at[n], sibling))
    for n in range(SUBS):
        gv[slab(core * HALF + n * SUB, SUB), :] = terms(core * HALF + n * SUB)

    quarters = []
    for n in range(SUBS):
        crossing[n].wait_recv()
        total = gbuf[n] + gv[slab(core * HALF + n * SUB, SUB), :]
        gbuf[n] = total
        gc[n] = coded(total, GRADIENT)
        quarters.append(
            [
                remote(
                    gc.at[n, slab(lax.rem(xi + d, 4) * QUARTER, QUARTER)],
                    xbuf.at[n, d], x_send.at[n, d], x_recv.at[n, d], along_x(d),
                )
                for d in (2, 1, 3)
            ]
        )
    lasts = []
    for n in range(SUBS):
        for copy in quarters[n]:
            copy.wait_recv()
        total = gbuf[n, slab(xi * QUARTER, QUARTER), :]
        for d in (1, 2, 3):
            total = total + decoded(xbuf[n, d], GRADIENT)
        hbuf[n, hi] = coded(total, GRADIENT)
        lasts.append(
            [
                remote(hbuf.at[n, hi], hbuf.at[n, hi], h_send.at[n, d], h_recv.at[n, d], along_z(d))
                for d in (2, 1, 3)
            ]
        )
    back_x = []
    for n in range(SUBS):
        for copy in lasts[n]:
            copy.wait_recv()
        total = decoded(hbuf[n, 0], GRADIENT) + decoded(hbuf[n, 1], GRADIENT)
        total = total + (decoded(hbuf[n, 2], GRADIENT) + decoded(hbuf[n, 3], GRADIENT))
        rows = slab(core * HALF + n * SUB + xi * QUARTER, QUARTER)
        back[rows, :] = coded(total, GRADIENT)
        back_x.append(
            [
                remote(back.at[rows], back.at[rows], e_send.at[n, d], e_recv.at[n, d], along_x(d))
                for d in (2, 1, 3)
            ]
        )
    back_core = []
    for n in range(SUBS):
        for copy in back_x[n]:
            copy.wait_recv()
        rows = slab(core * HALF + n * SUB, SUB)
        back_core.append(
            remote(back.at[rows], back.at[rows], k_send.at[n], k_recv.at[n], sibling)
        )
    for n in range(SUBS):
        rows = slab(core * HALF + n * SUB, SUB)
        grad_ref[rows, :] = decoded(back[rows, :], GRADIENT)
    for n in range(SUBS):
        back_core[n].wait_recv()
        rows = slab((1 - core) * HALF + n * SUB, SUB)
        grad_ref[rows, :] = decoded(back[rows, :], GRADIENT)
    for copy in sent:
        copy.wait_send()


def gradient(x, a, w, b, c, lin, sq, cube, y, r):
    dma = pltpu.SemaphoreType.DMA
    return pl.pallas_call(
        kernel,
        out_shape=pltpu.VMEM((COLS, PH), F32),
        in_specs=[pl.BlockSpec(memory_space=pltpu.HBM)] * 10,
        out_specs=pl.BlockSpec(memory_space=pltpu.VMEM),
        scratch_shapes=[
            pltpu.VMEM((ROWS, COLS), BF16),
            pltpu.VMEM((ROWS, COLS), BF16),
            pltpu.VMEM((COLS, PH), F32),
            pltpu.VMEM((COLS, PH), BF16),
            pltpu.VMEM((SMALL, ROWS, PH), BF16),
            pltpu.VMEM((ROWS, COLS), BF16),
            pltpu.VMEM((ROWS, COLS), BF16),
            pltpu.VMEM((ROWS, COLS), BF16),
            pltpu.VMEM((COLS, ROWS), BF16),
            pltpu.VMEM((COLS, 2 * ROWS), BF16),
            pltpu.VMEM((COLS, PH), BF16),
            pltpu.VMEM((COLS, PH), BF16),
            pltpu.VMEM((COLS, PH), BF16),
            pltpu.VMEM((ROWS, PH), F32),
            pltpu.VMEM((ROWS, PH), BF16),
            pltpu.VMEM((BLOCKS, FEATS, PIECE, PH), BF16),
            pltpu.VMEM((BLOCKS, 2, PIECE, PH), F32),
            pltpu.VMEM((SMALL, BLOCKS * PIECE, PH), BF16),
            pltpu.VMEM((SMALL, BLOCKS * PIECE, PH), BF16),
            pltpu.VMEM((2 * ROWS, PH), BF16),
            pltpu.VMEM((COLS, PH), F32),
            pltpu.VMEM((SUBS, SUB, PH), F32),
            pltpu.VMEM((SUBS, SUB, PH), BF16),
            pltpu.VMEM((SUBS, 4, QUARTER, PH), BF16),
            pltpu.VMEM((SUBS, 4, QUARTER, PH), BF16),
            pltpu.VMEM((COLS, PH), BF16),
            pltpu.SemaphoreType.REGULAR((3,)),
            pltpu.SemaphoreType.REGULAR((3,)),
            pltpu.SemaphoreType.REGULAR((1,)),
            dma((8,)),
            dma((CHUNKS, 2)),
            dma((CHUNKS,)), dma((CHUNKS,)),
            dma((2,)), dma((2,)),
            dma((1,)), dma((1,)),
            dma((BLOCKS, FEATS)), dma((BLOCKS, FEATS)),
            dma((BLOCKS,)), dma((BLOCKS,)),
            dma((BLOCKS, FEATS)), dma((BLOCKS, FEATS)),
            dma((SUBS,)), dma((SUBS,)),
            dma((SUBS, 4)), dma((SUBS, 4)),
            dma((SUBS, 4)), dma((SUBS, 4)),
            dma((SUBS, 4)), dma((SUBS, 4)),
            dma((SUBS,)), dma((SUBS,)),
        ],
        compiler_params=pltpu.CompilerParams(
            collective_id=0, has_side_effects=True, vmem_limit_bytes=60 * 2**20
        ),
        cost_estimate=pl.CostEstimate(
            flops=12 * ROWS * COLS * PH, bytes_accessed=5 * 2**20, transcendentals=0
        ),
    )(x, a, w, b, c, lin, sq, cube, y, r)


def shards(x, a, w, b, c, lin, sq, cube, y, r, grad_product):
    grad = gradient(x, a, w, b, c, lin, sq, cube, y, r)
    samples = x.shape[1] * lax.axis_size(SAMPLE)
    whole = grad + grad_product[0].astype(F32)
    return (w[0] - learn_rate / samples * whole)[None]


def solution(mesh):
    torus = Mesh(
        mesh.devices.reshape(mesh.shape["party"], 4, 4, 2, mesh.shape["feat"]),
        ("party", "sample_0", "sample_1", "sample_2", "feat"),
    )
    return jax.shard_map(
        shards,
        mesh=torus,
        in_specs=(
            P("party", SAMPLE, "feat"),
            P("party", SAMPLE, "feat"),
            P("party", "feat", None),
            P("party", "feat", None),
            P("party", SAMPLE, None),
            P("party", SAMPLE, None),
            P("party", SAMPLE, None),
            P("party", SAMPLE, None),
            P("party", SAMPLE, None),
            P("party", SAMPLE, None),
            P("party", "feat", None),
        ),
        out_specs=P("party", "feat", None),
        check_vma=False,
    )
```

```python
import functools

import jax
import jax.numpy as jnp
from jax import lax
from jax.experimental import pallas as pl
from jax.experimental.pallas import tpu as pltpu
from jax.sharding import Mesh
from jax.sharding import PartitionSpec as P

SAMPLE = ("sample_0", "sample_1", "sample_2")
MESH = pl.DeviceIdType.MESH
F32 = jnp.float32
BF16 = jnp.bfloat16

learn_rate = 64.0
slope_one = 0.197
cube_coef = 0.004

ROWS = 256
COLS = 1024
PH = 256
CHUNK = 64
CHUNKS = ROWS // CHUNK
BLOCKS = 2
BLOCK = ROWS // BLOCKS
PER = CHUNKS // BLOCKS
FEATS = 8
PIECE = BLOCK // FEATS
HALF = COLS // 2
SUBS = 4
SUB = HALF // SUBS
QUARTER = SUB // 4
SMALL = 6
ALONG = (4, 3, 5, 2, 6, 1, 7)
MIDDLE = 120.0
GRADIENT = (-22.0, 384.0)
MARGIN = (-14.0, 960.0)


def coded(value, span):
    least, step = span
    level = jnp.log2(jnp.maximum(jnp.abs(value), 2.0**least)) - least
    level = jnp.floor(level * step + 0.5)
    high = jnp.floor(level * (1 / 128))
    code = jnp.exp2(high - MIDDLE) * (1.0 + (level - 128.0 * high) * (1 / 128))
    return jnp.where(value < 0, -code, code).astype(BF16)


def decoded(code, span):
    least, step = span
    code = code.astype(F32)
    size = jnp.abs(code)
    high = jnp.floor(jnp.log2(size) + 0.003)
    low = size * jnp.exp2(-high) - 1.0
    value = jnp.exp2((low + (high + MIDDLE)) * (128 / step) + least)
    return jnp.where(code < 0, -value, value)


def kernel(
    samples,
    x_ref, a_ref, w_ref, b_ref, c_ref, lin_ref, sq_ref, cube_ref, y_ref, r_ref, p_ref,
    new_ref,
    xv, av, wv, bv, pv, sv, mv, om, ev, et, ea, wm, ow, opened, zv, zc, zbuf, psum, pack, pbuf,
    rr, gv, gbuf, gc, xbuf, hbuf, back,
    y_token, z_token, x_token, load_sem, first_sem, in_send, in_recv, wt_send, wt_recv, pk_send, pk_recv,
    z_send, z_recv, p_send, p_recv, r_send, r_recv, g_send, g_recv, x_send, x_recv,
    h_send, h_recv, e_send, e_recv, k_send, k_recv,
):
    party = lax.axis_index("party")
    xi = lax.axis_index("sample_0")
    hi = lax.axis_index("sample_1")
    core = lax.axis_index("sample_2")
    feat = lax.axis_index("feat")
    select = (party == 0).astype(F32)

    def at_place(p=None, x=None, h=None, c=None, f=None):
        return (
            party if p is None else p,
            xi if x is None else x,
            hi if h is None else h,
            core if c is None else c,
            feat if f is None else f,
        )

    partner = at_place(p=1 - party)
    sibling = at_place(c=1 - core)
    other_z = at_place(p=1 - party, h=lax.rem(hi + 3 + 2 * party, 4))

    def along_y(d):
        return at_place(f=lax.rem(feat + d, FEATS))

    def along_x(d):
        return at_place(x=lax.rem(xi + d, 4))

    def along_z(d):
        return at_place(h=lax.rem(hi + d, 4))

    near_y, near_x, near_z = [along_y(1), along_y(7)], [along_x(1), along_x(3)], [partner, other_z]
    greeted = near_z + [sibling] + near_y + near_x
    barrier = pltpu.get_barrier_semaphore()
    loads = [
        pltpu.make_async_copy(src.at[0], dst, load_sem.at[i])
        for i, (src, dst) in enumerate(
            [(w_ref, wv), (b_ref, bv)]
            + [
                (ref, sv.at[i])
                for i, ref in enumerate((c_ref, lin_ref, sq_ref, cube_ref, y_ref, r_ref))
            ]
        )
    ]
    first_loads = []
    for k in range(CHUNKS):
        rows = pl.ds(k * CHUNK, CHUNK)
        for i, (src, dst) in enumerate([(x_ref, xv), (a_ref, av)]):
            first_loads.append(
                pltpu.make_async_copy(src.at[0, rows], dst.at[rows], first_sem.at[k, i])
            )
            first_loads[-1].start()
    for place in greeted:
        pl.semaphore_signal(barrier, inc=1, device_id=place, device_id_type=MESH)
    for load in loads:
        load.start()


    def masked_chunk(k):
        first_loads[2 * k].wait()
        first_loads[2 * k + 1].wait()
        rows = pl.ds(k * CHUNK, CHUNK)
        mv[rows, :] = (xv[rows, :].astype(F32) - av[rows, :].astype(F32)).astype(BF16)

    masked_chunk(0)
    pl.semaphore_wait(barrier, len(greeted))

    def pass_on(r):
        for token, places in ((y_token, near_y), (z_token, near_z), (x_token, near_x)):
            if r < token.shape[0]:
                for place in places:
                    pl.semaphore_signal(token.at[r], inc=1, device_id=place, device_id_type=MESH)

    def hear(r):
        for token in (y_token, z_token, x_token):
            if r < token.shape[0]:
                pl.semaphore_wait(token.at[r], 2)

    sent = []

    def remote(src, dst, send, recv, place):
        copy = pltpu.make_async_remote_copy(
            src_ref=src, dst_ref=dst, send_sem=send, recv_sem=recv,
            device_id=place, device_id_type=MESH,
        )
        copy.start()
        sent.append(copy)
        return copy

    def slab(first, size):
        return pl.ds(pl.multiple_of(first, size), size)

    inputs = []
    for k in range(CHUNKS):
        if k > 0:
            masked_chunk(k)
        rows = pl.ds(k * CHUNK, CHUNK)
        inputs.append(remote(mv.at[rows], om.at[rows], in_send.at[k], in_recv.at[k], partner))
    my_half = slab(core * HALF, HALF)
    loads[0].wait()
    loads[1].wait()
    wm[...] = (wv[...] - bv[...].astype(F32)).astype(BF16)
    weights = remote(wm.at[my_half], ow.at[my_half], wt_send.at[0], wt_recv.at[0], other_z)
    pass_on(0)

    for load in loads[2:]:
        load.wait()
    load_p = pltpu.make_async_copy(p_ref.at[0], pv, load_sem.at[8])
    load_p.start()
    for i in range(SMALL):
        for j in range(BLOCKS):
            pack[i, pl.ds(j * PIECE, PIECE), :] = sv[i, slab(j * BLOCK + feat * PIECE, PIECE), :]
    packed = remote(pack, pbuf, pk_send.at[0], pk_recv.at[0], partner)

    ea[:, ROWS:] = av[...].T
    hear(0)
    pass_on(1)
    hear(1)
    pass_on(2)
    hear(2)
    weights.wait_recv()
    passed = remote(ow.at[my_half], ow.at[my_half], wt_send.at[1], wt_recv.at[1], sibling)
    passed.wait_recv()
    opened[...] = (wm[...].astype(F32) + ow[...].astype(F32)).astype(BF16)
    zv[...] = jnp.dot(av[...], opened[...], preferred_element_type=F32)

    def margins(k):
        rows = pl.ds(k * CHUNK, CHUNK)
        inputs[k].wait_recv()
        part = (mv[rows, :].astype(F32) + om[rows, :].astype(F32)).astype(BF16)
        ev[rows, :] = part
        both = select * jnp.dot(part, opened[...], preferred_element_type=F32)
        total = zv[rows, :] + both + jnp.dot(part, bv[...], preferred_element_type=F32)
        zv[rows, :] = total
        zc[rows, :] = coded(total, MARGIN)

    def share(j):
        copies = []
        for d in ALONG:
            rows = slab(j * BLOCK + lax.rem(feat + d, FEATS) * PIECE, PIECE)
            copies.append(
                remote(zc.at[rows], zbuf.at[j, d], z_send.at[j, d], z_recv.at[j, d], along_y(d))
            )
        return copies

    def add_up(j, copies):
        for copy in copies:
            copy.wait_recv()
        total = zv[slab(j * BLOCK + feat * PIECE, PIECE), :]
        for d in range(1, FEATS):
            total = total + decoded(zbuf[j, d], MARGIN)
        psum[j, 0] = total
        return remote(psum.at[j, 0], psum.at[j, 1], p_send.at[j], p_recv.at[j], partner)

    def residuals(j, copy):
        copy.wait_recv()
        own_rows = pl.ds(j * PIECE, PIECE)
        own = [pack[i, own_rows, :].astype(F32) for i in range(SMALL)]
        far = [pbuf[i, own_rows, :].astype(F32) for i in range(SMALL)]
        own_margin, far_margin = psum[j, 0] + own[0], psum[j, 1] + far[0]
        spread = (own_margin - own[1]) + (far_margin - far[1])

        def masked(s, margin, value):
            cubed = s * (spread * spread * spread) + 3.0 * (spread * spread) * value[1]
            cubed = cubed + 3.0 * spread * value[2] + value[3]
            result = 0.5 * s + slope_one * margin - cube_coef * cubed - value[4]
            return (result - value[5]).astype(BF16).astype(F32)

        both = masked(select, own_margin, own) + masked(1.0 - select, far_margin, far)
        rows = slab(j * BLOCK + feat * PIECE, PIECE)
        rr[rows, :] = both.astype(BF16)
        return [
            remote(rr.at[rows], rr.at[rows], r_send.at[j, d], r_recv.at[j, d], along_y(d))
            for d in ALONG
        ]

    def turned(j):
        rows = pl.ds(j * BLOCK, BLOCK)
        flipped = ev[rows, :].T
        et[:, rows] = flipped
        ea[:, rows] = (flipped.astype(F32) * select).astype(BF16)

    margins(0)
    margins(1)
    shared_0 = share(0)
    turned(0)
    margins(2)
    margins(3)
    shared_1 = share(1)
    summed_0 = add_up(0, shared_0)
    packed.wait_recv()
    opened_0 = residuals(0, summed_0)
    turned(1)
    gv[...] = jnp.dot(et[...], sv[SMALL - 1], preferred_element_type=F32)
    summed_1 = add_up(1, shared_1)
    opened_1 = residuals(1, summed_1)
    for copy in opened_0 + opened_1:
        copy.wait_recv()
    rr[ROWS:, :] = rr[:ROWS, :]

    def terms(first):
        rows = slab(first, SUB)
        return gv[rows, :] + jnp.dot(ea[rows, :], rr[...], preferred_element_type=F32)

    crossing, quarters = [], []

    def cross(n):
        rows = slab((1 - core) * HALF + n * SUB, SUB)
        gv[rows, :] = terms((1 - core) * HALF + n * SUB)
        crossing.append(remote(gv.at[rows], gbuf.at[n], g_send.at[n], g_recv.at[n], sibling))

    def keep(n):
        gv[slab(core * HALF + n * SUB, SUB), :] = terms(core * HALF + n * SUB)

    def over_x(n):
        crossing[n].wait_recv()
        total = gbuf[n] + gv[slab(core * HALF + n * SUB, SUB), :]
        gbuf[n] = total
        gc[n] = coded(total, GRADIENT)
        quarters.append(
            [
                remote(
                    gc.at[n, slab(lax.rem(xi + d, 4) * QUARTER, QUARTER)],
                    xbuf.at[n, d], x_send.at[n, d], x_recv.at[n, d], along_x(d),
                )
                for d in (2, 1, 3)
            ]
        )

    for step, n in (
        (cross, 0), (cross, 1), (keep, 0), (cross, 2), (keep, 1), (over_x, 0), (cross, 3),
        (keep, 2), (over_x, 1), (keep, 3), (over_x, 2), (over_x, 3),
    ):
        step(n)

    lasts = []
    for n in range(SUBS):
        for copy in quarters[n]:
            copy.wait_recv()
        total = gbuf[n, slab(xi * QUARTER, QUARTER), :]
        for d in (1, 2, 3):
            total = total + decoded(xbuf[n, d], GRADIENT)
        hbuf[n, hi] = coded(total, GRADIENT)
        lasts.append(
            [
                remote(hbuf.at[n, hi], hbuf.at[n, hi], h_send.at[n, d], h_recv.at[n, d], along_z(d))
                for d in (2, 1, 3)
            ]
        )
    back_x = []
    for n in range(SUBS):
        for copy in lasts[n]:
            copy.wait_recv()
        total = decoded(hbuf[n, 0], GRADIENT) + decoded(hbuf[n, 1], GRADIENT)
        total = total + (decoded(hbuf[n, 2], GRADIENT) + decoded(hbuf[n, 3], GRADIENT))
        rows = slab(core * HALF + n * SUB + xi * QUARTER, QUARTER)
        back[rows, :] = coded(total, GRADIENT)
        back_x.append(
            [
                remote(back.at[rows], back.at[rows], e_send.at[n, d], e_recv.at[n, d], along_x(d))
                for d in (2, 1, 3)
            ]
        )
    def update(first):
        rows = slab(first, SUB)
        whole = decoded(back[rows, :], GRADIENT) + pv[rows, :].astype(F32)
        new_ref[rows, :] = wv[rows, :] - learn_rate / samples * whole

    load_p.wait()
    back_core = []
    for n in range(SUBS):
        for copy in back_x[n]:
            copy.wait_recv()
        rows = slab(core * HALF + n * SUB, SUB)
        back_core.append(
            remote(back.at[rows], back.at[rows], k_send.at[n], k_recv.at[n], sibling)
        )
        update(core * HALF + n * SUB)
    for n in range(SUBS):
        back_core[n].wait_recv()
        update((1 - core) * HALF + n * SUB)
    for copy in sent:
        copy.wait_send()


def updated(samples, *arrays):
    dma = pltpu.SemaphoreType.DMA
    return pl.pallas_call(
        functools.partial(kernel, samples),
        out_shape=pltpu.VMEM((COLS, PH), F32),
        in_specs=[pl.BlockSpec(memory_space=pltpu.HBM)] * len(arrays),
        out_specs=pl.BlockSpec(memory_space=pltpu.VMEM),
        scratch_shapes=[
            pltpu.VMEM((ROWS, COLS), BF16),
            pltpu.VMEM((ROWS, COLS), BF16),
            pltpu.VMEM((COLS, PH), F32),
            pltpu.VMEM((COLS, PH), BF16),
            pltpu.VMEM((COLS, PH), BF16),
            pltpu.VMEM((SMALL, ROWS, PH), BF16),
            pltpu.VMEM((ROWS, COLS), BF16),
            pltpu.VMEM((ROWS, COLS), BF16),
            pltpu.VMEM((ROWS, COLS), BF16),
            pltpu.VMEM((COLS, ROWS), BF16),
            pltpu.VMEM((COLS, 2 * ROWS), BF16),
            pltpu.VMEM((COLS, PH), BF16),
            pltpu.VMEM((COLS, PH), BF16),
            pltpu.VMEM((COLS, PH), BF16),
            pltpu.VMEM((ROWS, PH), F32),
            pltpu.VMEM((ROWS, PH), BF16),
            pltpu.VMEM((BLOCKS, FEATS, PIECE, PH), BF16),
            pltpu.VMEM((BLOCKS, 2, PIECE, PH), F32),
            pltpu.VMEM((SMALL, BLOCKS * PIECE, PH), BF16),
            pltpu.VMEM((SMALL, BLOCKS * PIECE, PH), BF16),
            pltpu.VMEM((2 * ROWS, PH), BF16),
            pltpu.VMEM((COLS, PH), F32),
            pltpu.VMEM((SUBS, SUB, PH), F32),
            pltpu.VMEM((SUBS, SUB, PH), BF16),
            pltpu.VMEM((SUBS, 4, QUARTER, PH), BF16),
            pltpu.VMEM((SUBS, 4, QUARTER, PH), BF16),
            pltpu.VMEM((COLS, PH), BF16),
            pltpu.SemaphoreType.REGULAR((3,)),
            pltpu.SemaphoreType.REGULAR((3,)),
            pltpu.SemaphoreType.REGULAR((1,)),
            dma((9,)),
            dma((CHUNKS, 2)),
            dma((CHUNKS,)), dma((CHUNKS,)),
            dma((2,)), dma((2,)),
            dma((1,)), dma((1,)),
            dma((BLOCKS, FEATS)), dma((BLOCKS, FEATS)),
            dma((BLOCKS,)), dma((BLOCKS,)),
            dma((BLOCKS, FEATS)), dma((BLOCKS, FEATS)),
            dma((SUBS,)), dma((SUBS,)),
            dma((SUBS, 4)), dma((SUBS, 4)),
            dma((SUBS, 4)), dma((SUBS, 4)),
            dma((SUBS, 4)), dma((SUBS, 4)),
            dma((SUBS,)), dma((SUBS,)),
        ],
        compiler_params=pltpu.CompilerParams(
            collective_id=0, has_side_effects=True, vmem_limit_bytes=60 * 2**20
        ),
        cost_estimate=pl.CostEstimate(
            flops=12 * ROWS * COLS * PH, bytes_accessed=5 * 2**20, transcendentals=0
        ),
    )(*arrays)


def shards(*arrays):
    samples = arrays[0].shape[1] * lax.axis_size(SAMPLE)
    return updated(samples, *arrays)[None]


def solution(mesh):
    torus = Mesh(
        mesh.devices.reshape(mesh.shape["party"], 4, 4, 2, mesh.shape["feat"]),
        ("party", "sample_0", "sample_1", "sample_2", "feat"),
    )
    return jax.shard_map(
        shards,
        mesh=torus,
        in_specs=(
            P("party", SAMPLE, "feat"),
            P("party", SAMPLE, "feat"),
            P("party", "feat", None),
            P("party", "feat", None),
            P("party", SAMPLE, None),
            P("party", SAMPLE, None),
            P("party", SAMPLE, None),
            P("party", SAMPLE, None),
            P("party", SAMPLE, None),
            P("party", SAMPLE, None),
            P("party", "feat", None),
        ),
        out_specs=P("party", "feat", None),
        check_vma=False,
    )
```

```python
import functools

import jax
import jax.numpy as jnp
from jax import lax
from jax.experimental import pallas as pl
from jax.experimental.pallas import tpu as pltpu
from jax.sharding import Mesh
from jax.sharding import PartitionSpec as P

SAMPLE = ("sample_0", "sample_1", "sample_2")
MESH = pl.DeviceIdType.MESH
F32 = jnp.float32
BF16 = jnp.bfloat16

learn_rate = 64.0
slope_one = 0.197
cube_coef = 0.004

ROWS = 256
COLS = 1024
PH = 256
CHUNK = 64
CHUNKS = ROWS // CHUNK
BLOCKS = 2
BLOCK = ROWS // BLOCKS
PER = CHUNKS // BLOCKS
FEATS = 8
PIECE = BLOCK // FEATS
HALF = COLS // 2
SUBS = 4
SUB = HALF // SUBS
QUARTER = SUB // 4
SMALL = 6
ALONG = (4, 3, 5, 2, 6, 1, 7)
MIDDLE = 120.0
GRADIENT = (-22.0, 384.0)
MARGIN = (-14.0, 960.0)


def coded(value, span):
    least, step = span
    level = jnp.log2(jnp.maximum(jnp.abs(value), 2.0**least)) - least
    level = jnp.floor(level * step + 0.5)
    high = jnp.floor(level * (1 / 128))
    code = jnp.exp2(high - MIDDLE) * (1.0 + (level - 128.0 * high) * (1 / 128))
    return jnp.where(value < 0, -code, code).astype(BF16)


def decoded(code, span):
    least, step = span
    code = code.astype(F32)
    size = jnp.abs(code)
    high = jnp.floor(jnp.log2(size) + 0.003)
    low = size * jnp.exp2(-high) - 1.0
    value = jnp.exp2((low + (high + MIDDLE)) * (128 / step) + least)
    return jnp.where(code < 0, -value, value)


def kernel(
    samples,
    x_ref, a_ref, w_ref, b_ref, c_ref, lin_ref, sq_ref, cube_ref, y_ref, r_ref, p_ref,
    new_ref,
    xv, av, wv, bv, pv, sv, mv, om, ev, et, ea, wm, ow, opened, zv, zc, zbuf, psum, pack, pbuf,
    rr, gv, gbuf, gc, xbuf, hbuf, back,
    y_token, z_token, x_token, load_sem, first_sem, in_send, in_recv, wt_send, wt_recv, pk_send, pk_recv,
    z_send, z_recv, p_send, p_recv, r_send, r_recv, g_send, g_recv, x_send, x_recv,
    h_send, h_recv, e_send, e_recv, k_send, k_recv,
):
    party = lax.axis_index("party")
    xi = lax.axis_index("sample_0")
    hi = lax.axis_index("sample_1")
    core = lax.axis_index("sample_2")
    feat = lax.axis_index("feat")
    select = (party == 0).astype(F32)

    def at_place(p=None, x=None, h=None, c=None, f=None):
        return (
            party if p is None else p,
            xi if x is None else x,
            hi if h is None else h,
            core if c is None else c,
            feat if f is None else f,
        )

    partner = at_place(p=1 - party)
    sibling = at_place(c=1 - core)
    other_z = at_place(p=1 - party, h=lax.rem(hi + 3 + 2 * party, 4))

    def along_y(d):
        return at_place(f=lax.rem(feat + d, FEATS))

    def along_x(d):
        return at_place(x=lax.rem(xi + d, 4))

    def along_z(d):
        return at_place(h=lax.rem(hi + d, 4))

    near_y, near_x, near_z = [along_y(1), along_y(7)], [along_x(1), along_x(3)], [partner, other_z]
    greeted = near_z + [sibling] + near_y + near_x
    barrier = pltpu.get_barrier_semaphore()
    loads = [
        pltpu.make_async_copy(src.at[0], dst, load_sem.at[i])
        for i, (src, dst) in enumerate(
            [(w_ref, wv), (b_ref, bv)]
            + [
                (ref, sv.at[i])
                for i, ref in enumerate((c_ref, lin_ref, sq_ref, cube_ref, y_ref, r_ref))
            ]
        )
    ]
    first_loads = []
    for k in range(CHUNKS):
        rows = pl.ds(k * CHUNK, CHUNK)
        for i, (src, dst) in enumerate([(x_ref, xv), (a_ref, av)]):
            first_loads.append(
                pltpu.make_async_copy(src.at[0, rows], dst.at[rows], first_sem.at[k, i])
            )
            first_loads[-1].start()
    for place in greeted:
        pl.semaphore_signal(barrier, inc=1, device_id=place, device_id_type=MESH)
    for load in loads:
        load.start()


    def masked_chunk(k):
        first_loads[2 * k].wait()
        first_loads[2 * k + 1].wait()
        rows = pl.ds(k * CHUNK, CHUNK)
        mv[rows, :] = (xv[rows, :].astype(F32) - av[rows, :].astype(F32)).astype(BF16)

    masked_chunk(0)
    pl.semaphore_wait(barrier, len(greeted))

    def pass_on(r):
        for token, places in ((y_token, near_y), (z_token, near_z), (x_token, near_x)):
            if r < token.shape[0]:
                for place in places:
                    pl.semaphore_signal(token.at[r], inc=1, device_id=place, device_id_type=MESH)

    def hear(r):
        for token in (y_token, z_token, x_token):
            if r < token.shape[0]:
                pl.semaphore_wait(token.at[r], 2)

    sent = []

    def remote(src, dst, send, recv, place):
        copy = pltpu.make_async_remote_copy(
            src_ref=src, dst_ref=dst, send_sem=send, recv_sem=recv,
            device_id=place, device_id_type=MESH,
        )
        copy.start()
        sent.append(copy)
        return copy

    def settle(copies):
        for copy in copies:
            copy.wait_send()
            sent[:] = [other for other in sent if other is not copy]

    def slab(first, size):
        return pl.ds(pl.multiple_of(first, size), size)

    inputs = []
    for k in range(CHUNKS):
        if k > 0:
            masked_chunk(k)
        rows = pl.ds(k * CHUNK, CHUNK)
        inputs.append(remote(mv.at[rows], om.at[rows], in_send.at[k], in_recv.at[k], partner))
    my_half = slab(core * HALF, HALF)
    loads[0].wait()
    loads[1].wait()
    wm[...] = (wv[...] - bv[...].astype(F32)).astype(BF16)
    weights = remote(wm.at[my_half], ow.at[my_half], wt_send.at[0], wt_recv.at[0], other_z)
    pass_on(0)

    for load in loads[2:]:
        load.wait()
    load_p = pltpu.make_async_copy(p_ref.at[0], pv, load_sem.at[8])
    load_p.start()
    for i in range(SMALL):
        for j in range(BLOCKS):
            pack[i, pl.ds(j * PIECE, PIECE), :] = sv[i, slab(j * BLOCK + feat * PIECE, PIECE), :]
    packed = remote(pack, pbuf, pk_send.at[0], pk_recv.at[0], partner)

    ea[:, ROWS:] = av[...].T
    hear(0)
    pass_on(1)
    hear(1)
    pass_on(2)
    hear(2)
    weights.wait_recv()
    passed = remote(ow.at[my_half], ow.at[my_half], wt_send.at[1], wt_recv.at[1], sibling)
    passed.wait_recv()
    opened[...] = (wm[...].astype(F32) + ow[...].astype(F32)).astype(BF16)
    zv[...] = jnp.dot(av[...], opened[...], preferred_element_type=F32)

    def margins(k):
        rows = pl.ds(k * CHUNK, CHUNK)
        inputs[k].wait_recv()
        part = (mv[rows, :].astype(F32) + om[rows, :].astype(F32)).astype(BF16)
        ev[rows, :] = part
        both = select * jnp.dot(part, opened[...], preferred_element_type=F32)
        total = zv[rows, :] + both + jnp.dot(part, bv[...], preferred_element_type=F32)
        zv[rows, :] = total
        zc[rows, :] = coded(total, MARGIN)

    def share(j):
        copies = []
        for d in ALONG:
            rows = slab(j * BLOCK + lax.rem(feat + d, FEATS) * PIECE, PIECE)
            copies.append(
                remote(zc.at[rows], zbuf.at[j, d], z_send.at[j, d], z_recv.at[j, d], along_y(d))
            )
        return copies

    def add_up(j, copies):
        for copy in copies:
            copy.wait_recv()
        total = zv[slab(j * BLOCK + feat * PIECE, PIECE), :]
        for d in range(1, FEATS):
            total = total + decoded(zbuf[j, d], MARGIN)
        psum[j, 0] = total
        return remote(psum.at[j, 0], psum.at[j, 1], p_send.at[j], p_recv.at[j], partner)

    def residuals(j, copy):
        copy.wait_recv()
        own_rows = pl.ds(j * PIECE, PIECE)
        own = [pack[i, own_rows, :].astype(F32) for i in range(SMALL)]
        far = [pbuf[i, own_rows, :].astype(F32) for i in range(SMALL)]
        own_margin, far_margin = psum[j, 0] + own[0], psum[j, 1] + far[0]
        spread = (own_margin - own[1]) + (far_margin - far[1])

        def masked(s, margin, value):
            cubed = s * (spread * spread * spread) + 3.0 * (spread * spread) * value[1]
            cubed = cubed + 3.0 * spread * value[2] + value[3]
            result = 0.5 * s + slope_one * margin - cube_coef * cubed - value[4]
            return (result - value[5]).astype(BF16).astype(F32)

        both = masked(select, own_margin, own) + masked(1.0 - select, far_margin, far)
        rows = slab(j * BLOCK + feat * PIECE, PIECE)
        rr[rows, :] = both.astype(BF16)
        return [
            remote(rr.at[rows], rr.at[rows], r_send.at[j, d], r_recv.at[j, d], along_y(d))
            for d in ALONG
        ]

    def turned(j):
        rows = pl.ds(j * BLOCK, BLOCK)
        flipped = ev[rows, :].T
        et[:, rows] = flipped
        ea[:, rows] = (flipped.astype(F32) * select).astype(BF16)

    margins(0)
    margins(1)
    shared_0 = share(0)
    turned(0)
    margins(2)
    settle([weights, passed])
    margins(3)
    shared_1 = share(1)
    summed_0 = add_up(0, shared_0)
    packed.wait_recv()
    opened_0 = residuals(0, summed_0)
    turned(1)
    gv[...] = jnp.dot(et[...], sv[SMALL - 1], preferred_element_type=F32)
    settle(inputs + [packed] + shared_0)
    summed_1 = add_up(1, shared_1)
    settle(shared_1 + [summed_0])
    opened_1 = residuals(1, summed_1)
    settle(opened_0 + [summed_1])
    for copy in opened_0 + opened_1:
        copy.wait_recv()
    rr[ROWS:, :] = rr[:ROWS, :]

    def terms(first):
        rows = slab(first, SUB)
        return gv[rows, :] + jnp.dot(ea[rows, :], rr[...], preferred_element_type=F32)

    crossing, quarters = [], []

    def cross(n):
        rows = slab((1 - core) * HALF + n * SUB, SUB)
        gv[rows, :] = terms((1 - core) * HALF + n * SUB)
        crossing.append(remote(gv.at[rows], gbuf.at[n], g_send.at[n], g_recv.at[n], sibling))

    def keep(n):
        gv[slab(core * HALF + n * SUB, SUB), :] = terms(core * HALF + n * SUB)

    def over_x(n):
        crossing[n].wait_recv()
        total = gbuf[n] + gv[slab(core * HALF + n * SUB, SUB), :]
        gbuf[n] = total
        gc[n] = coded(total, GRADIENT)
        quarters.append(
            [
                remote(
                    gc.at[n, slab(lax.rem(xi + d, 4) * QUARTER, QUARTER)],
                    xbuf.at[n, d], x_send.at[n, d], x_recv.at[n, d], along_x(d),
                )
                for d in (2, 1, 3)
            ]
        )

    for step, n in (
        (cross, 0), (cross, 1), (keep, 0), (cross, 2), (keep, 1), (over_x, 0), (cross, 3),
        (keep, 2), (over_x, 1), (keep, 3), (over_x, 2), (over_x, 3),
    ):
        step(n)

    settle(opened_1 + crossing)
    lasts = []
    for n in range(SUBS):
        for copy in quarters[n]:
            copy.wait_recv()
        total = gbuf[n, slab(xi * QUARTER, QUARTER), :]
        for d in (1, 2, 3):
            total = total + decoded(xbuf[n, d], GRADIENT)
        hbuf[n, hi] = coded(total, GRADIENT)
        lasts.append(
            [
                remote(hbuf.at[n, hi], hbuf.at[n, hi], h_send.at[n, d], h_recv.at[n, d], along_z(d))
                for d in (2, 1, 3)
            ]
        )
    settle(sum(quarters, []))
    back_x = []
    for n in range(SUBS):
        for copy in lasts[n]:
            copy.wait_recv()
        total = decoded(hbuf[n, 0], GRADIENT) + decoded(hbuf[n, 1], GRADIENT)
        total = total + (decoded(hbuf[n, 2], GRADIENT) + decoded(hbuf[n, 3], GRADIENT))
        rows = slab(core * HALF + n * SUB + xi * QUARTER, QUARTER)
        back[rows, :] = coded(total, GRADIENT)
        back_x.append(
            [
                remote(back.at[rows], back.at[rows], e_send.at[n, d], e_recv.at[n, d], along_x(d))
                for d in (2, 1, 3)
            ]
        )
    def update(first):
        rows = slab(first, SUB)
        whole = decoded(back[rows, :], GRADIENT) + pv[rows, :].astype(F32)
        new_ref[rows, :] = wv[rows, :] - learn_rate / samples * whole

    load_p.wait()
    settle(sum(lasts, []))
    back_core = []
    for n in range(SUBS):
        for copy in back_x[n]:
            copy.wait_recv()
        rows = slab(core * HALF + n * SUB, SUB)
        back_core.append(
            remote(back.at[rows], back.at[rows], k_send.at[n], k_recv.at[n], sibling)
        )
        update(core * HALF + n * SUB)
    settle(sum(back_x, []))
    for n in range(SUBS):
        back_core[n].wait_recv()
        update((1 - core) * HALF + n * SUB)
    for copy in sent:
        copy.wait_send()


def updated(samples, *arrays):
    dma = pltpu.SemaphoreType.DMA
    return pl.pallas_call(
        functools.partial(kernel, samples),
        out_shape=pltpu.VMEM((COLS, PH), F32),
        in_specs=[pl.BlockSpec(memory_space=pltpu.HBM)] * len(arrays),
        out_specs=pl.BlockSpec(memory_space=pltpu.VMEM),
        scratch_shapes=[
            pltpu.VMEM((ROWS, COLS), BF16),
            pltpu.VMEM((ROWS, COLS), BF16),
            pltpu.VMEM((COLS, PH), F32),
            pltpu.VMEM((COLS, PH), BF16),
            pltpu.VMEM((COLS, PH), BF16),
            pltpu.VMEM((SMALL, ROWS, PH), BF16),
            pltpu.VMEM((ROWS, COLS), BF16),
            pltpu.VMEM((ROWS, COLS), BF16),
            pltpu.VMEM((ROWS, COLS), BF16),
            pltpu.VMEM((COLS, ROWS), BF16),
            pltpu.VMEM((COLS, 2 * ROWS), BF16),
            pltpu.VMEM((COLS, PH), BF16),
            pltpu.VMEM((COLS, PH), BF16),
            pltpu.VMEM((COLS, PH), BF16),
            pltpu.VMEM((ROWS, PH), F32),
            pltpu.VMEM((ROWS, PH), BF16),
            pltpu.VMEM((BLOCKS, FEATS, PIECE, PH), BF16),
            pltpu.VMEM((BLOCKS, 2, PIECE, PH), F32),
            pltpu.VMEM((SMALL, BLOCKS * PIECE, PH), BF16),
            pltpu.VMEM((SMALL, BLOCKS * PIECE, PH), BF16),
            pltpu.VMEM((2 * ROWS, PH), BF16),
            pltpu.VMEM((COLS, PH), F32),
            pltpu.VMEM((SUBS, SUB, PH), F32),
            pltpu.VMEM((SUBS, SUB, PH), BF16),
            pltpu.VMEM((SUBS, 4, QUARTER, PH), BF16),
            pltpu.VMEM((SUBS, 4, QUARTER, PH), BF16),
            pltpu.VMEM((COLS, PH), BF16),
            pltpu.SemaphoreType.REGULAR((3,)),
            pltpu.SemaphoreType.REGULAR((3,)),
            pltpu.SemaphoreType.REGULAR((1,)),
            dma((9,)),
            dma((CHUNKS, 2)),
            dma((CHUNKS,)), dma((CHUNKS,)),
            dma((2,)), dma((2,)),
            dma((1,)), dma((1,)),
            dma((BLOCKS, FEATS)), dma((BLOCKS, FEATS)),
            dma((BLOCKS,)), dma((BLOCKS,)),
            dma((BLOCKS, FEATS)), dma((BLOCKS, FEATS)),
            dma((SUBS,)), dma((SUBS,)),
            dma((SUBS, 4)), dma((SUBS, 4)),
            dma((SUBS, 4)), dma((SUBS, 4)),
            dma((SUBS, 4)), dma((SUBS, 4)),
            dma((SUBS,)), dma((SUBS,)),
        ],
        compiler_params=pltpu.CompilerParams(
            collective_id=0, has_side_effects=True, vmem_limit_bytes=60 * 2**20
        ),
        cost_estimate=pl.CostEstimate(
            flops=12 * ROWS * COLS * PH, bytes_accessed=5 * 2**20, transcendentals=0
        ),
    )(*arrays)


def shards(*arrays):
    samples = arrays[0].shape[1] * lax.axis_size(SAMPLE)
    return updated(samples, *arrays)[None]


def solution(mesh):
    torus = Mesh(
        mesh.devices.reshape(mesh.shape["party"], 4, 4, 2, mesh.shape["feat"]),
        ("party", "sample_0", "sample_1", "sample_2", "feat"),
    )
    return jax.shard_map(
        shards,
        mesh=torus,
        in_specs=(
            P("party", SAMPLE, "feat"),
            P("party", SAMPLE, "feat"),
            P("party", "feat", None),
            P("party", "feat", None),
            P("party", SAMPLE, None),
            P("party", SAMPLE, None),
            P("party", SAMPLE, None),
            P("party", SAMPLE, None),
            P("party", SAMPLE, None),
            P("party", SAMPLE, None),
            P("party", "feat", None),
        ),
        out_specs=P("party", "feat", None),
        check_vma=False,
    )
```

```python
import functools

import jax
import jax.numpy as jnp
from jax import lax
from jax.experimental import pallas as pl
from jax.experimental.pallas import tpu as pltpu
from jax.sharding import Mesh
from jax.sharding import PartitionSpec as P

SAMPLE = ("sample_0", "sample_1", "sample_2")
MESH = pl.DeviceIdType.MESH
F32 = jnp.float32
BF16 = jnp.bfloat16

learn_rate = 64.0
slope_one = 0.197
cube_coef = 0.004

ROWS = 256
COLS = 1024
PH = 256
CHUNK = 64
CHUNKS = ROWS // CHUNK
BLOCKS = 2
BLOCK = ROWS // BLOCKS
PER = CHUNKS // BLOCKS
FEATS = 8
PIECE = BLOCK // FEATS
HALF = COLS // 2
SUBS = 4
SUB = HALF // SUBS
QUARTER = SUB // 4
SMALL = 6
ALONG = (4, 3, 5, 2, 6, 1, 7)
MIDDLE = 120.0
GRADIENT = (-22.0, 384.0)
MARGIN = (-14.0, 960.0)


def coded(value, span):
    least, step = span
    level = jnp.log2(jnp.maximum(jnp.abs(value), 2.0**least)) - least
    level = jnp.floor(level * step + 0.5)
    high = jnp.floor(level * (1 / 128))
    code = jnp.exp2(high - MIDDLE) * (1.0 + (level - 128.0 * high) * (1 / 128))
    return jnp.where(value < 0, -code, code).astype(BF16)


def decoded(code, span):
    least, step = span
    code = code.astype(F32)
    size = jnp.abs(code)
    high = jnp.floor(jnp.log2(size) + 0.003)
    low = size * jnp.exp2(-high) - 1.0
    value = jnp.exp2((low + (high + MIDDLE)) * (128 / step) + least)
    return jnp.where(code < 0, -value, value)


def kernel(
    samples,
    x_ref, a_ref, w_ref, b_ref, c_ref, lin_ref, sq_ref, cube_ref, y_ref, r_ref, p_ref,
    new_ref,
    xv, av, wv, bv, pv, sv, mv, om, ev, et, ea, wm, ow, opened, zv, zc, zbuf, zfar, psum, pack, pbuf,
    rr, gv, gbuf, gc, xbuf, hbuf, back,
    y_token, z_token, x_token, p_token, load_sem, first_sem, in_send, in_recv, wt_send, wt_recv, pk_send, pk_recv,
    z_send, z_recv, q_send, q_recv, p_send, p_recv, r_send, r_recv, g_send, g_recv, x_send, x_recv,
    h_send, h_recv, e_send, e_recv, k_send, k_recv,
):
    party = lax.axis_index("party")
    xi = lax.axis_index("sample_0")
    hi = lax.axis_index("sample_1")
    core = lax.axis_index("sample_2")
    feat = lax.axis_index("feat")
    select = (party == 0).astype(F32)

    def at_place(p=None, x=None, h=None, c=None, f=None):
        return (
            party if p is None else p,
            xi if x is None else x,
            hi if h is None else h,
            core if c is None else c,
            feat if f is None else f,
        )

    partner = at_place(p=1 - party)
    sibling = at_place(c=1 - core)
    other_z = at_place(p=1 - party, h=lax.rem(hi + 3 + 2 * party, 4))

    def along_y(d):
        return at_place(f=lax.rem(feat + d, FEATS))

    def across_y(d):
        return at_place(p=1 - party, f=lax.rem(feat + d, FEATS))

    def along_x(d):
        return at_place(x=lax.rem(xi + d, 4))

    def along_z(d):
        return at_place(h=lax.rem(hi + d, 4))

    near_y, near_x, near_z = [along_y(1), along_y(7)], [along_x(1), along_x(3)], [partner, other_z]
    greeted = near_z + [sibling] + near_y + near_x
    barrier = pltpu.get_barrier_semaphore()
    loads = [
        pltpu.make_async_copy(src.at[0], dst, load_sem.at[i])
        for i, (src, dst) in enumerate(
            [(w_ref, wv), (b_ref, bv)]
            + [
                (ref, sv.at[i])
                for i, ref in enumerate((c_ref, lin_ref, sq_ref, cube_ref, y_ref, r_ref))
            ]
        )
    ]
    first_loads = []
    for k in range(CHUNKS):
        rows = pl.ds(k * CHUNK, CHUNK)
        for i, (src, dst) in enumerate([(x_ref, xv), (a_ref, av)]):
            first_loads.append(
                pltpu.make_async_copy(src.at[0, rows], dst.at[rows], first_sem.at[k, i])
            )
            first_loads[-1].start()
    for place in greeted:
        pl.semaphore_signal(barrier, inc=1, device_id=place, device_id_type=MESH)
    for load in loads:
        load.start()


    def masked_chunk(k):
        first_loads[2 * k].wait()
        first_loads[2 * k + 1].wait()
        rows = pl.ds(k * CHUNK, CHUNK)
        mv[rows, :] = (xv[rows, :].astype(F32) - av[rows, :].astype(F32)).astype(BF16)

    masked_chunk(0)
    pl.semaphore_wait(barrier, len(greeted))

    def pass_on(r):
        for token, places in ((y_token, near_y), (z_token, near_z), (x_token, near_x)):
            if r < token.shape[0]:
                for place in places:
                    pl.semaphore_signal(token.at[r], inc=1, device_id=place, device_id_type=MESH)

    def hear(r):
        for token in (y_token, z_token, x_token):
            if r < token.shape[0]:
                pl.semaphore_wait(token.at[r], 2)

    sent = []

    def remote(src, dst, send, recv, place):
        copy = pltpu.make_async_remote_copy(
            src_ref=src, dst_ref=dst, send_sem=send, recv_sem=recv,
            device_id=place, device_id_type=MESH,
        )
        copy.start()
        sent.append(copy)
        return copy

    def slab(first, size):
        return pl.ds(pl.multiple_of(first, size), size)

    inputs = []
    for k in range(CHUNKS):
        if k > 0:
            masked_chunk(k)
        rows = pl.ds(k * CHUNK, CHUNK)
        inputs.append(remote(mv.at[rows], om.at[rows], in_send.at[k], in_recv.at[k], partner))
    my_half = slab(core * HALF, HALF)
    loads[0].wait()
    loads[1].wait()
    wm[...] = (wv[...] - bv[...].astype(F32)).astype(BF16)
    weights = remote(wm.at[my_half], ow.at[my_half], wt_send.at[0], wt_recv.at[0], other_z)
    pass_on(0)

    for load in loads[2:]:
        load.wait()
    load_p = pltpu.make_async_copy(p_ref.at[0], pv, load_sem.at[8])
    load_p.start()
    for i in range(SMALL):
        for j in range(BLOCKS):
            pack[i, pl.ds(j * PIECE, PIECE), :] = sv[i, slab(j * BLOCK + feat * PIECE, PIECE), :]
    packed = remote(pack, pbuf, pk_send.at[0], pk_recv.at[0], partner)

    ea[:, ROWS:] = av[...].T
    hear(0)
    pass_on(1)
    hear(1)
    pass_on(2)
    hear(2)
    pl.semaphore_signal(p_token, inc=1, device_id=partner, device_id_type=MESH)
    weights.wait_recv()
    passed = remote(ow.at[my_half], ow.at[my_half], wt_send.at[1], wt_recv.at[1], sibling)
    passed.wait_recv()
    opened[...] = (wm[...].astype(F32) + ow[...].astype(F32)).astype(BF16)
    zv[...] = jnp.dot(av[...], opened[...], preferred_element_type=F32)

    def margins(k):
        rows = pl.ds(k * CHUNK, CHUNK)
        inputs[k].wait_recv()
        part = (mv[rows, :].astype(F32) + om[rows, :].astype(F32)).astype(BF16)
        ev[rows, :] = part
        both = select * jnp.dot(part, opened[...], preferred_element_type=F32)
        total = zv[rows, :] + both + jnp.dot(part, bv[...], preferred_element_type=F32)
        zv[rows, :] = total
        zc[rows, :] = coded(total, MARGIN)

    def share(j):
        copies = []
        for d in ALONG:
            rows = slab(j * BLOCK + lax.rem(feat + d, FEATS) * PIECE, PIECE)
            copies.append(
                remote(zc.at[rows], zbuf.at[j, d], z_send.at[j, d], z_recv.at[j, d], along_y(d))
            )
        return copies

    def add_up(j, copies):
        for copy in copies:
            copy.wait_recv()
        total = zv[slab(j * BLOCK + feat * PIECE, PIECE), :]
        for d in range(1, FEATS):
            total = total + decoded(zbuf[j, d], MARGIN)
        psum[0] = total
        return remote(psum.at[0], psum.at[1], p_send.at[0], p_recv.at[0], partner)

    def share_with_both():
        own, far = {}, {}
        for d in ALONG + (0,):
            rows = slab(BLOCK + lax.rem(feat + d, FEATS) * PIECE, PIECE)
            far[d] = remote(zc.at[rows], zfar.at[d], q_send.at[d], q_recv.at[d], across_y(d))
            if d:
                own[d] = remote(zc.at[rows], zbuf.at[1, d], z_send.at[1, d], z_recv.at[1, d], along_y(d))
        return own, far

    def both_sums(own, far):
        own_sum = decoded(zc[slab(BLOCK + feat * PIECE, PIECE), :], MARGIN)
        far[0].wait_recv()
        far_sum = decoded(zfar[0], MARGIN)
        for d in range(1, FEATS):
            own[d].wait_recv()
            own_sum = own_sum + decoded(zbuf[1, d], MARGIN)
            far[d].wait_recv()
            far_sum = far_sum + decoded(zfar[d], MARGIN)
        return own_sum, far_sum

    def residuals(j, own_sum, far_sum):
        own_rows = pl.ds(j * PIECE, PIECE)
        own = [pack[i, own_rows, :].astype(F32) for i in range(SMALL)]
        far = [pbuf[i, own_rows, :].astype(F32) for i in range(SMALL)]
        own_margin, far_margin = own_sum + own[0], far_sum + far[0]
        spread = (own_margin - own[1]) + (far_margin - far[1])

        def masked(s, margin, value):
            cubed = s * (spread * spread * spread) + 3.0 * (spread * spread) * value[1]
            cubed = cubed + 3.0 * spread * value[2] + value[3]
            result = 0.5 * s + slope_one * margin - cube_coef * cubed - value[4]
            return (result - value[5]).astype(BF16).astype(F32)

        both = masked(select, own_margin, own) + masked(1.0 - select, far_margin, far)
        rows = slab(j * BLOCK + feat * PIECE, PIECE)
        rr[rows, :] = both.astype(BF16)
        return [
            remote(rr.at[rows], rr.at[rows], r_send.at[j, d], r_recv.at[j, d], along_y(d))
            for d in ALONG
        ]

    def turned(j):
        rows = pl.ds(j * BLOCK, BLOCK)
        flipped = ev[rows, :].T
        et[:, rows] = flipped
        ea[:, rows] = (flipped.astype(F32) * select).astype(BF16)

    margins(0)
    margins(1)
    shared_0 = share(0)
    turned(0)
    margins(2)
    pl.semaphore_wait(p_token, 1)
    margins(3)
    shared_1 = share_with_both()
    summed_0 = add_up(0, shared_0)
    packed.wait_recv()
    summed_0.wait_recv()
    opened_0 = residuals(0, psum[0], psum[1])
    turned(1)
    gv[...] = jnp.dot(et[...], sv[SMALL - 1], preferred_element_type=F32)
    sums_1 = both_sums(*shared_1)
    opened_1 = residuals(1, *sums_1)
    for copy in opened_0 + opened_1:
        copy.wait_recv()
    rr[ROWS:, :] = rr[:ROWS, :]

    def terms(first):
        rows = slab(first, SUB)
        return gv[rows, :] + jnp.dot(ea[rows, :], rr[...], preferred_element_type=F32)

    crossing, quarters = [], []

    def cross(n):
        rows = slab((1 - core) * HALF + n * SUB, SUB)
        gv[rows, :] = terms((1 - core) * HALF + n * SUB)
        crossing.append(remote(gv.at[rows], gbuf.at[n], g_send.at[n], g_recv.at[n], sibling))

    def keep(n):
        gv[slab(core * HALF + n * SUB, SUB), :] = terms(core * HALF + n * SUB)

    def over_x(n):
        crossing[n].wait_recv()
        total = gbuf[n] + gv[slab(core * HALF + n * SUB, SUB), :]
        gbuf[n] = total
        gc[n] = coded(total, GRADIENT)
        quarters.append(
            [
                remote(
                    gc.at[n, slab(lax.rem(xi + d, 4) * QUARTER, QUARTER)],
                    xbuf.at[n, d], x_send.at[n, d], x_recv.at[n, d], along_x(d),
                )
                for d in (2, 1, 3)
            ]
        )

    steps = [(cross, 0), (cross, 1), (keep, 0)]
    for n in range(SUBS):
        if n + 2 < SUBS:
            steps.append((cross, n + 2))
        if n + 1 < SUBS:
            steps.append((keep, n + 1))
        steps.append((over_x, n))
    for step, n in steps:
        step(n)

    lasts = []
    for n in range(SUBS):
        for copy in quarters[n]:
            copy.wait_recv()
        total = gbuf[n, slab(xi * QUARTER, QUARTER), :]
        for d in (1, 2, 3):
            total = total + decoded(xbuf[n, d], GRADIENT)
        hbuf[n, hi] = coded(total, GRADIENT)
        lasts.append(
            [
                remote(hbuf.at[n, hi], hbuf.at[n, hi], h_send.at[n, d], h_recv.at[n, d], along_z(d))
                for d in (2, 1, 3)
            ]
        )
    back_x = []
    for n in range(SUBS):
        for copy in lasts[n]:
            copy.wait_recv()
        total = decoded(hbuf[n, 0], GRADIENT) + decoded(hbuf[n, 1], GRADIENT)
        total = total + (decoded(hbuf[n, 2], GRADIENT) + decoded(hbuf[n, 3], GRADIENT))
        rows = slab(core * HALF + n * SUB + xi * QUARTER, QUARTER)
        back[rows, :] = coded(total, GRADIENT)
        back_x.append(
            [
                remote(back.at[rows], back.at[rows], e_send.at[n, d], e_recv.at[n, d], along_x(d))
                for d in (2, 1, 3)
            ]
        )
    def update(first):
        rows = slab(first, SUB)
        whole = decoded(back[rows, :], GRADIENT) + pv[rows, :].astype(F32)
        new_ref[rows, :] = wv[rows, :] - learn_rate / samples * whole

    load_p.wait()
    back_core = []
    for n in range(SUBS):
        for copy in back_x[n]:
            copy.wait_recv()
        rows = slab(core * HALF + n * SUB, SUB)
        back_core.append(
            remote(back.at[rows], back.at[rows], k_send.at[n], k_recv.at[n], sibling)
        )
        update(core * HALF + n * SUB)
    for n in range(SUBS):
        back_core[n].wait_recv()
        update((1 - core) * HALF + n * SUB)
    for copy in sent:
        copy.wait_send()


def updated(samples, *arrays):
    dma = pltpu.SemaphoreType.DMA
    return pl.pallas_call(
        functools.partial(kernel, samples),
        out_shape=pltpu.VMEM((COLS, PH), F32),
        in_specs=[pl.BlockSpec(memory_space=pltpu.HBM)] * len(arrays),
        out_specs=pl.BlockSpec(memory_space=pltpu.VMEM),
        scratch_shapes=[
            pltpu.VMEM((ROWS, COLS), BF16),
            pltpu.VMEM((ROWS, COLS), BF16),
            pltpu.VMEM((COLS, PH), F32),
            pltpu.VMEM((COLS, PH), BF16),
            pltpu.VMEM((COLS, PH), BF16),
            pltpu.VMEM((SMALL, ROWS, PH), BF16),
            pltpu.VMEM((ROWS, COLS), BF16),
            pltpu.VMEM((ROWS, COLS), BF16),
            pltpu.VMEM((ROWS, COLS), BF16),
            pltpu.VMEM((COLS, ROWS), BF16),
            pltpu.VMEM((COLS, 2 * ROWS), BF16),
            pltpu.VMEM((COLS, PH), BF16),
            pltpu.VMEM((COLS, PH), BF16),
            pltpu.VMEM((COLS, PH), BF16),
            pltpu.VMEM((ROWS, PH), F32),
            pltpu.VMEM((ROWS, PH), BF16),
            pltpu.VMEM((BLOCKS, FEATS, PIECE, PH), BF16),
            pltpu.VMEM((FEATS, PIECE, PH), BF16),
            pltpu.VMEM((2, PIECE, PH), F32),
            pltpu.VMEM((SMALL, BLOCKS * PIECE, PH), BF16),
            pltpu.VMEM((SMALL, BLOCKS * PIECE, PH), BF16),
            pltpu.VMEM((2 * ROWS, PH), BF16),
            pltpu.VMEM((COLS, PH), F32),
            pltpu.VMEM((SUBS, SUB, PH), F32),
            pltpu.VMEM((SUBS, SUB, PH), BF16),
            pltpu.VMEM((SUBS, 4, QUARTER, PH), BF16),
            pltpu.VMEM((SUBS, 4, QUARTER, PH), BF16),
            pltpu.VMEM((COLS, PH), BF16),
            pltpu.SemaphoreType.REGULAR((3,)),
            pltpu.SemaphoreType.REGULAR((3,)),
            pltpu.SemaphoreType.REGULAR((1,)),
            pltpu.SemaphoreType.REGULAR,
            dma((9,)),
            dma((CHUNKS, 2)),
            dma((CHUNKS,)), dma((CHUNKS,)),
            dma((2,)), dma((2,)),
            dma((1,)), dma((1,)),
            dma((BLOCKS, FEATS)), dma((BLOCKS, FEATS)),
            dma((FEATS,)), dma((FEATS,)),
            dma((1,)), dma((1,)),
            dma((BLOCKS, FEATS)), dma((BLOCKS, FEATS)),
            dma((SUBS,)), dma((SUBS,)),
            dma((SUBS, 4)), dma((SUBS, 4)),
            dma((SUBS, 4)), dma((SUBS, 4)),
            dma((SUBS, 4)), dma((SUBS, 4)),
            dma((SUBS,)), dma((SUBS,)),
        ],
        compiler_params=pltpu.CompilerParams(
            collective_id=0, has_side_effects=True, vmem_limit_bytes=60 * 2**20
        ),
        cost_estimate=pl.CostEstimate(
            flops=12 * ROWS * COLS * PH, bytes_accessed=5 * 2**20, transcendentals=0
        ),
    )(*arrays)


def shards(*arrays):
    samples = arrays[0].shape[1] * lax.axis_size(SAMPLE)
    return updated(samples, *arrays)[None]


def solution(mesh):
    torus = Mesh(
        mesh.devices.reshape(mesh.shape["party"], 4, 4, 2, mesh.shape["feat"]),
        ("party", "sample_0", "sample_1", "sample_2", "feat"),
    )
    return jax.shard_map(
        shards,
        mesh=torus,
        in_specs=(
            P("party", SAMPLE, "feat"),
            P("party", SAMPLE, "feat"),
            P("party", "feat", None),
            P("party", "feat", None),
            P("party", SAMPLE, None),
            P("party", SAMPLE, None),
            P("party", SAMPLE, None),
            P("party", SAMPLE, None),
            P("party", SAMPLE, None),
            P("party", SAMPLE, None),
            P("party", "feat", None),
        ),
        out_specs=P("party", "feat", None),
        check_vma=False,
    )
```

```python
import functools

import jax
import jax.numpy as jnp
from jax import lax
from jax.experimental import pallas as pl
from jax.experimental.pallas import tpu as pltpu
from jax.sharding import Mesh
from jax.sharding import PartitionSpec as P

SAMPLE = ("sample_0", "sample_1", "sample_2")
MESH = pl.DeviceIdType.MESH
F32 = jnp.float32
BF16 = jnp.bfloat16

learn_rate = 64.0
slope_one = 0.197
cube_coef = 0.004

ROWS = 256
COLS = 1024
PH = 256
CHUNK = 64
CHUNKS = ROWS // CHUNK
BLOCKS = 2
BLOCK = ROWS // BLOCKS
PER = CHUNKS // BLOCKS
FEATS = 8
PIECE = BLOCK // FEATS
HALF = COLS // 2
SUBS = 4
SUB = HALF // SUBS
QUARTER = SUB // 4
SMALL = 6
ALONG = (4, 3, 5, 2, 6, 1, 7)
MIDDLE = 120.0
GRADIENT = (-22.0, 384.0)
MARGIN = (-14.0, 960.0)


def coded(value, span):
    least, step = span
    level = jnp.log2(jnp.maximum(jnp.abs(value), 2.0**least)) - least
    level = jnp.floor(level * step + 0.5)
    high = jnp.floor(level * (1 / 128))
    code = jnp.exp2(high - MIDDLE) * (1.0 + (level - 128.0 * high) * (1 / 128))
    return jnp.where(value < 0, -code, code).astype(BF16)


def decoded(code, span):
    least, step = span
    code = code.astype(F32)
    size = jnp.abs(code)
    high = jnp.floor(jnp.log2(size) + 0.003)
    low = size * jnp.exp2(-high) - 1.0
    value = jnp.exp2((low + (high + MIDDLE)) * (128 / step) + least)
    return jnp.where(code < 0, -value, value)


def kernel(
    samples,
    x_ref, a_ref, w_ref, b_ref, c_ref, lin_ref, sq_ref, cube_ref, y_ref, r_ref, p_ref,
    new_ref,
    xv, av, wv, bv, pv, sv, mv, om, ev, et, ea, wm, ow, opened, zv, zc, zbuf, zfar, psum, pack, pbuf,
    rr, gv, gbuf, gc, xbuf, hbuf, back,
    y_token, z_token, x_token, p_token, load_sem, first_sem, in_send, in_recv, wt_send, wt_recv, pk_send, pk_recv,
    z_send, z_recv, q_send, q_recv, p_send, p_recv, r_send, r_recv, g_send, g_recv, x_send, x_recv,
    h_send, h_recv, e_send, e_recv, k_send, k_recv,
):
    party = lax.axis_index("party")
    xi = lax.axis_index("sample_0")
    hi = lax.axis_index("sample_1")
    core = lax.axis_index("sample_2")
    feat = lax.axis_index("feat")
    select = (party == 0).astype(F32)

    def at_place(p=None, x=None, h=None, c=None, f=None):
        return (
            party if p is None else p,
            xi if x is None else x,
            hi if h is None else h,
            core if c is None else c,
            feat if f is None else f,
        )

    partner = at_place(p=1 - party)
    sibling = at_place(c=1 - core)
    other_z = at_place(p=1 - party, h=lax.rem(hi + 3 + 2 * party, 4))

    def along_y(d):
        return at_place(f=lax.rem(feat + d, FEATS))

    def across_y(d):
        return at_place(p=1 - party, f=lax.rem(feat + d, FEATS))

    def along_x(d):
        return at_place(x=lax.rem(xi + d, 4))

    def along_z(d):
        return at_place(h=lax.rem(hi + d, 4))

    near_y, near_x, near_z = [along_y(1), along_y(7)], [along_x(1), along_x(3)], [partner, other_z]
    greeted = near_z + [sibling] + near_y + near_x
    barrier = pltpu.get_barrier_semaphore()
    loads = [
        pltpu.make_async_copy(src.at[0], dst, load_sem.at[i])
        for i, (src, dst) in enumerate(
            [(w_ref, wv), (b_ref, bv)]
            + [
                (ref, sv.at[i])
                for i, ref in enumerate((c_ref, lin_ref, sq_ref, cube_ref, y_ref, r_ref))
            ]
        )
    ]
    first_loads = []
    for k in range(CHUNKS):
        rows = pl.ds(k * CHUNK, CHUNK)
        for i, (src, dst) in enumerate([(x_ref, xv), (a_ref, av)]):
            first_loads.append(
                pltpu.make_async_copy(src.at[0, rows], dst.at[rows], first_sem.at[k, i])
            )
            first_loads[-1].start()
    for place in greeted:
        pl.semaphore_signal(barrier, inc=1, device_id=place, device_id_type=MESH)
    for load in loads:
        load.start()


    def masked_chunk(k):
        first_loads[2 * k].wait()
        first_loads[2 * k + 1].wait()
        rows = pl.ds(k * CHUNK, CHUNK)
        mv[rows, :] = (xv[rows, :].astype(F32) - av[rows, :].astype(F32)).astype(BF16)

    masked_chunk(0)
    pl.semaphore_wait(barrier, len(greeted))

    def pass_on(r):
        for token, places in ((y_token, near_y), (z_token, near_z), (x_token, near_x)):
            if r < token.shape[0]:
                for place in places:
                    pl.semaphore_signal(token.at[r], inc=1, device_id=place, device_id_type=MESH)

    def hear(r):
        for token in (y_token, z_token, x_token):
            if r < token.shape[0]:
                pl.semaphore_wait(token.at[r], 2)

    sent = []

    def remote(src, dst, send, recv, place):
        copy = pltpu.make_async_remote_copy(
            src_ref=src, dst_ref=dst, send_sem=send, recv_sem=recv,
            device_id=place, device_id_type=MESH,
        )
        copy.start()
        sent.append(copy)
        return copy

    def slab(first, size):
        return pl.ds(pl.multiple_of(first, size), size)

    inputs = []
    for k in range(CHUNKS):
        if k > 0:
            masked_chunk(k)
        rows = pl.ds(k * CHUNK, CHUNK)
        inputs.append(remote(mv.at[rows], om.at[rows], in_send.at[k], in_recv.at[k], partner))
    my_half = slab(core * HALF, HALF)
    loads[0].wait()
    loads[1].wait()
    wm[...] = (wv[...] - bv[...].astype(F32)).astype(BF16)
    weights = remote(wm.at[my_half], ow.at[my_half], wt_send.at[0], wt_recv.at[0], other_z)
    pass_on(0)

    for load in loads[2:]:
        load.wait()
    load_p = pltpu.make_async_copy(p_ref.at[0], pv, load_sem.at[8])
    load_p.start()
    for i in range(SMALL):
        for j in range(BLOCKS):
            pack[i, pl.ds(j * PIECE, PIECE), :] = sv[i, slab(j * BLOCK + feat * PIECE, PIECE), :]
    packed = remote(pack, pbuf, pk_send.at[0], pk_recv.at[0], partner)

    ea[:, ROWS:] = av[...].T
    hear(0)
    pass_on(1)
    hear(1)
    pass_on(2)
    hear(2)
    pl.semaphore_signal(p_token, inc=1, device_id=partner, device_id_type=MESH)
    weights.wait_recv()
    passed = remote(ow.at[my_half], ow.at[my_half], wt_send.at[1], wt_recv.at[1], sibling)
    passed.wait_recv()
    opened[...] = (wm[...].astype(F32) + ow[...].astype(F32)).astype(BF16)
    zv[...] = jnp.dot(av[...], opened[...], preferred_element_type=F32)

    def margins(k):
        rows = pl.ds(k * CHUNK, CHUNK)
        inputs[k].wait_recv()
        part = (mv[rows, :].astype(F32) + om[rows, :].astype(F32)).astype(BF16)
        ev[rows, :] = part
        both = select * jnp.dot(part, opened[...], preferred_element_type=F32)
        total = zv[rows, :] + both + jnp.dot(part, bv[...], preferred_element_type=F32)
        zv[rows, :] = total
        zc[rows, :] = coded(total, MARGIN)

    def share(j):
        copies = []
        for d in ALONG:
            rows = slab(j * BLOCK + lax.rem(feat + d, FEATS) * PIECE, PIECE)
            copies.append(
                remote(zc.at[rows], zbuf.at[j, d], z_send.at[j, d], z_recv.at[j, d], along_y(d))
            )
        return copies

    def add_up(j, copies):
        for copy in copies:
            copy.wait_recv()
        total = zv[slab(j * BLOCK + feat * PIECE, PIECE), :]
        for d in range(1, FEATS):
            total = total + decoded(zbuf[j, d], MARGIN)
        psum[0] = total
        return remote(psum.at[0], psum.at[1], p_send.at[0], p_recv.at[0], partner)

    def share_with_both():
        own, far = {}, {}
        for d in ALONG + (0,):
            rows = slab(BLOCK + lax.rem(feat + d, FEATS) * PIECE, PIECE)
            far[d] = remote(zc.at[rows], zfar.at[d], q_send.at[d], q_recv.at[d], across_y(d))
            if d:
                own[d] = remote(zc.at[rows], zbuf.at[1, d], z_send.at[1, d], z_recv.at[1, d], along_y(d))
        return own, far

    def both_sums(own, far):
        own_sum = decoded(zc[slab(BLOCK + feat * PIECE, PIECE), :], MARGIN)
        far[0].wait_recv()
        far_sum = decoded(zfar[0], MARGIN)
        for d in range(1, FEATS):
            own[d].wait_recv()
            own_sum = own_sum + decoded(zbuf[1, d], MARGIN)
            far[d].wait_recv()
            far_sum = far_sum + decoded(zfar[d], MARGIN)
        return own_sum, far_sum

    def residuals(j, own_sum, far_sum):
        own_rows = pl.ds(j * PIECE, PIECE)
        own = [pack[i, own_rows, :].astype(F32) for i in range(SMALL)]
        far = [pbuf[i, own_rows, :].astype(F32) for i in range(SMALL)]
        own_margin, far_margin = own_sum + own[0], far_sum + far[0]
        spread = (own_margin - own[1]) + (far_margin - far[1])

        def masked(s, margin, value):
            cubed = s * (spread * spread * spread) + 3.0 * (spread * spread) * value[1]
            cubed = cubed + 3.0 * spread * value[2] + value[3]
            result = 0.5 * s + slope_one * margin - cube_coef * cubed - value[4]
            return (result - value[5]).astype(BF16).astype(F32)

        both = masked(select, own_margin, own) + masked(1.0 - select, far_margin, far)
        rows = slab(j * BLOCK + feat * PIECE, PIECE)
        rr[rows, :] = both.astype(BF16)
        return [
            remote(rr.at[rows], rr.at[rows], r_send.at[j, d], r_recv.at[j, d], along_y(d))
            for d in ALONG
        ]

    def turned(j):
        rows = pl.ds(j * BLOCK, BLOCK)
        flipped = ev[rows, :].T
        et[:, rows] = flipped
        ea[:, rows] = (flipped.astype(F32) * select).astype(BF16)

    margins(0)
    margins(1)
    shared_0 = share(0)
    turned(0)
    margins(2)
    pl.semaphore_wait(p_token, 1)
    margins(3)
    shared_1 = share_with_both()
    summed_0 = add_up(0, shared_0)
    packed.wait_recv()
    summed_0.wait_recv()
    opened_0 = residuals(0, psum[0], psum[1])
    turned(1)
    gv[...] = jnp.dot(et[...], sv[SMALL - 1], preferred_element_type=F32)
    sums_1 = both_sums(*shared_1)
    opened_1 = residuals(1, *sums_1)
    for copy in opened_0 + opened_1:
        copy.wait_recv()
    rr[ROWS:, :] = rr[:ROWS, :]

    def terms(first, size):
        rows = pl.ds(pl.multiple_of(first, SUB), size)
        gv[rows, :] += jnp.dot(ea[rows, :], rr[...], preferred_element_type=F32)

    crossing, quarters = [], []
    their, own = (1 - core) * HALF, core * HALF

    def cross(n):
        rows = slab(their + n * SUB, SUB)
        crossing.append(remote(gv.at[rows], gbuf.at[n], g_send.at[n], g_recv.at[n], sibling))

    terms(their, SUB)
    cross(0)
    terms(their + SUB, HALF - SUB)
    for n in range(1, SUBS):
        cross(n)
    terms(own, SUB)
    terms(own + SUB, HALF - SUB)

    def over_x(n):
        crossing[n].wait_recv()
        total = gbuf[n] + gv[slab(core * HALF + n * SUB, SUB), :]
        gbuf[n] = total
        gc[n] = coded(total, GRADIENT)
        quarters.append(
            [
                remote(
                    gc.at[n, slab(lax.rem(xi + d, 4) * QUARTER, QUARTER)],
                    xbuf.at[n, d], x_send.at[n, d], x_recv.at[n, d], along_x(d),
                )
                for d in (2, 1, 3)
            ]
        )

    for n in range(SUBS):
        over_x(n)

    lasts = []
    for n in range(SUBS):
        for copy in quarters[n]:
            copy.wait_recv()
        total = gbuf[n, slab(xi * QUARTER, QUARTER), :]
        for d in (1, 2, 3):
            total = total + decoded(xbuf[n, d], GRADIENT)
        hbuf[n, hi] = coded(total, GRADIENT)
        lasts.append(
            [
                remote(hbuf.at[n, hi], hbuf.at[n, hi], h_send.at[n, d], h_recv.at[n, d], along_z(d))
                for d in (2, 1, 3)
            ]
        )
    back_x = []
    for n in range(SUBS):
        for copy in lasts[n]:
            copy.wait_recv()
        total = decoded(hbuf[n, 0], GRADIENT) + decoded(hbuf[n, 1], GRADIENT)
        total = total + (decoded(hbuf[n, 2], GRADIENT) + decoded(hbuf[n, 3], GRADIENT))
        rows = slab(core * HALF + n * SUB + xi * QUARTER, QUARTER)
        back[rows, :] = coded(total, GRADIENT)
        back_x.append(
            [
                remote(back.at[rows], back.at[rows], e_send.at[n, d], e_recv.at[n, d], along_x(d))
                for d in (2, 1, 3)
            ]
        )
    def update(first):
        rows = slab(first, SUB)
        whole = decoded(back[rows, :], GRADIENT) + pv[rows, :].astype(F32)
        new_ref[rows, :] = wv[rows, :] - learn_rate / samples * whole

    load_p.wait()
    back_core = []
    for n in range(SUBS):
        for copy in back_x[n]:
            copy.wait_recv()
        rows = slab(core * HALF + n * SUB, SUB)
        back_core.append(
            remote(back.at[rows], back.at[rows], k_send.at[n], k_recv.at[n], sibling)
        )
        update(core * HALF + n * SUB)
        if n > 0:
            back_core[n - 1].wait_recv()
            update((1 - core) * HALF + (n - 1) * SUB)
    back_core[SUBS - 1].wait_recv()
    update((1 - core) * HALF + (SUBS - 1) * SUB)
    for copy in sent:
        copy.wait_send()


def updated(samples, *arrays):
    dma = pltpu.SemaphoreType.DMA
    return pl.pallas_call(
        functools.partial(kernel, samples),
        out_shape=pltpu.VMEM((COLS, PH), F32),
        in_specs=[pl.BlockSpec(memory_space=pltpu.HBM)] * len(arrays),
        out_specs=pl.BlockSpec(memory_space=pltpu.VMEM),
        scratch_shapes=[
            pltpu.VMEM((ROWS, COLS), BF16),
            pltpu.VMEM((ROWS, COLS), BF16),
            pltpu.VMEM((COLS, PH), F32),
            pltpu.VMEM((COLS, PH), BF16),
            pltpu.VMEM((COLS, PH), BF16),
            pltpu.VMEM((SMALL, ROWS, PH), BF16),
            pltpu.VMEM((ROWS, COLS), BF16),
            pltpu.VMEM((ROWS, COLS), BF16),
            pltpu.VMEM((ROWS, COLS), BF16),
            pltpu.VMEM((COLS, ROWS), BF16),
            pltpu.VMEM((COLS, 2 * ROWS), BF16),
            pltpu.VMEM((COLS, PH), BF16),
            pltpu.VMEM((COLS, PH), BF16),
            pltpu.VMEM((COLS, PH), BF16),
            pltpu.VMEM((ROWS, PH), F32),
            pltpu.VMEM((ROWS, PH), BF16),
            pltpu.VMEM((BLOCKS, FEATS, PIECE, PH), BF16),
            pltpu.VMEM((FEATS, PIECE, PH), BF16),
            pltpu.VMEM((2, PIECE, PH), F32),
            pltpu.VMEM((SMALL, BLOCKS * PIECE, PH), BF16),
            pltpu.VMEM((SMALL, BLOCKS * PIECE, PH), BF16),
            pltpu.VMEM((2 * ROWS, PH), BF16),
            pltpu.VMEM((COLS, PH), F32),
            pltpu.VMEM((SUBS, SUB, PH), F32),
            pltpu.VMEM((SUBS, SUB, PH), BF16),
            pltpu.VMEM((SUBS, 4, QUARTER, PH), BF16),
            pltpu.VMEM((SUBS, 4, QUARTER, PH), BF16),
            pltpu.VMEM((COLS, PH), BF16),
            pltpu.SemaphoreType.REGULAR((3,)),
            pltpu.SemaphoreType.REGULAR((3,)),
            pltpu.SemaphoreType.REGULAR((1,)),
            pltpu.SemaphoreType.REGULAR,
            dma((9,)),
            dma((CHUNKS, 2)),
            dma((CHUNKS,)), dma((CHUNKS,)),
            dma((2,)), dma((2,)),
            dma((1,)), dma((1,)),
            dma((BLOCKS, FEATS)), dma((BLOCKS, FEATS)),
            dma((FEATS,)), dma((FEATS,)),
            dma((1,)), dma((1,)),
            dma((BLOCKS, FEATS)), dma((BLOCKS, FEATS)),
            dma((SUBS,)), dma((SUBS,)),
            dma((SUBS, 4)), dma((SUBS, 4)),
            dma((SUBS, 4)), dma((SUBS, 4)),
            dma((SUBS, 4)), dma((SUBS, 4)),
            dma((SUBS,)), dma((SUBS,)),
        ],
        compiler_params=pltpu.CompilerParams(
            collective_id=0, has_side_effects=True, vmem_limit_bytes=60 * 2**20
        ),
        cost_estimate=pl.CostEstimate(
            flops=12 * ROWS * COLS * PH, bytes_accessed=5 * 2**20, transcendentals=0
        ),
    )(*arrays)


def shards(*arrays):
    samples = arrays[0].shape[1] * lax.axis_size(SAMPLE)
    return updated(samples, *arrays)[None]


def solution(mesh):
    torus = Mesh(
        mesh.devices.reshape(mesh.shape["party"], 4, 4, 2, mesh.shape["feat"]),
        ("party", "sample_0", "sample_1", "sample_2", "feat"),
    )
    return jax.shard_map(
        shards,
        mesh=torus,
        in_specs=(
            P("party", SAMPLE, "feat"),
            P("party", SAMPLE, "feat"),
            P("party", "feat", None),
            P("party", "feat", None),
            P("party", SAMPLE, None),
            P("party", SAMPLE, None),
            P("party", SAMPLE, None),
            P("party", SAMPLE, None),
            P("party", SAMPLE, None),
            P("party", SAMPLE, None),
            P("party", "feat", None),
        ),
        out_specs=P("party", "feat", None),
        check_vma=False,
    )
```

```python
import functools

import jax
import jax.numpy as jnp
from jax import lax
from jax.experimental import pallas as pl
from jax.experimental.pallas import tpu as pltpu
from jax.sharding import Mesh
from jax.sharding import PartitionSpec as P

SAMPLE = ("sample_0", "sample_1", "sample_2")
MESH = pl.DeviceIdType.MESH
F32 = jnp.float32
BF16 = jnp.bfloat16

learn_rate = 64.0
slope_one = 0.197
cube_coef = 0.004

ROWS = 256
COLS = 1024
PH = 256
CHUNK = 64
CHUNKS = ROWS // CHUNK
BLOCKS = 2
BLOCK = ROWS // BLOCKS
PER = CHUNKS // BLOCKS
FEATS = 8
PIECE = BLOCK // FEATS
HALF = COLS // 2
SUBS = 4
SUB = HALF // SUBS
QUARTER = SUB // 4
SMALL = 6
ALONG = (4, 3, 5, 2, 6, 1, 7)
MIDDLE = 120.0
GRADIENT = (-22.0, 384.0)
MARGIN = (-14.0, 960.0)


def coded(value, span):
    least, step = span
    level = jnp.log2(jnp.maximum(jnp.abs(value), 2.0**least)) - least
    level = jnp.floor(level * step + 0.5)
    high = jnp.floor(level * (1 / 128))
    code = jnp.exp2(high - MIDDLE) * (1.0 + (level - 128.0 * high) * (1 / 128))
    return jnp.where(value < 0, -code, code).astype(BF16)


def decoded(code, span):
    least, step = span
    code = code.astype(F32)
    size = jnp.abs(code)
    high = jnp.floor(jnp.log2(size) + 0.003)
    low = size * jnp.exp2(-high) - 1.0
    value = jnp.exp2((low + (high + MIDDLE)) * (128 / step) + least)
    return jnp.where(code < 0, -value, value)


def kernel(
    samples,
    x_ref, a_ref, w_ref, b_ref, c_ref, lin_ref, sq_ref, cube_ref, y_ref, r_ref, p_ref,
    new_ref,
    xv, av, wv, bv, pv, sv, mv, om, ev, et, ea, wm, ow, opened, zv, zc, zbuf, zfar, psum, pack, pbuf,
    rr, gv, gbuf, gc, xbuf, hbuf, back,
    y_token, z_token, x_token, p_token, load_sem, first_sem, in_send, in_recv, wt_send, wt_recv, pk_send, pk_recv,
    z_send, z_recv, q_send, q_recv, p_send, p_recv, r_send, r_recv, g_send, g_recv, x_send, x_recv,
    h_send, h_recv, e_send, e_recv, k_send, k_recv,
):
    party = lax.axis_index("party")
    xi = lax.axis_index("sample_0")
    hi = lax.axis_index("sample_1")
    core = lax.axis_index("sample_2")
    feat = lax.axis_index("feat")
    select = (party == 0).astype(F32)

    def at_place(p=None, x=None, h=None, c=None, f=None):
        return (
            party if p is None else p,
            xi if x is None else x,
            hi if h is None else h,
            core if c is None else c,
            feat if f is None else f,
        )

    partner = at_place(p=1 - party)
    sibling = at_place(c=1 - core)
    other_z = at_place(p=1 - party, h=lax.rem(hi + 3 + 2 * party, 4))

    def along_y(d):
        return at_place(f=lax.rem(feat + d, FEATS))

    def across_y(d):
        return at_place(p=1 - party, f=lax.rem(feat + d, FEATS))

    def along_x(d):
        return at_place(x=lax.rem(xi + d, 4))

    def along_z(d):
        return at_place(h=lax.rem(hi + d, 4))

    near_y, near_x, near_z = [along_y(1), along_y(7)], [along_x(1), along_x(3)], [partner, other_z]
    greeted = near_z + [sibling] + near_y + near_x
    barrier = pltpu.get_barrier_semaphore()
    loads = [
        pltpu.make_async_copy(src.at[0], dst, load_sem.at[i])
        for i, (src, dst) in enumerate(
            [(w_ref, wv), (b_ref, bv)]
            + [
                (ref, sv.at[i])
                for i, ref in enumerate((c_ref, lin_ref, sq_ref, cube_ref, y_ref, r_ref))
            ]
        )
    ]
    first_loads = []
    for k in range(CHUNKS):
        rows = pl.ds(k * CHUNK, CHUNK)
        for i, (src, dst) in enumerate([(x_ref, xv), (a_ref, av)]):
            first_loads.append(
                pltpu.make_async_copy(src.at[0, rows], dst.at[rows], first_sem.at[k, i])
            )
            first_loads[-1].start()
    for place in greeted:
        pl.semaphore_signal(barrier, inc=1, device_id=place, device_id_type=MESH)
    for load in loads:
        load.start()


    def masked_chunk(k):
        first_loads[2 * k].wait()
        first_loads[2 * k + 1].wait()
        rows = pl.ds(k * CHUNK, CHUNK)
        mv[rows, :] = (xv[rows, :].astype(F32) - av[rows, :].astype(F32)).astype(BF16)

    masked_chunk(0)
    pl.semaphore_wait(barrier, len(greeted))

    def pass_on(r):
        for token, places in ((y_token, near_y), (z_token, near_z), (x_token, near_x)):
            if r < token.shape[0]:
                for place in places:
                    pl.semaphore_signal(token.at[r], inc=1, device_id=place, device_id_type=MESH)

    def hear(r):
        for token in (y_token, z_token, x_token):
            if r < token.shape[0]:
                pl.semaphore_wait(token.at[r], 2)

    sent = []

    def remote(src, dst, send, recv, place):
        copy = pltpu.make_async_remote_copy(
            src_ref=src, dst_ref=dst, send_sem=send, recv_sem=recv,
            device_id=place, device_id_type=MESH,
        )
        copy.start()
        sent.append(copy)
        return copy

    def slab(first, size):
        return pl.ds(pl.multiple_of(first, size), size)

    inputs = []
    for k in range(CHUNKS):
        if k > 0:
            masked_chunk(k)
        rows = pl.ds(k * CHUNK, CHUNK)
        inputs.append(remote(mv.at[rows], om.at[rows], in_send.at[k], in_recv.at[k], partner))
    my_half = slab(core * HALF, HALF)
    loads[0].wait()
    loads[1].wait()
    wm[...] = (wv[...] - bv[...].astype(F32)).astype(BF16)
    weights = remote(wm.at[my_half], ow.at[my_half], wt_send.at[0], wt_recv.at[0], other_z)
    pass_on(0)

    for load in loads[2:]:
        load.wait()
    load_p = pltpu.make_async_copy(p_ref.at[0], pv, load_sem.at[8])
    load_p.start()
    for i in range(SMALL):
        for j in range(BLOCKS):
            pack[i, pl.ds(j * PIECE, PIECE), :] = sv[i, slab(j * BLOCK + feat * PIECE, PIECE), :]
    packed = remote(pack, pbuf, pk_send.at[0], pk_recv.at[0], partner)

    ea[:, ROWS:] = av[...].T
    hear(0)
    pass_on(1)
    hear(1)
    pass_on(2)
    hear(2)
    pl.semaphore_signal(p_token, inc=1, device_id=partner, device_id_type=MESH)
    weights.wait_recv()
    passed = remote(ow.at[my_half], ow.at[my_half], wt_send.at[1], wt_recv.at[1], sibling)
    passed.wait_recv()
    opened[...] = (wm[...].astype(F32) + ow[...].astype(F32)).astype(BF16)
    zv[...] = jnp.dot(av[...], opened[...], preferred_element_type=F32)

    def margins(k):
        rows = pl.ds(k * CHUNK, CHUNK)
        inputs[k].wait_recv()
        part = (mv[rows, :].astype(F32) + om[rows, :].astype(F32)).astype(BF16)
        ev[rows, :] = part
        both = select * jnp.dot(part, opened[...], preferred_element_type=F32)
        total = zv[rows, :] + both + jnp.dot(part, bv[...], preferred_element_type=F32)
        zv[rows, :] = total
        zc[rows, :] = coded(total, MARGIN)

    def share(j):
        copies = []
        for d in ALONG:
            rows = slab(j * BLOCK + lax.rem(feat + d, FEATS) * PIECE, PIECE)
            copies.append(
                remote(zc.at[rows], zbuf.at[j, d], z_send.at[j, d], z_recv.at[j, d], along_y(d))
            )
        return copies

    def add_up(j, copies):
        for copy in copies:
            copy.wait_recv()
        total = zv[slab(j * BLOCK + feat * PIECE, PIECE), :]
        for d in range(1, FEATS):
            total = total + decoded(zbuf[j, d], MARGIN)
        psum[0] = total
        return remote(psum.at[0], psum.at[1], p_send.at[0], p_recv.at[0], partner)

    def share_with_both():
        own, far = {}, {}
        for d in ALONG + (0,):
            rows = slab(BLOCK + lax.rem(feat + d, FEATS) * PIECE, PIECE)
            far[d] = remote(zc.at[rows], zfar.at[d], q_send.at[d], q_recv.at[d], across_y(d))
            if d:
                own[d] = remote(zc.at[rows], zbuf.at[1, d], z_send.at[1, d], z_recv.at[1, d], along_y(d))
        return own, far

    def both_sums(own, far):
        own_sum = decoded(zc[slab(BLOCK + feat * PIECE, PIECE), :], MARGIN)
        far[0].wait_recv()
        far_sum = decoded(zfar[0], MARGIN)
        for d in range(1, FEATS):
            own[d].wait_recv()
            own_sum = own_sum + decoded(zbuf[1, d], MARGIN)
            far[d].wait_recv()
            far_sum = far_sum + decoded(zfar[d], MARGIN)
        return own_sum, far_sum

    def residuals(j, own_sum, far_sum):
        own_rows = pl.ds(j * PIECE, PIECE)
        own = [pack[i, own_rows, :].astype(F32) for i in range(SMALL)]
        far = [pbuf[i, own_rows, :].astype(F32) for i in range(SMALL)]
        own_margin, far_margin = own_sum + own[0], far_sum + far[0]
        spread = (own_margin - own[1]) + (far_margin - far[1])

        def masked(s, margin, value):
            cubed = s * (spread * spread * spread) + 3.0 * (spread * spread) * value[1]
            cubed = cubed + 3.0 * spread * value[2] + value[3]
            result = 0.5 * s + slope_one * margin - cube_coef * cubed - value[4]
            return (result - value[5]).astype(BF16).astype(F32)

        both = masked(select, own_margin, own) + masked(1.0 - select, far_margin, far)
        rows = slab(j * BLOCK + feat * PIECE, PIECE)
        rr[rows, :] = both.astype(BF16)
        return [
            remote(rr.at[rows], rr.at[rows], r_send.at[j, d], r_recv.at[j, d], along_y(d))
            for d in ALONG
        ]

    def turned(j):
        rows = pl.ds(j * BLOCK, BLOCK)
        flipped = ev[rows, :].T
        et[:, rows] = flipped
        ea[:, rows] = (flipped.astype(F32) * select).astype(BF16)

    margins(0)
    margins(1)
    shared_0 = share(0)
    turned(0)
    margins(2)
    pl.semaphore_wait(p_token, 1)
    margins(3)
    shared_1 = share_with_both()
    summed_0 = add_up(0, shared_0)
    packed.wait_recv()
    summed_0.wait_recv()
    opened_0 = residuals(0, psum[0], psum[1])
    turned(1)
    gv[...] = jnp.dot(et[...], sv[SMALL - 1], preferred_element_type=F32)
    sums_1 = both_sums(*shared_1)
    opened_1 = residuals(1, *sums_1)
    for copy in opened_0 + opened_1:
        copy.wait_recv()
    rr[ROWS:, :] = rr[:ROWS, :]

    def terms(first, size):
        rows = pl.ds(pl.multiple_of(first, SUB), size)
        gv[rows, :] += jnp.dot(ea[rows, :], rr[...], preferred_element_type=F32)

    crossing, quarters = [], []
    their, own = (1 - core) * HALF, core * HALF

    def cross(n):
        rows = slab(their + n * SUB, SUB)
        crossing.append(remote(gv.at[rows], gbuf.at[n], g_send.at[n], g_recv.at[n], sibling))

    terms(their, SUB)
    cross(0)
    terms(their + SUB, HALF - SUB)
    for n in range(1, SUBS):
        cross(n)
    terms(own, SUB)
    terms(own + SUB, HALF - SUB)

    def over_x(n):
        crossing[n].wait_recv()
        total = gbuf[n] + gv[slab(core * HALF + n * SUB, SUB), :]
        gbuf[n] = total
        gc[n] = coded(total, GRADIENT)
        quarters.append(
            [
                remote(
                    gc.at[n, slab(lax.rem(xi + d, 4) * QUARTER, QUARTER)],
                    xbuf.at[n, d], x_send.at[n, d], x_recv.at[n, d], along_x(d),
                )
                for d in (2, 1, 3)
            ]
        )

    for n in range(SUBS):
        over_x(n)

    lasts, passing, back_x = [], [], []
    below, above = lax.rem(hi + 3, 4), lax.rem(hi + 1, 4)

    def over_z(n):
        for copy in quarters[n]:
            copy.wait_recv()
        total = gbuf[n, slab(xi * QUARTER, QUARTER), :]
        for d in (1, 2, 3):
            total = total + decoded(xbuf[n, d], GRADIENT)
        hbuf[n, hi] = coded(total, GRADIENT)
        lasts.append(
            [
                remote(hbuf.at[n, hi], hbuf.at[n, hi], h_send.at[n, d], h_recv.at[n, d], along_z(d))
                for d in (1, 3)
            ]
        )

    def pass_along(n):
        lasts[n][0].wait_recv()
        first = hbuf.at[n, below, pl.ds(0, QUARTER // 2)]
        upward = remote(first, first, h_send.at[n, 0], h_recv.at[n, 0], along_z(1))
        lasts[n][1].wait_recv()
        second = hbuf.at[n, above, pl.ds(QUARTER // 2, QUARTER // 2)]
        downward = remote(second, second, h_send.at[n, 2], h_recv.at[n, 2], along_z(3))
        passing.append([upward, downward])

    def return_over_x(n):
        for copy in passing[n]:
            copy.wait_recv()
        total = decoded(hbuf[n, 0], GRADIENT) + decoded(hbuf[n, 1], GRADIENT)
        total = total + (decoded(hbuf[n, 2], GRADIENT) + decoded(hbuf[n, 3], GRADIENT))
        rows = slab(core * HALF + n * SUB + xi * QUARTER, QUARTER)
        back[rows, :] = coded(total, GRADIENT)
        back_x.append(
            [
                remote(back.at[rows], back.at[rows], e_send.at[n, d], e_recv.at[n, d], along_x(d))
                for d in (2, 1, 3)
            ]
        )

    for n in range(SUBS + 4):
        if n < SUBS:
            over_z(n)
        if 2 <= n < SUBS + 2:
            pass_along(n - 2)
        if n >= 4:
            return_over_x(n - 4)
    def update(first):
        rows = slab(first, SUB)
        whole = decoded(back[rows, :], GRADIENT) + pv[rows, :].astype(F32)
        new_ref[rows, :] = wv[rows, :] - learn_rate / samples * whole

    load_p.wait()
    back_core = []
    for n in range(SUBS):
        for copy in back_x[n]:
            copy.wait_recv()
        rows = slab(core * HALF + n * SUB, SUB)
        back_core.append(
            remote(back.at[rows], back.at[rows], k_send.at[n], k_recv.at[n], sibling)
        )
        update(core * HALF + n * SUB)
        if n > 0:
            back_core[n - 1].wait_recv()
            update((1 - core) * HALF + (n - 1) * SUB)
    back_core[SUBS - 1].wait_recv()
    update((1 - core) * HALF + (SUBS - 1) * SUB)
    for copy in sent:
        copy.wait_send()


def updated(samples, *arrays):
    dma = pltpu.SemaphoreType.DMA
    return pl.pallas_call(
        functools.partial(kernel, samples),
        out_shape=pltpu.VMEM((COLS, PH), F32),
        in_specs=[pl.BlockSpec(memory_space=pltpu.HBM)] * len(arrays),
        out_specs=pl.BlockSpec(memory_space=pltpu.VMEM),
        scratch_shapes=[
            pltpu.VMEM((ROWS, COLS), BF16),
            pltpu.VMEM((ROWS, COLS), BF16),
            pltpu.VMEM((COLS, PH), F32),
            pltpu.VMEM((COLS, PH), BF16),
            pltpu.VMEM((COLS, PH), BF16),
            pltpu.VMEM((SMALL, ROWS, PH), BF16),
            pltpu.VMEM((ROWS, COLS), BF16),
            pltpu.VMEM((ROWS, COLS), BF16),
            pltpu.VMEM((ROWS, COLS), BF16),
            pltpu.VMEM((COLS, ROWS), BF16),
            pltpu.VMEM((COLS, 2 * ROWS), BF16),
            pltpu.VMEM((COLS, PH), BF16),
            pltpu.VMEM((COLS, PH), BF16),
            pltpu.VMEM((COLS, PH), BF16),
            pltpu.VMEM((ROWS, PH), F32),
            pltpu.VMEM((ROWS, PH), BF16),
            pltpu.VMEM((BLOCKS, FEATS, PIECE, PH), BF16),
            pltpu.VMEM((FEATS, PIECE, PH), BF16),
            pltpu.VMEM((2, PIECE, PH), F32),
            pltpu.VMEM((SMALL, BLOCKS * PIECE, PH), BF16),
            pltpu.VMEM((SMALL, BLOCKS * PIECE, PH), BF16),
            pltpu.VMEM((2 * ROWS, PH), BF16),
            pltpu.VMEM((COLS, PH), F32),
            pltpu.VMEM((SUBS, SUB, PH), F32),
            pltpu.VMEM((SUBS, SUB, PH), BF16),
            pltpu.VMEM((SUBS, 4, QUARTER, PH), BF16),
            pltpu.VMEM((SUBS, 4, QUARTER, PH), BF16),
            pltpu.VMEM((COLS, PH), BF16),
            pltpu.SemaphoreType.REGULAR((3,)),
            pltpu.SemaphoreType.REGULAR((3,)),
            pltpu.SemaphoreType.REGULAR((1,)),
            pltpu.SemaphoreType.REGULAR,
            dma((9,)),
            dma((CHUNKS, 2)),
            dma((CHUNKS,)), dma((CHUNKS,)),
            dma((2,)), dma((2,)),
            dma((1,)), dma((1,)),
            dma((BLOCKS, FEATS)), dma((BLOCKS, FEATS)),
            dma((FEATS,)), dma((FEATS,)),
            dma((1,)), dma((1,)),
            dma((BLOCKS, FEATS)), dma((BLOCKS, FEATS)),
            dma((SUBS,)), dma((SUBS,)),
            dma((SUBS, 4)), dma((SUBS, 4)),
            dma((SUBS, 4)), dma((SUBS, 4)),
            dma((SUBS, 4)), dma((SUBS, 4)),
            dma((SUBS,)), dma((SUBS,)),
        ],
        compiler_params=pltpu.CompilerParams(
            collective_id=0, has_side_effects=True, vmem_limit_bytes=60 * 2**20
        ),
        cost_estimate=pl.CostEstimate(
            flops=12 * ROWS * COLS * PH, bytes_accessed=5 * 2**20, transcendentals=0
        ),
    )(*arrays)


def shards(*arrays):
    samples = arrays[0].shape[1] * lax.axis_size(SAMPLE)
    return updated(samples, *arrays)[None]


def solution(mesh):
    torus = Mesh(
        mesh.devices.reshape(mesh.shape["party"], 4, 4, 2, mesh.shape["feat"]),
        ("party", "sample_0", "sample_1", "sample_2", "feat"),
    )
    return jax.shard_map(
        shards,
        mesh=torus,
        in_specs=(
            P("party", SAMPLE, "feat"),
            P("party", SAMPLE, "feat"),
            P("party", "feat", None),
            P("party", "feat", None),
            P("party", SAMPLE, None),
            P("party", SAMPLE, None),
            P("party", SAMPLE, None),
            P("party", SAMPLE, None),
            P("party", SAMPLE, None),
            P("party", SAMPLE, None),
            P("party", "feat", None),
        ),
        out_specs=P("party", "feat", None),
        check_vma=False,
    )
```

```python
import functools

import jax
import jax.numpy as jnp
from jax import lax
from jax.experimental import pallas as pl
from jax.experimental.pallas import tpu as pltpu
from jax.sharding import Mesh
from jax.sharding import PartitionSpec as P

SAMPLE = ("sample_0", "sample_1", "sample_2")
MESH = pl.DeviceIdType.MESH
F32 = jnp.float32
BF16 = jnp.bfloat16

learn_rate = 64.0
slope_one = 0.197
cube_coef = 0.004

ROWS = 256
COLS = 1024
PH = 256
CHUNK = 64
CHUNKS = ROWS // CHUNK
BLOCKS = 2
BLOCK = ROWS // BLOCKS
PER = CHUNKS // BLOCKS
FEATS = 8
PIECE = BLOCK // FEATS
HALF = COLS // 2
SUBS = 4
SUB = HALF // SUBS
QUARTER = SUB // 4
SMALL = 6
ALONG = (4, 3, 5, 2, 6, 1, 7)
MIDDLE = 120.0
GRADIENT = (-22.0, 384.0)
MARGIN = (-14.0, 960.0)


def coded(value, span):
    least, step = span
    level = jnp.log2(jnp.maximum(jnp.abs(value), 2.0**least)) - least
    level = jnp.floor(level * step + 0.5)
    high = jnp.floor(level * (1 / 128))
    code = jnp.exp2(high - MIDDLE) * (1.0 + (level - 128.0 * high) * (1 / 128))
    return jnp.where(value < 0, -code, code).astype(BF16)


def decoded(code, span):
    least, step = span
    code = code.astype(F32)
    size = jnp.abs(code)
    high = jnp.floor(jnp.log2(size) + 0.003)
    low = size * jnp.exp2(-high) - 1.0
    value = jnp.exp2((low + (high + MIDDLE)) * (128 / step) + least)
    return jnp.where(code < 0, -value, value)


def kernel(
    samples,
    x_ref, a_ref, w_ref, b_ref, c_ref, lin_ref, sq_ref, cube_ref, y_ref, r_ref, p_ref,
    new_ref,
    xv, av, wv, bv, pv, sv, mv, om, ev, et, ea, wm, ow, opened, zv, zc, zbuf, zfar, psum, pack, pbuf,
    rr, gv, gbuf, gc, xbuf, hbuf, back,
    y_token, z_token, x_token, p_token, load_sem, first_sem, in_send, in_recv, wt_send, wt_recv, pk_send, pk_recv,
    z_send, z_recv, q_send, q_recv, p_send, p_recv, r_send, r_recv, g_send, g_recv, x_send, x_recv,
    h_send, h_recv, e_send, e_recv, k_send, k_recv,
):
    party = lax.axis_index("party")
    xi = lax.axis_index("sample_0")
    hi = lax.axis_index("sample_1")
    core = lax.axis_index("sample_2")
    feat = lax.axis_index("feat")
    select = (party == 0).astype(F32)

    def at_place(p=None, x=None, h=None, c=None, f=None):
        return (
            party if p is None else p,
            xi if x is None else x,
            hi if h is None else h,
            core if c is None else c,
            feat if f is None else f,
        )

    partner = at_place(p=1 - party)
    sibling = at_place(c=1 - core)
    other_z = at_place(p=1 - party, h=lax.rem(hi + 3 + 2 * party, 4))

    def along_y(d):
        return at_place(f=lax.rem(feat + d, FEATS))

    def across_y(d):
        return at_place(p=1 - party, f=lax.rem(feat + d, FEATS))

    def along_x(d):
        return at_place(x=lax.rem(xi + d, 4))

    def across_x(d):
        return at_place(x=lax.rem(xi + d, 4), c=1 - core)

    def along_z(d):
        return at_place(h=lax.rem(hi + d, 4))

    near_y, near_x, near_z = [along_y(1), along_y(7)], [along_x(1), along_x(3)], [partner, other_z]
    greeted = near_z + [sibling] + near_y + near_x
    barrier = pltpu.get_barrier_semaphore()
    loads = [
        pltpu.make_async_copy(src.at[0], dst, load_sem.at[i])
        for i, (src, dst) in enumerate(
            [(w_ref, wv), (b_ref, bv)]
            + [
                (ref, sv.at[i])
                for i, ref in enumerate((c_ref, lin_ref, sq_ref, cube_ref, y_ref, r_ref))
            ]
        )
    ]
    first_loads = []
    for k in range(CHUNKS):
        rows = pl.ds(k * CHUNK, CHUNK)
        for i, (src, dst) in enumerate([(x_ref, xv), (a_ref, av)]):
            first_loads.append(
                pltpu.make_async_copy(src.at[0, rows], dst.at[rows], first_sem.at[k, i])
            )
            first_loads[-1].start()
    for place in greeted:
        pl.semaphore_signal(barrier, inc=1, device_id=place, device_id_type=MESH)
    for load in loads:
        load.start()


    def masked_chunk(k):
        first_loads[2 * k].wait()
        first_loads[2 * k + 1].wait()
        rows = pl.ds(k * CHUNK, CHUNK)
        mv[rows, :] = (xv[rows, :].astype(F32) - av[rows, :].astype(F32)).astype(BF16)

    masked_chunk(0)
    pl.semaphore_wait(barrier, len(greeted))

    def pass_on(r):
        for token, places in ((y_token, near_y), (z_token, near_z), (x_token, near_x)):
            if r < token.shape[0]:
                for place in places:
                    pl.semaphore_signal(token.at[r], inc=1, device_id=place, device_id_type=MESH)

    def hear(r):
        for token in (y_token, z_token, x_token):
            if r < token.shape[0]:
                pl.semaphore_wait(token.at[r], 2)

    sent = []

    def remote(src, dst, send, recv, place):
        copy = pltpu.make_async_remote_copy(
            src_ref=src, dst_ref=dst, send_sem=send, recv_sem=recv,
            device_id=place, device_id_type=MESH,
        )
        copy.start()
        sent.append(copy)
        return copy

    def slab(first, size):
        return pl.ds(pl.multiple_of(first, size), size)

    inputs = []
    for k in range(CHUNKS):
        if k > 0:
            masked_chunk(k)
        rows = pl.ds(k * CHUNK, CHUNK)
        inputs.append(remote(mv.at[rows], om.at[rows], in_send.at[k], in_recv.at[k], partner))
    my_half = slab(core * HALF, HALF)
    loads[0].wait()
    loads[1].wait()
    wm[...] = (wv[...] - bv[...].astype(F32)).astype(BF16)
    weights = remote(wm.at[my_half], ow.at[my_half], wt_send.at[0], wt_recv.at[0], other_z)
    pass_on(0)

    for load in loads[2:]:
        load.wait()
    load_p = pltpu.make_async_copy(p_ref.at[0], pv, load_sem.at[8])
    load_p.start()
    for i in range(SMALL):
        for j in range(BLOCKS):
            pack[i, pl.ds(j * PIECE, PIECE), :] = sv[i, slab(j * BLOCK + feat * PIECE, PIECE), :]
    packed = remote(pack, pbuf, pk_send.at[0], pk_recv.at[0], partner)

    ea[:, ROWS:] = av[...].T
    hear(0)
    pass_on(1)
    hear(1)
    pass_on(2)
    hear(2)
    pl.semaphore_signal(p_token, inc=1, device_id=partner, device_id_type=MESH)
    weights.wait_recv()
    passed = remote(ow.at[my_half], ow.at[my_half], wt_send.at[1], wt_recv.at[1], sibling)
    passed.wait_recv()
    opened[...] = (wm[...].astype(F32) + ow[...].astype(F32)).astype(BF16)
    zv[...] = jnp.dot(av[...], opened[...], preferred_element_type=F32)

    def margins(k):
        rows = pl.ds(k * CHUNK, CHUNK)
        inputs[k].wait_recv()
        part = (mv[rows, :].astype(F32) + om[rows, :].astype(F32)).astype(BF16)
        ev[rows, :] = part
        both = select * jnp.dot(part, opened[...], preferred_element_type=F32)
        total = zv[rows, :] + both + jnp.dot(part, bv[...], preferred_element_type=F32)
        zv[rows, :] = total
        zc[rows, :] = coded(total, MARGIN)

    def share(j):
        copies = []
        for d in ALONG:
            rows = slab(j * BLOCK + lax.rem(feat + d, FEATS) * PIECE, PIECE)
            copies.append(
                remote(zc.at[rows], zbuf.at[j, d], z_send.at[j, d], z_recv.at[j, d], along_y(d))
            )
        return copies

    def add_up(j, copies):
        for copy in copies:
            copy.wait_recv()
        total = zv[slab(j * BLOCK + feat * PIECE, PIECE), :]
        for d in range(1, FEATS):
            total = total + decoded(zbuf[j, d], MARGIN)
        psum[0] = total
        return remote(psum.at[0], psum.at[1], p_send.at[0], p_recv.at[0], partner)

    def share_with_both():
        own, far = {}, {}
        for d in ALONG + (0,):
            rows = slab(BLOCK + lax.rem(feat + d, FEATS) * PIECE, PIECE)
            far[d] = remote(zc.at[rows], zfar.at[d], q_send.at[d], q_recv.at[d], across_y(d))
            if d:
                own[d] = remote(zc.at[rows], zbuf.at[1, d], z_send.at[1, d], z_recv.at[1, d], along_y(d))
        return own, far

    def both_sums(own, far):
        own_sum = decoded(zc[slab(BLOCK + feat * PIECE, PIECE), :], MARGIN)
        far[0].wait_recv()
        far_sum = decoded(zfar[0], MARGIN)
        for d in range(1, FEATS):
            own[d].wait_recv()
            own_sum = own_sum + decoded(zbuf[1, d], MARGIN)
            far[d].wait_recv()
            far_sum = far_sum + decoded(zfar[d], MARGIN)
        return own_sum, far_sum

    def residuals(j, own_sum, far_sum):
        own_rows = pl.ds(j * PIECE, PIECE)
        own = [pack[i, own_rows, :].astype(F32) for i in range(SMALL)]
        far = [pbuf[i, own_rows, :].astype(F32) for i in range(SMALL)]
        own_margin, far_margin = own_sum + own[0], far_sum + far[0]
        spread = (own_margin - own[1]) + (far_margin - far[1])

        def masked(s, margin, value):
            cubed = s * (spread * spread * spread) + 3.0 * (spread * spread) * value[1]
            cubed = cubed + 3.0 * spread * value[2] + value[3]
            result = 0.5 * s + slope_one * margin - cube_coef * cubed - value[4]
            return (result - value[5]).astype(BF16).astype(F32)

        both = masked(select, own_margin, own) + masked(1.0 - select, far_margin, far)
        rows = slab(j * BLOCK + feat * PIECE, PIECE)
        rr[rows, :] = both.astype(BF16)
        return [
            remote(rr.at[rows], rr.at[rows], r_send.at[j, d], r_recv.at[j, d], along_y(d))
            for d in ALONG
        ]

    def turned(j):
        rows = pl.ds(j * BLOCK, BLOCK)
        flipped = ev[rows, :].T
        et[:, rows] = flipped
        ea[:, rows] = (flipped.astype(F32) * select).astype(BF16)

    margins(0)
    margins(1)
    shared_0 = share(0)
    turned(0)
    margins(2)
    pl.semaphore_wait(p_token, 1)
    margins(3)
    shared_1 = share_with_both()
    summed_0 = add_up(0, shared_0)
    packed.wait_recv()
    summed_0.wait_recv()
    opened_0 = residuals(0, psum[0], psum[1])
    turned(1)
    gv[...] = jnp.dot(et[...], sv[SMALL - 1], preferred_element_type=F32)
    sums_1 = both_sums(*shared_1)
    opened_1 = residuals(1, *sums_1)
    for copy in opened_0 + opened_1:
        copy.wait_recv()
    rr[ROWS:, :] = rr[:ROWS, :]

    def terms(first, size):
        rows = pl.ds(pl.multiple_of(first, SUB), size)
        gv[rows, :] += jnp.dot(ea[rows, :], rr[...], preferred_element_type=F32)

    crossing, quarters = [], []
    their, own = (1 - core) * HALF, core * HALF

    def cross(n):
        rows = slab(their + n * SUB, SUB)
        crossing.append(remote(gv.at[rows], gbuf.at[n], g_send.at[n], g_recv.at[n], sibling))

    terms(their, SUB)
    cross(0)
    terms(their + SUB, HALF - SUB)
    for n in range(1, SUBS):
        cross(n)
    terms(own, SUB)
    terms(own + SUB, HALF - SUB)

    def over_x(n):
        crossing[n].wait_recv()
        total = gbuf[n] + gv[slab(core * HALF + n * SUB, SUB), :]
        gbuf[n] = total
        gc[n] = coded(total, GRADIENT)
        quarters.append(
            [
                remote(
                    gc.at[n, slab(lax.rem(xi + d, 4) * QUARTER, QUARTER)],
                    xbuf.at[n, d], x_send.at[n, d], x_recv.at[n, d], along_x(d),
                )
                for d in (2, 1, 3)
            ]
        )

    for n in range(SUBS):
        over_x(n)

    lasts = []
    for n in range(SUBS):
        for copy in quarters[n]:
            copy.wait_recv()
        total = gbuf[n, slab(xi * QUARTER, QUARTER), :]
        for d in (1, 2, 3):
            total = total + decoded(xbuf[n, d], GRADIENT)
        hbuf[n, hi] = coded(total, GRADIENT)
        lasts.append(
            [
                remote(hbuf.at[n, hi], hbuf.at[n, hi], h_send.at[n, d], h_recv.at[n, d], along_z(d))
                for d in (2, 1, 3)
            ]
        )
    back_x, back_core = [], []
    for n in range(SUBS):
        for copy in lasts[n]:
            copy.wait_recv()
        total = decoded(hbuf[n, 0], GRADIENT) + decoded(hbuf[n, 1], GRADIENT)
        total = total + (decoded(hbuf[n, 2], GRADIENT) + decoded(hbuf[n, 3], GRADIENT))
        rows = slab(core * HALF + n * SUB + xi * QUARTER, QUARTER)
        back[rows, :] = coded(total, GRADIENT)
        back_x.append(
            [
                remote(back.at[rows], back.at[rows], e_send.at[n, d], e_recv.at[n, d], along_x(d))
                for d in (2, 1, 3)
            ]
        )
        back_core.append(
            [
                remote(back.at[rows], back.at[rows], k_send.at[n, d], k_recv.at[n, d], across_x(d))
                for d in (2, 1, 3, 0)
            ]
        )
    def update(first):
        rows = slab(first, SUB)
        whole = decoded(back[rows, :], GRADIENT) + pv[rows, :].astype(F32)
        new_ref[rows, :] = wv[rows, :] - learn_rate / samples * whole

    load_p.wait()
    for n in range(SUBS):
        for copy in back_x[n]:
            copy.wait_recv()
        update(core * HALF + n * SUB)
        for copy in back_core[n]:
            copy.wait_recv()
        update((1 - core) * HALF + n * SUB)
    for copy in sent:
        copy.wait_send()


def updated(samples, *arrays):
    dma = pltpu.SemaphoreType.DMA
    return pl.pallas_call(
        functools.partial(kernel, samples),
        out_shape=pltpu.VMEM((COLS, PH), F32),
        in_specs=[pl.BlockSpec(memory_space=pltpu.HBM)] * len(arrays),
        out_specs=pl.BlockSpec(memory_space=pltpu.VMEM),
        scratch_shapes=[
            pltpu.VMEM((ROWS, COLS), BF16),
            pltpu.VMEM((ROWS, COLS), BF16),
            pltpu.VMEM((COLS, PH), F32),
            pltpu.VMEM((COLS, PH), BF16),
            pltpu.VMEM((COLS, PH), BF16),
            pltpu.VMEM((SMALL, ROWS, PH), BF16),
            pltpu.VMEM((ROWS, COLS), BF16),
            pltpu.VMEM((ROWS, COLS), BF16),
            pltpu.VMEM((ROWS, COLS), BF16),
            pltpu.VMEM((COLS, ROWS), BF16),
            pltpu.VMEM((COLS, 2 * ROWS), BF16),
            pltpu.VMEM((COLS, PH), BF16),
            pltpu.VMEM((COLS, PH), BF16),
            pltpu.VMEM((COLS, PH), BF16),
            pltpu.VMEM((ROWS, PH), F32),
            pltpu.VMEM((ROWS, PH), BF16),
            pltpu.VMEM((BLOCKS, FEATS, PIECE, PH), BF16),
            pltpu.VMEM((FEATS, PIECE, PH), BF16),
            pltpu.VMEM((2, PIECE, PH), F32),
            pltpu.VMEM((SMALL, BLOCKS * PIECE, PH), BF16),
            pltpu.VMEM((SMALL, BLOCKS * PIECE, PH), BF16),
            pltpu.VMEM((2 * ROWS, PH), BF16),
            pltpu.VMEM((COLS, PH), F32),
            pltpu.VMEM((SUBS, SUB, PH), F32),
            pltpu.VMEM((SUBS, SUB, PH), BF16),
            pltpu.VMEM((SUBS, 4, QUARTER, PH), BF16),
            pltpu.VMEM((SUBS, 4, QUARTER, PH), BF16),
            pltpu.VMEM((COLS, PH), BF16),
            pltpu.SemaphoreType.REGULAR((3,)),
            pltpu.SemaphoreType.REGULAR((3,)),
            pltpu.SemaphoreType.REGULAR((1,)),
            pltpu.SemaphoreType.REGULAR,
            dma((9,)),
            dma((CHUNKS, 2)),
            dma((CHUNKS,)), dma((CHUNKS,)),
            dma((2,)), dma((2,)),
            dma((1,)), dma((1,)),
            dma((BLOCKS, FEATS)), dma((BLOCKS, FEATS)),
            dma((FEATS,)), dma((FEATS,)),
            dma((1,)), dma((1,)),
            dma((BLOCKS, FEATS)), dma((BLOCKS, FEATS)),
            dma((SUBS,)), dma((SUBS,)),
            dma((SUBS, 4)), dma((SUBS, 4)),
            dma((SUBS, 4)), dma((SUBS, 4)),
            dma((SUBS, 4)), dma((SUBS, 4)),
            dma((SUBS, 4)), dma((SUBS, 4)),
        ],
        compiler_params=pltpu.CompilerParams(
            collective_id=0, has_side_effects=True, vmem_limit_bytes=60 * 2**20
        ),
        cost_estimate=pl.CostEstimate(
            flops=12 * ROWS * COLS * PH, bytes_accessed=5 * 2**20, transcendentals=0
        ),
    )(*arrays)


def shards(*arrays):
    samples = arrays[0].shape[1] * lax.axis_size(SAMPLE)
    return updated(samples, *arrays)[None]


def solution(mesh):
    torus = Mesh(
        mesh.devices.reshape(mesh.shape["party"], 4, 4, 2, mesh.shape["feat"]),
        ("party", "sample_0", "sample_1", "sample_2", "feat"),
    )
    return jax.shard_map(
        shards,
        mesh=torus,
        in_specs=(
            P("party", SAMPLE, "feat"),
            P("party", SAMPLE, "feat"),
            P("party", "feat", None),
            P("party", "feat", None),
            P("party", SAMPLE, None),
            P("party", SAMPLE, None),
            P("party", SAMPLE, None),
            P("party", SAMPLE, None),
            P("party", SAMPLE, None),
            P("party", SAMPLE, None),
            P("party", "feat", None),
        ),
        out_specs=P("party", "feat", None),
        check_vma=False,
    )
```

```python
import functools

import jax
import jax.numpy as jnp
from jax import lax
from jax.experimental import pallas as pl
from jax.experimental.pallas import tpu as pltpu
from jax.sharding import Mesh
from jax.sharding import PartitionSpec as P

SAMPLE = ("sample_0", "sample_1", "sample_2")
MESH = pl.DeviceIdType.MESH
F32 = jnp.float32
BF16 = jnp.bfloat16

learn_rate = 64.0
slope_one = 0.197
cube_coef = 0.004

ROWS = 256
COLS = 1024
PH = 256
CHUNK = 64
CHUNKS = ROWS // CHUNK
BLOCKS = 2
BLOCK = ROWS // BLOCKS
PER = CHUNKS // BLOCKS
FEATS = 8
PIECE = BLOCK // FEATS
HALF = COLS // 2
SUBS = 4
SUB = HALF // SUBS
QUARTER = SUB // 4
SMALL = 6
ALONG = (4, 3, 5, 2, 6, 1, 7)
MIDDLE = 120.0
GRADIENT = (-22.0, 384.0)
MARGIN = (-14.0, 960.0)


def coded(value, span):
    least, step = span
    level = jnp.log2(jnp.maximum(jnp.abs(value), 2.0**least)) - least
    level = jnp.floor(level * step + 0.5)
    high = jnp.floor(level * (1 / 128))
    code = jnp.exp2(high - MIDDLE) * (1.0 + (level - 128.0 * high) * (1 / 128))
    return jnp.where(value < 0, -code, code).astype(BF16)


def decoded(code, span):
    least, step = span
    code = code.astype(F32)
    size = jnp.abs(code)
    high = jnp.floor(jnp.log2(size) + 0.003)
    low = size * jnp.exp2(-high) - 1.0
    value = jnp.exp2((low + (high + MIDDLE)) * (128 / step) + least)
    return jnp.where(code < 0, -value, value)


def kernel(
    samples,
    x_ref, a_ref, w_ref, b_ref, c_ref, lin_ref, sq_ref, cube_ref, y_ref, r_ref, p_ref,
    new_ref,
    xv, av, wv, bv, pv, sv, mv, om, ev, et, ea, wm, ow, opened, zv, zc, zbuf, zfar, psum, pack, pbuf,
    rr, gv, gbuf, gc, xbuf, hbuf, back,
    y_token, z_token, x_token, p_token, load_sem, first_sem, in_send, in_recv, wt_send, wt_recv, pk_send, pk_recv,
    z_send, z_recv, q_send, q_recv, p_send, p_recv, r_send, r_recv, g_send, g_recv, x_send, x_recv,
    h_send, h_recv, e_send, e_recv, k_send, k_recv,
):
    party = lax.axis_index("party")
    xi = lax.axis_index("sample_0")
    hi = lax.axis_index("sample_1")
    core = lax.axis_index("sample_2")
    feat = lax.axis_index("feat")
    select = (party == 0).astype(F32)

    def at_place(p=None, x=None, h=None, c=None, f=None):
        return (
            party if p is None else p,
            xi if x is None else x,
            hi if h is None else h,
            core if c is None else c,
            feat if f is None else f,
        )

    partner = at_place(p=1 - party)
    sibling = at_place(c=1 - core)
    other_z = at_place(p=1 - party, h=lax.rem(hi + 3 + 2 * party, 4))

    def along_y(d):
        return at_place(f=lax.rem(feat + d, FEATS))

    def across_y(d):
        return at_place(p=1 - party, f=lax.rem(feat + d, FEATS))

    def along_x(d):
        return at_place(x=lax.rem(xi + d, 4))

    def across_x(d):
        return at_place(x=lax.rem(xi + d, 4), c=1 - core)

    def along_z(d):
        return at_place(h=lax.rem(hi + d, 4))

    near_y, near_x, near_z = [along_y(1), along_y(7)], [along_x(1), along_x(3)], [partner, other_z]
    greeted = near_z + [sibling] + near_y + near_x
    barrier = pltpu.get_barrier_semaphore()
    loads = [
        pltpu.make_async_copy(src.at[0], dst, load_sem.at[i])
        for i, (src, dst) in enumerate(
            [(w_ref, wv), (b_ref, bv)]
            + [
                (ref, sv.at[i])
                for i, ref in enumerate((c_ref, lin_ref, sq_ref, cube_ref, y_ref, r_ref))
            ]
        )
    ]
    first_loads = []
    for k in range(CHUNKS):
        rows = pl.ds(k * CHUNK, CHUNK)
        for i, (src, dst) in enumerate([(x_ref, xv), (a_ref, av)]):
            first_loads.append(
                pltpu.make_async_copy(src.at[0, rows], dst.at[rows], first_sem.at[k, i])
            )
            first_loads[-1].start()
    for place in greeted:
        pl.semaphore_signal(barrier, inc=1, device_id=place, device_id_type=MESH)
    for load in loads:
        load.start()


    def masked_chunk(k):
        first_loads[2 * k].wait()
        first_loads[2 * k + 1].wait()
        rows = pl.ds(k * CHUNK, CHUNK)
        mv[rows, :] = (xv[rows, :].astype(F32) - av[rows, :].astype(F32)).astype(BF16)

    masked_chunk(0)
    pl.semaphore_wait(barrier, len(greeted))

    def pass_on(r):
        for token, places in ((y_token, near_y), (z_token, near_z), (x_token, near_x)):
            if r < token.shape[0]:
                for place in places:
                    pl.semaphore_signal(token.at[r], inc=1, device_id=place, device_id_type=MESH)

    def hear(r):
        for token in (y_token, z_token, x_token):
            if r < token.shape[0]:
                pl.semaphore_wait(token.at[r], 2)

    sent = []

    def remote(src, dst, send, recv, place):
        copy = pltpu.make_async_remote_copy(
            src_ref=src, dst_ref=dst, send_sem=send, recv_sem=recv,
            device_id=place, device_id_type=MESH,
        )
        copy.start()
        sent.append(copy)
        return copy

    def slab(first, size):
        return pl.ds(pl.multiple_of(first, size), size)

    inputs = []
    for k in range(CHUNKS):
        if k > 0:
            masked_chunk(k)
        rows = pl.ds(k * CHUNK, CHUNK)
        inputs.append(remote(mv.at[rows], om.at[rows], in_send.at[k], in_recv.at[k], partner))
    my_half = slab(core * HALF, HALF)
    loads[0].wait()
    loads[1].wait()
    wm[...] = (wv[...] - bv[...].astype(F32)).astype(BF16)
    weights = remote(wm.at[my_half], ow.at[my_half], wt_send.at[0], wt_recv.at[0], other_z)
    pass_on(0)

    for load in loads[2:]:
        load.wait()
    load_p = pltpu.make_async_copy(p_ref.at[0], pv, load_sem.at[8])
    load_p.start()
    for i in range(SMALL):
        for j in range(BLOCKS):
            pack[i, pl.ds(j * PIECE, PIECE), :] = sv[i, slab(j * BLOCK + feat * PIECE, PIECE), :]

    ea[:, ROWS:] = av[...].T
    hear(0)
    pass_on(1)
    hear(1)
    pass_on(2)
    hear(2)
    pl.semaphore_signal(p_token, inc=1, device_id=partner, device_id_type=MESH)
    weights.wait_recv()
    passed = remote(ow.at[my_half], ow.at[my_half], wt_send.at[1], wt_recv.at[1], sibling)
    passed.wait_recv()
    opened[...] = (wm[...].astype(F32) + ow[...].astype(F32)).astype(BF16)
    zv[...] = jnp.dot(av[...], opened[...], preferred_element_type=F32)

    def margins(k):
        rows = pl.ds(k * CHUNK, CHUNK)
        inputs[k].wait_recv()
        part = (mv[rows, :].astype(F32) + om[rows, :].astype(F32)).astype(BF16)
        ev[rows, :] = part
        both = select * jnp.dot(part, opened[...], preferred_element_type=F32)
        total = zv[rows, :] + both + jnp.dot(part, bv[...], preferred_element_type=F32)
        zv[rows, :] = total
        zc[rows, :] = coded(total, MARGIN)

    def share(j):
        copies = []
        for d in ALONG:
            rows = slab(j * BLOCK + lax.rem(feat + d, FEATS) * PIECE, PIECE)
            copies.append(
                remote(zc.at[rows], zbuf.at[j, d], z_send.at[j, d], z_recv.at[j, d], along_y(d))
            )
        return copies

    def add_up(j, copies):
        for copy in copies:
            copy.wait_recv()
        total = zv[slab(j * BLOCK + feat * PIECE, PIECE), :]
        for d in range(1, FEATS):
            total = total + decoded(zbuf[j, d], MARGIN)
        psum[0] = total
        return remote(psum.at[0], psum.at[1], p_send.at[0], p_recv.at[0], partner)

    def share_with_both():
        own, far = {}, {}
        for d in ALONG + (0,):
            rows = slab(BLOCK + lax.rem(feat + d, FEATS) * PIECE, PIECE)
            far[d] = remote(zc.at[rows], zfar.at[d], q_send.at[d], q_recv.at[d], across_y(d))
            if d:
                own[d] = remote(zc.at[rows], zbuf.at[1, d], z_send.at[1, d], z_recv.at[1, d], along_y(d))
        return own, far

    def both_sums(own, far):
        own_sum = decoded(zc[slab(BLOCK + feat * PIECE, PIECE), :], MARGIN)
        far[0].wait_recv()
        far_sum = decoded(zfar[0], MARGIN)
        for d in range(1, FEATS):
            own[d].wait_recv()
            own_sum = own_sum + decoded(zbuf[1, d], MARGIN)
            far[d].wait_recv()
            far_sum = far_sum + decoded(zfar[d], MARGIN)
        return own_sum, far_sum

    def residuals(j, own_sum, far_sum):
        own_rows = pl.ds(j * PIECE, PIECE)
        own = [pack[i, own_rows, :].astype(F32) for i in range(SMALL)]
        far = [pbuf[i, own_rows, :].astype(F32) for i in range(SMALL)]
        own_margin, far_margin = own_sum + own[0], far_sum + far[0]
        spread = (own_margin - own[1]) + (far_margin - far[1])

        def masked(s, margin, value):
            cubed = s * (spread * spread * spread) + 3.0 * (spread * spread) * value[1]
            cubed = cubed + 3.0 * spread * value[2] + value[3]
            result = 0.5 * s + slope_one * margin - cube_coef * cubed - value[4]
            return (result - value[5]).astype(BF16).astype(F32)

        both = masked(select, own_margin, own) + masked(1.0 - select, far_margin, far)
        rows = slab(j * BLOCK + feat * PIECE, PIECE)
        rr[rows, :] = both.astype(BF16)
        return [
            remote(rr.at[rows], rr.at[rows], r_send.at[j, d], r_recv.at[j, d], along_y(d))
            for d in ALONG
        ]

    def turned(j):
        rows = pl.ds(j * BLOCK, BLOCK)
        flipped = ev[rows, :].T
        et[:, rows] = flipped
        ea[:, rows] = (flipped.astype(F32) * select).astype(BF16)

    margins(0)
    margins(1)
    shared_0 = share(0)
    turned(0)
    margins(2)
    pl.semaphore_wait(p_token, 1)
    margins(3)
    shared_1 = share_with_both()
    packed = remote(pack, pbuf, pk_send.at[0], pk_recv.at[0], partner)
    summed_0 = add_up(0, shared_0)
    packed.wait_recv()
    summed_0.wait_recv()
    opened_0 = residuals(0, psum[0], psum[1])
    turned(1)
    gv[...] = jnp.dot(et[...], sv[SMALL - 1], preferred_element_type=F32)
    sums_1 = both_sums(*shared_1)
    opened_1 = residuals(1, *sums_1)
    for copy in opened_0 + opened_1:
        copy.wait_recv()
    rr[ROWS:, :] = rr[:ROWS, :]

    def terms(first, size):
        rows = pl.ds(pl.multiple_of(first, SUB), size)
        gv[rows, :] += jnp.dot(ea[rows, :], rr[...], preferred_element_type=F32)

    crossing, quarters = [], []
    their, own = (1 - core) * HALF, core * HALF

    def cross(n):
        rows = slab(their + n * SUB, SUB)
        crossing.append(remote(gv.at[rows], gbuf.at[n], g_send.at[n], g_recv.at[n], sibling))

    terms(their, SUB)
    cross(0)
    terms(their + SUB, HALF - SUB)
    for n in range(1, SUBS):
        cross(n)
    terms(own, SUB)
    terms(own + SUB, HALF - SUB)

    def over_x(n):
        crossing[n].wait_recv()
        total = gbuf[n] + gv[slab(core * HALF + n * SUB, SUB), :]
        gbuf[n] = total
        gc[n] = coded(total, GRADIENT)
        quarters.append(
            [
                remote(
                    gc.at[n, slab(lax.rem(xi + d, 4) * QUARTER, QUARTER)],
                    xbuf.at[n, d], x_send.at[n, d], x_recv.at[n, d], along_x(d),
                )
                for d in (2, 1, 3)
            ]
        )

    for n in range(SUBS):
        over_x(n)

    lasts = []
    for n in range(SUBS):
        for copy in quarters[n]:
            copy.wait_recv()
        total = gbuf[n, slab(xi * QUARTER, QUARTER), :]
        for d in (1, 2, 3):
            total = total + decoded(xbuf[n, d], GRADIENT)
        hbuf[n, hi] = coded(total, GRADIENT)
        lasts.append(
            [
                remote(hbuf.at[n, hi], hbuf.at[n, hi], h_send.at[n, d], h_recv.at[n, d], along_z(d))
                for d in (2, 1, 3)
            ]
        )
    back_x, back_core = [], []
    for n in range(SUBS):
        for copy in lasts[n]:
            copy.wait_recv()
        total = decoded(hbuf[n, 0], GRADIENT) + decoded(hbuf[n, 1], GRADIENT)
        total = total + (decoded(hbuf[n, 2], GRADIENT) + decoded(hbuf[n, 3], GRADIENT))
        rows = slab(core * HALF + n * SUB + xi * QUARTER, QUARTER)
        back[rows, :] = coded(total, GRADIENT)
        back_x.append(
            [
                remote(back.at[rows], back.at[rows], e_send.at[n, d], e_recv.at[n, d], along_x(d))
                for d in (2, 1, 3)
            ]
        )
        back_core.append(
            [
                remote(back.at[rows], back.at[rows], k_send.at[n, d], k_recv.at[n, d], across_x(d))
                for d in (2, 1, 3, 0)
            ]
        )
    def update(first):
        rows = slab(first, SUB)
        whole = decoded(back[rows, :], GRADIENT) + pv[rows, :].astype(F32)
        new_ref[rows, :] = wv[rows, :] - learn_rate / samples * whole

    load_p.wait()
    for n in range(SUBS):
        for copy in back_x[n]:
            copy.wait_recv()
        update(core * HALF + n * SUB)
        for copy in back_core[n]:
            copy.wait_recv()
        update((1 - core) * HALF + n * SUB)
    for copy in sent:
        copy.wait_send()


def updated(samples, *arrays):
    dma = pltpu.SemaphoreType.DMA
    return pl.pallas_call(
        functools.partial(kernel, samples),
        out_shape=pltpu.VMEM((COLS, PH), F32),
        in_specs=[pl.BlockSpec(memory_space=pltpu.HBM)] * len(arrays),
        out_specs=pl.BlockSpec(memory_space=pltpu.VMEM),
        scratch_shapes=[
            pltpu.VMEM((ROWS, COLS), BF16),
            pltpu.VMEM((ROWS, COLS), BF16),
            pltpu.VMEM((COLS, PH), F32),
            pltpu.VMEM((COLS, PH), BF16),
            pltpu.VMEM((COLS, PH), BF16),
            pltpu.VMEM((SMALL, ROWS, PH), BF16),
            pltpu.VMEM((ROWS, COLS), BF16),
            pltpu.VMEM((ROWS, COLS), BF16),
            pltpu.VMEM((ROWS, COLS), BF16),
            pltpu.VMEM((COLS, ROWS), BF16),
            pltpu.VMEM((COLS, 2 * ROWS), BF16),
            pltpu.VMEM((COLS, PH), BF16),
            pltpu.VMEM((COLS, PH), BF16),
            pltpu.VMEM((COLS, PH), BF16),
            pltpu.VMEM((ROWS, PH), F32),
            pltpu.VMEM((ROWS, PH), BF16),
            pltpu.VMEM((BLOCKS, FEATS, PIECE, PH), BF16),
            pltpu.VMEM((FEATS, PIECE, PH), BF16),
            pltpu.VMEM((2, PIECE, PH), F32),
            pltpu.VMEM((SMALL, BLOCKS * PIECE, PH), BF16),
            pltpu.VMEM((SMALL, BLOCKS * PIECE, PH), BF16),
            pltpu.VMEM((2 * ROWS, PH), BF16),
            pltpu.VMEM((COLS, PH), F32),
            pltpu.VMEM((SUBS, SUB, PH), F32),
            pltpu.VMEM((SUBS, SUB, PH), BF16),
            pltpu.VMEM((SUBS, 4, QUARTER, PH), BF16),
            pltpu.VMEM((SUBS, 4, QUARTER, PH), BF16),
            pltpu.VMEM((COLS, PH), BF16),
            pltpu.SemaphoreType.REGULAR((3,)),
            pltpu.SemaphoreType.REGULAR((3,)),
            pltpu.SemaphoreType.REGULAR((1,)),
            pltpu.SemaphoreType.REGULAR,
            dma((9,)),
            dma((CHUNKS, 2)),
            dma((CHUNKS,)), dma((CHUNKS,)),
            dma((2,)), dma((2,)),
            dma((1,)), dma((1,)),
            dma((BLOCKS, FEATS)), dma((BLOCKS, FEATS)),
            dma((FEATS,)), dma((FEATS,)),
            dma((1,)), dma((1,)),
            dma((BLOCKS, FEATS)), dma((BLOCKS, FEATS)),
            dma((SUBS,)), dma((SUBS,)),
            dma((SUBS, 4)), dma((SUBS, 4)),
            dma((SUBS, 4)), dma((SUBS, 4)),
            dma((SUBS, 4)), dma((SUBS, 4)),
            dma((SUBS, 4)), dma((SUBS, 4)),
        ],
        compiler_params=pltpu.CompilerParams(
            collective_id=0, has_side_effects=True, vmem_limit_bytes=60 * 2**20
        ),
        cost_estimate=pl.CostEstimate(
            flops=12 * ROWS * COLS * PH, bytes_accessed=5 * 2**20, transcendentals=0
        ),
    )(*arrays)


def shards(*arrays):
    samples = arrays[0].shape[1] * lax.axis_size(SAMPLE)
    return updated(samples, *arrays)[None]


def solution(mesh):
    torus = Mesh(
        mesh.devices.reshape(mesh.shape["party"], 4, 4, 2, mesh.shape["feat"]),
        ("party", "sample_0", "sample_1", "sample_2", "feat"),
    )
    return jax.shard_map(
        shards,
        mesh=torus,
        in_specs=(
            P("party", SAMPLE, "feat"),
            P("party", SAMPLE, "feat"),
            P("party", "feat", None),
            P("party", "feat", None),
            P("party", SAMPLE, None),
            P("party", SAMPLE, None),
            P("party", SAMPLE, None),
            P("party", SAMPLE, None),
            P("party", SAMPLE, None),
            P("party", SAMPLE, None),
            P("party", "feat", None),
        ),
        out_specs=P("party", "feat", None),
        check_vma=False,
    )
```

```python
import functools

import jax
import jax.numpy as jnp
from jax import lax
from jax.experimental import pallas as pl
from jax.experimental.pallas import tpu as pltpu
from jax.sharding import Mesh
from jax.sharding import PartitionSpec as P

SAMPLE = ("sample_0", "sample_1", "sample_2")
MESH = pl.DeviceIdType.MESH
F32 = jnp.float32
BF16 = jnp.bfloat16

learn_rate = 64.0
slope_one = 0.197
cube_coef = 0.004

ROWS = 256
COLS = 1024
PH = 256
CHUNK = 64
CHUNKS = ROWS // CHUNK
BLOCKS = 2
BLOCK = ROWS // BLOCKS
PER = CHUNKS // BLOCKS
FEATS = 8
PIECE = BLOCK // FEATS
HALF = COLS // 2
SUBS = 4
SUB = HALF // SUBS
QUARTER = SUB // 4
SMALL = 6
ALONG = (4, 3, 5, 2, 6, 1, 7)
MIDDLE = 120.0
GRADIENT = (-22.0, 384.0)
MARGIN = (-14.0, 960.0)


def coded(value, span):
    least, step = span
    level = jnp.log2(jnp.maximum(jnp.abs(value), 2.0**least)) - least
    level = jnp.floor(level * step + 0.5)
    high = jnp.floor(level * (1 / 128))
    code = jnp.exp2(high - MIDDLE) * (1.0 + (level - 128.0 * high) * (1 / 128))
    return jnp.where(value < 0, -code, code).astype(BF16)


def decoded(code, span):
    least, step = span
    code = code.astype(F32)
    size = jnp.abs(code)
    high = jnp.floor(jnp.log2(size) + 0.003)
    low = size * jnp.exp2(-high) - 1.0
    value = jnp.exp2((low + (high + MIDDLE)) * (128 / step) + least)
    return jnp.where(code < 0, -value, value)


def kernel(
    samples,
    x_ref, a_ref, w_ref, b_ref, c_ref, lin_ref, sq_ref, cube_ref, y_ref, r_ref, p_ref,
    new_ref,
    xv, av, wv, bv, pv, sv, mv, om, ev, et, ea, wm, ow, opened, zv, zc, zbuf, zfar, psum, pack, pbuf,
    rr, gv, gbuf, gc, xbuf, hbuf, back,
    y_token, z_token, x_token, p_token, load_sem, first_sem, in_send, in_recv, wt_send, wt_recv, pk_send, pk_recv,
    z_send, z_recv, q_send, q_recv, p_send, p_recv, r_send, r_recv, g_send, g_recv, x_send, x_recv,
    h_send, h_recv, e_send, e_recv, k_send, k_recv,
):
    party = lax.axis_index("party")
    xi = lax.axis_index("sample_0")
    hi = lax.axis_index("sample_1")
    core = lax.axis_index("sample_2")
    feat = lax.axis_index("feat")
    select = (party == 0).astype(F32)

    def at_place(p=None, x=None, h=None, c=None, f=None):
        return (
            party if p is None else p,
            xi if x is None else x,
            hi if h is None else h,
            core if c is None else c,
            feat if f is None else f,
        )

    partner = at_place(p=1 - party)
    sibling = at_place(c=1 - core)
    other_z = at_place(p=1 - party, h=lax.rem(hi + 3 + 2 * party, 4))

    def along_y(d):
        return at_place(f=lax.rem(feat + d, FEATS))

    def across_y(d):
        return at_place(p=1 - party, f=lax.rem(feat + d, FEATS))

    def along_x(d):
        return at_place(x=lax.rem(xi + d, 4))

    def across_x(d):
        return at_place(x=lax.rem(xi + d, 4), c=1 - core)

    def along_z(d):
        return at_place(h=lax.rem(hi + d, 4))

    near_y, near_x, near_z = [along_y(1), along_y(7)], [along_x(1), along_x(3)], [partner, other_z]
    greeted = near_z + [sibling] + near_y + near_x
    barrier = pltpu.get_barrier_semaphore()
    loads = [
        pltpu.make_async_copy(src.at[0], dst, load_sem.at[i])
        for i, (src, dst) in enumerate(
            [(w_ref, wv), (b_ref, bv)]
            + [
                (ref, sv.at[i])
                for i, ref in enumerate((c_ref, lin_ref, sq_ref, cube_ref, y_ref, r_ref))
            ]
        )
    ]
    first_loads = []
    for k in range(CHUNKS):
        rows = pl.ds(k * CHUNK, CHUNK)
        for i, (src, dst) in enumerate([(x_ref, xv), (a_ref, av)]):
            first_loads.append(
                pltpu.make_async_copy(src.at[0, rows], dst.at[rows], first_sem.at[k, i])
            )
            first_loads[-1].start()
    for place in greeted:
        pl.semaphore_signal(barrier, inc=1, device_id=place, device_id_type=MESH)
    for load in loads:
        load.start()


    def masked_chunk(k):
        first_loads[2 * k].wait()
        first_loads[2 * k + 1].wait()
        rows = pl.ds(k * CHUNK, CHUNK)
        mv[rows, :] = (xv[rows, :].astype(F32) - av[rows, :].astype(F32)).astype(BF16)

    masked_chunk(0)
    pl.semaphore_wait(barrier, len(greeted))

    def pass_on(r):
        for token, places in ((y_token, near_y), (z_token, near_z), (x_token, near_x)):
            if r < token.shape[0]:
                for place in places:
                    pl.semaphore_signal(token.at[r], inc=1, device_id=place, device_id_type=MESH)

    def hear(r):
        for token in (y_token, z_token, x_token):
            if r < token.shape[0]:
                pl.semaphore_wait(token.at[r], 2)

    sent = []

    def remote(src, dst, send, recv, place):
        copy = pltpu.make_async_remote_copy(
            src_ref=src, dst_ref=dst, send_sem=send, recv_sem=recv,
            device_id=place, device_id_type=MESH,
        )
        copy.start()
        sent.append(copy)
        return copy

    def slab(first, size):
        return pl.ds(pl.multiple_of(first, size), size)

    inputs = []
    for k in range(CHUNKS):
        if k > 0:
            masked_chunk(k)
        rows = pl.ds(k * CHUNK, CHUNK)
        inputs.append(remote(mv.at[rows], om.at[rows], in_send.at[k], in_recv.at[k], partner))
    my_half = slab(core * HALF, HALF)
    loads[0].wait()
    loads[1].wait()
    wm[...] = (wv[...] - bv[...].astype(F32)).astype(BF16)
    weights = remote(wm.at[my_half], ow.at[my_half], wt_send.at[0], wt_recv.at[0], other_z)
    pass_on(0)

    for load in loads[2:]:
        load.wait()
    load_p = pltpu.make_async_copy(p_ref.at[0], pv, load_sem.at[8])
    load_p.start()
    for i in range(SMALL):
        for j in range(BLOCKS):
            pack[i, pl.ds(j * PIECE, PIECE), :] = sv[i, slab(j * BLOCK + feat * PIECE, PIECE), :]

    ea[:, ROWS:] = av[...].T
    hear(0)
    pass_on(1)
    hear(1)
    pass_on(2)
    hear(2)
    pl.semaphore_signal(p_token, inc=1, device_id=partner, device_id_type=MESH)
    weights.wait_recv()
    passed = remote(ow.at[my_half], ow.at[my_half], wt_send.at[1], wt_recv.at[1], sibling)
    passed.wait_recv()
    opened[...] = (wm[...].astype(F32) + ow[...].astype(F32)).astype(BF16)
    zv[...] = jnp.dot(av[...], opened[...], preferred_element_type=F32)

    def margins(k):
        rows = pl.ds(k * CHUNK, CHUNK)
        inputs[k].wait_recv()
        part = (mv[rows, :].astype(F32) + om[rows, :].astype(F32)).astype(BF16)
        ev[rows, :] = part
        both = select * jnp.dot(part, opened[...], preferred_element_type=F32)
        total = zv[rows, :] + both + jnp.dot(part, bv[...], preferred_element_type=F32)
        zv[rows, :] = total
        zc[rows, :] = coded(total, MARGIN)

    def share(j):
        copies = []
        for d in ALONG:
            rows = slab(j * BLOCK + lax.rem(feat + d, FEATS) * PIECE, PIECE)
            copies.append(
                remote(zc.at[rows], zbuf.at[j, d], z_send.at[j, d], z_recv.at[j, d], along_y(d))
            )
        return copies

    def add_up(j, copies):
        for copy in copies:
            copy.wait_recv()
        total = zv[slab(j * BLOCK + feat * PIECE, PIECE), :]
        for d in range(1, FEATS):
            total = total + decoded(zbuf[j, d], MARGIN)
        psum[0] = total
        return remote(psum.at[0], psum.at[1], p_send.at[0], p_recv.at[0], partner)

    def share_with_both():
        own, far = {}, {}
        for d in ALONG + (0,):
            rows = slab(BLOCK + lax.rem(feat + d, FEATS) * PIECE, PIECE)
            far[d] = remote(zc.at[rows], zfar.at[d], q_send.at[d], q_recv.at[d], across_y(d))
            if d:
                own[d] = remote(zc.at[rows], zbuf.at[1, d], z_send.at[1, d], z_recv.at[1, d], along_y(d))
        return own, far

    def both_sums(own, far):
        own_sum = decoded(zc[slab(BLOCK + feat * PIECE, PIECE), :], MARGIN)
        far[0].wait_recv()
        far_sum = decoded(zfar[0], MARGIN)
        for d in range(1, FEATS):
            own[d].wait_recv()
            own_sum = own_sum + decoded(zbuf[1, d], MARGIN)
            far[d].wait_recv()
            far_sum = far_sum + decoded(zfar[d], MARGIN)
        return own_sum, far_sum

    def residuals(j, own_sum, far_sum):
        own_rows = pl.ds(j * PIECE, PIECE)
        own = [pack[i, own_rows, :].astype(F32) for i in range(SMALL)]
        far = [pbuf[i, own_rows, :].astype(F32) for i in range(SMALL)]
        own_margin, far_margin = own_sum + own[0], far_sum + far[0]
        spread = (own_margin - own[1]) + (far_margin - far[1])

        def masked(s, margin, value):
            cubed = s * (spread * spread * spread) + 3.0 * (spread * spread) * value[1]
            cubed = cubed + 3.0 * spread * value[2] + value[3]
            result = 0.5 * s + slope_one * margin - cube_coef * cubed - value[4]
            return (result - value[5]).astype(BF16).astype(F32)

        both = masked(select, own_margin, own) + masked(1.0 - select, far_margin, far)
        rows = slab(j * BLOCK + feat * PIECE, PIECE)
        rr[rows, :] = both.astype(BF16)
        return [
            remote(rr.at[rows], rr.at[rows], r_send.at[j, d], r_recv.at[j, d], along_y(d))
            for d in ALONG
        ]

    def turned(j):
        rows = pl.ds(j * BLOCK, BLOCK)
        flipped = ev[rows, :].T
        et[:, rows] = flipped
        ea[:, rows] = (flipped.astype(F32) * select).astype(BF16)

    margins(0)
    margins(1)
    shared_0 = share(0)
    turned(0)
    margins(2)
    pl.semaphore_wait(p_token, 1)
    margins(3)
    shared_1 = share_with_both()
    packed = remote(pack, pbuf, pk_send.at[0], pk_recv.at[0], partner)
    summed_0 = add_up(0, shared_0)
    turned(1)
    gv[...] = jnp.dot(et[...], sv[SMALL - 1], preferred_element_type=F32)
    packed.wait_recv()
    summed_0.wait_recv()
    opened_0 = residuals(0, psum[0], psum[1])
    sums_1 = both_sums(*shared_1)
    opened_1 = residuals(1, *sums_1)
    for copy in opened_0 + opened_1:
        copy.wait_recv()
    rr[ROWS:, :] = rr[:ROWS, :]

    def terms(first, size):
        rows = pl.ds(pl.multiple_of(first, SUB), size)
        gv[rows, :] += jnp.dot(ea[rows, :], rr[...], preferred_element_type=F32)

    crossing, quarters = [], []
    their, own = (1 - core) * HALF, core * HALF

    def cross(n):
        rows = slab(their + n * SUB, SUB)
        crossing.append(remote(gv.at[rows], gbuf.at[n], g_send.at[n], g_recv.at[n], sibling))

    terms(their, SUB)
    cross(0)
    terms(their + SUB, HALF - SUB)
    for n in range(1, SUBS):
        cross(n)
    terms(own, SUB)
    terms(own + SUB, HALF - SUB)

    def over_x(n):
        crossing[n].wait_recv()
        total = gbuf[n] + gv[slab(core * HALF + n * SUB, SUB), :]
        gbuf[n] = total
        gc[n] = coded(total, GRADIENT)
        quarters.append(
            [
                remote(
                    gc.at[n, slab(lax.rem(xi + d, 4) * QUARTER, QUARTER)],
                    xbuf.at[n, d], x_send.at[n, d], x_recv.at[n, d], along_x(d),
                )
                for d in (2, 1, 3)
            ]
        )

    for n in range(SUBS):
        over_x(n)

    lasts = []
    for n in range(SUBS):
        for copy in quarters[n]:
            copy.wait_recv()
        total = gbuf[n, slab(xi * QUARTER, QUARTER), :]
        for d in (1, 2, 3):
            total = total + decoded(xbuf[n, d], GRADIENT)
        hbuf[n, hi] = coded(total, GRADIENT)
        lasts.append(
            [
                remote(hbuf.at[n, hi], hbuf.at[n, hi], h_send.at[n, d], h_recv.at[n, d], along_z(d))
                for d in (2, 1, 3)
            ]
        )
    back_x, back_core = [], []
    for n in range(SUBS):
        for copy in lasts[n]:
            copy.wait_recv()
        total = decoded(hbuf[n, 0], GRADIENT) + decoded(hbuf[n, 1], GRADIENT)
        total = total + (decoded(hbuf[n, 2], GRADIENT) + decoded(hbuf[n, 3], GRADIENT))
        rows = slab(core * HALF + n * SUB + xi * QUARTER, QUARTER)
        back[rows, :] = coded(total, GRADIENT)
        back_x.append(
            [
                remote(back.at[rows], back.at[rows], e_send.at[n, d], e_recv.at[n, d], along_x(d))
                for d in (2, 1, 3)
            ]
        )
        back_core.append(
            [
                remote(back.at[rows], back.at[rows], k_send.at[n, d], k_recv.at[n, d], across_x(d))
                for d in (2, 1, 3, 0)
            ]
        )
    def update(first):
        rows = slab(first, SUB)
        whole = decoded(back[rows, :], GRADIENT) + pv[rows, :].astype(F32)
        new_ref[rows, :] = wv[rows, :] - learn_rate / samples * whole

    load_p.wait()
    for n in range(SUBS):
        for copy in back_x[n]:
            copy.wait_recv()
        update(core * HALF + n * SUB)
        for copy in back_core[n]:
            copy.wait_recv()
        update((1 - core) * HALF + n * SUB)
    for copy in sent:
        copy.wait_send()


def updated(samples, *arrays):
    dma = pltpu.SemaphoreType.DMA
    return pl.pallas_call(
        functools.partial(kernel, samples),
        out_shape=pltpu.VMEM((COLS, PH), F32),
        in_specs=[pl.BlockSpec(memory_space=pltpu.HBM)] * len(arrays),
        out_specs=pl.BlockSpec(memory_space=pltpu.VMEM),
        scratch_shapes=[
            pltpu.VMEM((ROWS, COLS), BF16),
            pltpu.VMEM((ROWS, COLS), BF16),
            pltpu.VMEM((COLS, PH), F32),
            pltpu.VMEM((COLS, PH), BF16),
            pltpu.VMEM((COLS, PH), BF16),
            pltpu.VMEM((SMALL, ROWS, PH), BF16),
            pltpu.VMEM((ROWS, COLS), BF16),
            pltpu.VMEM((ROWS, COLS), BF16),
            pltpu.VMEM((ROWS, COLS), BF16),
            pltpu.VMEM((COLS, ROWS), BF16),
            pltpu.VMEM((COLS, 2 * ROWS), BF16),
            pltpu.VMEM((COLS, PH), BF16),
            pltpu.VMEM((COLS, PH), BF16),
            pltpu.VMEM((COLS, PH), BF16),
            pltpu.VMEM((ROWS, PH), F32),
            pltpu.VMEM((ROWS, PH), BF16),
            pltpu.VMEM((BLOCKS, FEATS, PIECE, PH), BF16),
            pltpu.VMEM((FEATS, PIECE, PH), BF16),
            pltpu.VMEM((2, PIECE, PH), F32),
            pltpu.VMEM((SMALL, BLOCKS * PIECE, PH), BF16),
            pltpu.VMEM((SMALL, BLOCKS * PIECE, PH), BF16),
            pltpu.VMEM((2 * ROWS, PH), BF16),
            pltpu.VMEM((COLS, PH), F32),
            pltpu.VMEM((SUBS, SUB, PH), F32),
            pltpu.VMEM((SUBS, SUB, PH), BF16),
            pltpu.VMEM((SUBS, 4, QUARTER, PH), BF16),
            pltpu.VMEM((SUBS, 4, QUARTER, PH), BF16),
            pltpu.VMEM((COLS, PH), BF16),
            pltpu.SemaphoreType.REGULAR((3,)),
            pltpu.SemaphoreType.REGULAR((3,)),
            pltpu.SemaphoreType.REGULAR((1,)),
            pltpu.SemaphoreType.REGULAR,
            dma((9,)),
            dma((CHUNKS, 2)),
            dma((CHUNKS,)), dma((CHUNKS,)),
            dma((2,)), dma((2,)),
            dma((1,)), dma((1,)),
            dma((BLOCKS, FEATS)), dma((BLOCKS, FEATS)),
            dma((FEATS,)), dma((FEATS,)),
            dma((1,)), dma((1,)),
            dma((BLOCKS, FEATS)), dma((BLOCKS, FEATS)),
            dma((SUBS,)), dma((SUBS,)),
            dma((SUBS, 4)), dma((SUBS, 4)),
            dma((SUBS, 4)), dma((SUBS, 4)),
            dma((SUBS, 4)), dma((SUBS, 4)),
            dma((SUBS, 4)), dma((SUBS, 4)),
        ],
        compiler_params=pltpu.CompilerParams(
            collective_id=0, has_side_effects=True, vmem_limit_bytes=60 * 2**20
        ),
        cost_estimate=pl.CostEstimate(
            flops=12 * ROWS * COLS * PH, bytes_accessed=5 * 2**20, transcendentals=0
        ),
    )(*arrays)


def shards(*arrays):
    samples = arrays[0].shape[1] * lax.axis_size(SAMPLE)
    return updated(samples, *arrays)[None]


def solution(mesh):
    torus = Mesh(
        mesh.devices.reshape(mesh.shape["party"], 4, 4, 2, mesh.shape["feat"]),
        ("party", "sample_0", "sample_1", "sample_2", "feat"),
    )
    return jax.shard_map(
        shards,
        mesh=torus,
        in_specs=(
            P("party", SAMPLE, "feat"),
            P("party", SAMPLE, "feat"),
            P("party", "feat", None),
            P("party", "feat", None),
            P("party", SAMPLE, None),
            P("party", SAMPLE, None),
            P("party", SAMPLE, None),
            P("party", SAMPLE, None),
            P("party", SAMPLE, None),
            P("party", SAMPLE, None),
            P("party", "feat", None),
        ),
        out_specs=P("party", "feat", None),
        check_vma=False,
    )
```
